32 devices in a mesh: dp: 4 (over y, x), fsdp: 8 (over z, core).
Axes of the slice: x: 2, y: 2, z: 4, core: 2. Of those that a mesh axis runs over, the one named last changes fastest.
Arguments:
- tokens: bfloat16 [50176, 1024], P(('dp', 'fsdp')), may hold values from -6 to 6
- band_code: int32 [1024], P(('dp', 'fsdp')), may hold values from 0 to 3, as said below
- gsd_code: int32 [1024], P(('dp', 'fsdp')), may hold values from 0 to 6, as said below
- norm1_gain: bfloat16 [1024], P('fsdp'), may hold values from 0.5 to 1.5
- norm1_bias: bfloat16 [1024], P('fsdp'), may hold values from -1.75 to 1.75
- qkv_weight: bfloat16 [1024, 3072], P('fsdp'), may hold values from -0.25 to 0.25
- bias_q: bfloat16 [1024], P('fsdp'), may hold values from -1.75 to 1.75
- bias_v: bfloat16 [1024], P('fsdp'), may hold values from -1.75 to 1.75
- out_weight: bfloat16 [1024, 1024], P(None, 'fsdp'), may hold values from -0.5 to 0.5
- bias_out: bfloat16 [1024], P('fsdp'), may hold values from -1.75 to 1.75
- norm2_gain: bfloat16 [1024], P('fsdp'), may hold values from 0.5 to 1.5
- norm2_bias: bfloat16 [1024], P('fsdp'), may hold values from -1.75 to 1.75
- up_weight: bfloat16 [1024, 4096], P('fsdp'), may hold values from -0.1875 to 0.1875
- bias_up: bfloat16 [4096], P('fsdp'), may hold values from -1.75 to 1.75
- down_weight: bfloat16 [4096, 1024], P(None, 'fsdp'), may hold values from -0.1875 to 0.1875
- bias_down: bfloat16 [1024], P('fsdp'), may hold values from -1.75 to 1.75
- grad_out: bfloat16 [50176, 1024], P(('dp', 'fsdp')), may hold values from -6 to 6
Outputs:
- block_out: bfloat16 [50176, 1024], P(('dp', 'fsdp'))
- grad_tokens: float32 [50176, 1024], P(('dp', 'fsdp'))
- grad_norm1_gain: float32 [1024], P('fsdp')
- grad_norm1_bias: float32 [1024], P('fsdp')
- grad_qkv_weight: float32 [1024, 3072], P('fsdp')
- grad_bias_q: float32 [1024], P('fsdp')
- grad_bias_v: float32 [1024], P('fsdp')
- grad_out_weight: float32 [1024, 1024], P(None, 'fsdp')
- grad_bias_out: float32 [1024], P('fsdp')
- grad_norm2_gain: float32 [1024], P('fsdp')
- grad_norm2_bias: float32 [1024], P('fsdp')
- grad_up_weight: float32 [1024, 4096], P('fsdp')
- grad_bias_up: float32 [4096], P('fsdp')
- grad_down_weight: float32 [4096, 1024], P(None, 'fsdp')
- grad_bias_down: float32 [1024], P('fsdp')
The draws below stay inside these ranges and needn't reach their ends.
Inputs may be any that keep to these rules, and one draw needn't show every extreme that they name: `band_code`: each device's units form 4 buffers of 8 units. A unit with code 0 is a whole RGB item; a unit with code 1 is followed in the same buffer by units with codes 2 and 3, the three band groups of one multispectral item; no item crosses a buffer. `gsd_code`: the units of one item share one level.
All inputs are finite; a program needn't handle non-finite values.
Results may differ from the reference program's by a relative error of at most 0.017.
Values may be sent and summed in bfloat16 or wider, within the bound.
A program may use at most 384 MiB of HBM per device.

```python
import math
import jax
import jax.numpy as jnp
from jax import lax

D = 1024
FF = 4096
HEADS = 16
HEAD_DIM = 64
GRID = 7
UNITS_MB = 8
MB = 4
ROWS = 50176
UNITS_ALL = 1024


def item_layout(key):
    buffers = UNITS_ALL // UNITS_MB
    starts = jax.random.randint(jax.random.fold_in(key, 11), (buffers, UNITS_MB), 0, 2)
    levels = jax.random.randint(jax.random.fold_in(key, 12), (buffers, UNITS_MB), 0, 7)
    code_list = []
    level_list = []
    previous = jnp.zeros((buffers,), jnp.int32)
    previous_level = jnp.zeros((buffers,), jnp.int32)
    for column in range(UNITS_MB):
        has_room = column + 3 <= UNITS_MB
        ongoing = (previous == 1) | (previous == 2)
        starting = jnp.where((starts[:, column] == 1) & has_room, 1, 0)
        unit_code = jnp.where(ongoing, previous + 1, starting).astype(jnp.int32)
        unit_level = jnp.where(ongoing, previous_level, levels[:, column]).astype(jnp.int32)
        code_list.append(unit_code)
        level_list.append(unit_level)
        previous = unit_code
        previous_level = unit_level
    return (jnp.stack(code_list, axis=1).reshape(-1), jnp.stack(level_list, axis=1).reshape(-1))


def draw_band_code(key, part):
    layout = item_layout(key)
    return layout[0]


def draw_gsd_code(key, part):
    layout = item_layout(key)
    return layout[1]


def strengthened(values, own_key, source, target, parts, factor):
    owner, partner = [(jnp.arange(values.shape[position]) // (values.shape[position] // parts)).reshape([-1 if axis == position else 1 for axis in range(values.ndim)]) for position in (source, target)]
    chosen = jax.random.permutation(own_key, parts)[partner]
    strong = (owner == chosen) | (owner == (partner + parts // 2) % parts)
    return jnp.where(strong, factor * values, values)


def shard_levels(rng, extent, cuts, smallest, largest):
    loudness = 1.0
    for position, blocks in cuts:
        heights = jax.random.uniform(jax.random.fold_in(jax.random.fold_in(rng, 6), position), (blocks,), jnp.float32, smallest / len(cuts), largest / len(cuts))
        loudness = loudness * jnp.repeat(jnp.exp(heights), extent[position] // blocks).reshape((-1,) + (1,) * (len(extent) - 1 - position))
    return loudness


def noise(own_key, dims, scale, bound, shards=(), kind=jnp.bfloat16):
    gain = shard_levels(own_key, dims, shards, -0.22, 0.18) if shards else 1.0
    array = jax.random.normal(own_key, dims, jnp.float32) * scale * gain
    return jnp.minimum(jnp.maximum(array, -bound), bound).astype(kind)


def noise_with(own_key, extent, width, limit, cuts, heavy, kind=jnp.bfloat16):
    result = width * jax.random.normal(own_key, extent, jnp.float32)
    if cuts:
        result = result * shard_levels(own_key, extent, cuts, -0.22, 0.18)
    return jnp.clip(strengthened(result, jax.random.fold_in(own_key, 3), *heavy), -limit, limit).astype(kind)


def setup_inputs(seed: int = 0) -> dict:
    key_list = jax.random.split(jax.random.key(seed), 18)
    tokens = noise(key_list[0], (ROWS, D), 1.0, 6.0, ((0, 32),))
    band_code = draw_band_code(jax.random.fold_in(key_list[17], 71), 0)
    gsd_code = draw_gsd_code(jax.random.fold_in(key_list[17], 71), 0)
    norm1_gain = jnp.clip(1.0 + 0.1 * jax.random.normal(key_list[3], (D,), jnp.float32), 0.5, 1.5).astype(jnp.bfloat16)
    norm1_bias = noise(key_list[4], (D,), 0.3, 1.75, ((0, 8),))
    qkv_weight = noise(key_list[5], (D, 3 * D), (D // 2) ** -0.5, 0.25, ((0, 8),))
    bias_q = noise(key_list[6], (D,), 0.3, 1.75, ((0, 8),))
    bias_v = noise(key_list[7], (D,), 0.3, 1.75, ((0, 8),))
    out_weight = noise(key_list[8], (D, D), (D // 8) ** -0.5, 0.5, ((1, 8),))
    bias_out = noise(key_list[9], (D,), 0.3, 1.75, ((0, 8),))
    norm2_gain = jnp.clip(1.0 + 0.1 * jax.random.normal(key_list[10], (D,), jnp.float32), 0.5, 1.5).astype(jnp.bfloat16)
    norm2_bias = noise(key_list[11], (D,), 0.3, 1.75, ((0, 8),))
    up_weight = noise(key_list[12], (D, FF), D ** -0.5, 0.1875, ((0, 8),))
    bias_up = noise(key_list[13], (FF,), 0.3, 1.75, ((0, 8),))
    down_weight = noise(key_list[14], (FF, D), (FF // 4) ** -0.5, 0.1875, ((1, 8),))
    bias_down = noise(key_list[15], (D,), 0.3, 1.75, ((0, 8),))
    grad_out = noise_with(key_list[16], (ROWS, D), 1.0, 6.0, ((0, 32),), (0, 1, 32, 2.75))
    return dict(tokens=tokens, band_code=band_code, gsd_code=gsd_code, norm1_gain=norm1_gain, norm1_bias=norm1_bias, qkv_weight=qkv_weight, bias_q=bias_q, bias_v=bias_v, out_weight=out_weight, bias_out=bias_out, norm2_gain=norm2_gain, norm2_bias=norm2_bias, up_weight=up_weight, bias_up=bias_up, down_weight=down_weight, bias_down=bias_down, grad_out=grad_out)


@jax.custom_vjp
def low(v):
    return lax.optimization_barrier(v.astype(jnp.bfloat16)).astype(jnp.float32)

@jax.custom_vjp
def low_back(v):
    return v

def low_keep(v):
    return (low(v), None)

def low_pass(kept, grad):
    return (grad,)

def back_keep(v):
    return (v, None)

def back_low(kept, grad):
    return (low(grad),)
low.defvjp(low_keep, low_pass)
low_back.defvjp(back_keep, back_low)
HIGHEST = lax.Precision.HIGHEST
EPSILON = 1e-06

def layer_norm(row_block, gain_row, shift_row):
    center = row_block - lax.optimization_barrier(jnp.mean(row_block, axis=-1, keepdims=True))
    spread = lax.optimization_barrier(jnp.mean(center * center, axis=-1, keepdims=True))
    return center * lax.rsqrt(spread + EPSILON) * gain_row + shift_row

def gelu_exact(values):
    return 0.5 * values * (1.0 + lax.erf(values * 0.7071067811865476))

def positions(gsd_code):
    patches = GRID * GRID
    patch_place = jnp.arange(gsd_code.shape[0] * patches, dtype=jnp.int32) % patches
    across = (patch_place // GRID).astype(jnp.float32)
    along_row = (patch_place % GRID).astype(jnp.float32)
    gsd_ratio = jnp.repeat(jnp.exp2((gsd_code.astype(jnp.float32) - 3.0) * 0.5), patches)
    quarter = D // 4
    frequency = jnp.exp2(jnp.arange(quarter, dtype=jnp.float32) * (-math.log2(10000.0) / quarter))
    angle_y = (across * gsd_ratio)[:, None] * frequency[None, :]
    angle_x = (along_row * gsd_ratio)[:, None] * frequency[None, :]
    return jnp.concatenate([jnp.sin(angle_y), jnp.cos(angle_y), jnp.sin(angle_x), jnp.cos(angle_x)], axis=1)

def segment_rows(band_code):
    units = band_code.reshape(-1, UNITS_MB)
    labels = jnp.cumsum((units <= 1).astype(jnp.int32), axis=1).astype(jnp.int32)
    return jnp.repeat(labels, GRID * GRID, axis=1)

def layer_rows(params, row_block, labels):
    gain_one, shift_one, w_qkv, bias_query, bias_value, w_out, bias_output, gain_two, shift_two, w_up, bias_hidden, w_down, bias_final = params
    buffers = labels.shape[0]
    length = labels.shape[1]
    model_width = HEADS * HEAD_DIM
    score_scale = 1.0 / math.sqrt(HEAD_DIM)
    normed = low(layer_norm(row_block, gain_one, shift_one))
    joined = jnp.concatenate([bias_query, jnp.zeros_like(bias_query), bias_value])
    mixed = low(low_back(jnp.dot(normed, w_qkv, precision=HIGHEST) + joined))
    split_heads = mixed.reshape(buffers, length, 3, HEADS, HEAD_DIM)
    queries = split_heads[:, :, 0]
    keys_all = split_heads[:, :, 1]
    values_all = split_heads[:, :, 2]
    scores = low_back(jnp.einsum('bqhe,bkhe->bhqk', queries, keys_all, precision=HIGHEST) * score_scale)
    same_item = labels[:, None, :, None] == labels[:, None, None, :]
    scores = jnp.where(same_item, scores, -1e+30)
    row_max = lax.optimization_barrier(jnp.max(scores, axis=-1, keepdims=True))
    expon = jnp.exp(scores - row_max)
    probs = expon / lax.optimization_barrier(jnp.sum(expon, axis=-1, keepdims=True))
    attended = jnp.einsum('bhqk,bkhe->bqhe', low(probs), values_all, precision=HIGHEST)
    attended = low(low_back(attended.reshape(buffers * length, model_width)))
    branch = low_back(jnp.dot(attended, w_out, precision=HIGHEST) + bias_output)
    middle = row_block + branch
    normed_two = low(layer_norm(middle, gain_two, shift_two))
    hidden = low_back(jnp.dot(normed_two, w_up, precision=HIGHEST) + bias_hidden)
    active = low(gelu_exact(hidden))
    return middle + jnp.dot(active, w_down, precision=HIGHEST) + bias_final

def reference(tokens, band_code, gsd_code, norm1_gain, norm1_bias, qkv_weight, bias_q, bias_v, out_weight, bias_out, norm2_gain, norm2_bias, up_weight, bias_up, down_weight, bias_down, grad_out):
    params = tuple((weight_in.astype(jnp.float32) for weight_in in (norm1_gain, norm1_bias, qkv_weight, bias_q, bias_v, out_weight, bias_out, norm2_gain, norm2_bias, up_weight, bias_up, down_weight, bias_down)))
    labels = segment_rows(band_code).reshape(-1, MB, UNITS_MB * GRID * GRID)
    inputs = tokens.astype(jnp.float32) + positions(gsd_code)
    grouped = inputs.reshape(labels.shape[0], -1, inputs.shape[1])

    def forward(weights_f, grouped_rows):

        def one_group(pieces):
            return layer_rows(weights_f, pieces[0], pieces[1])
        return lax.map(jax.checkpoint(one_group), (grouped_rows, labels))
    outputs, pullback = jax.vjp(forward, params, grouped)
    cotangent = grad_out.astype(jnp.float32).reshape(grouped.shape)
    grad_params, grad_rows = pullback(cotangent)
    return (outputs.reshape(tokens.shape).astype(jnp.bfloat16), grad_rows.reshape(tokens.shape), grad_params[0], grad_params[1], grad_params[2], grad_params[3], grad_params[4], grad_params[5], grad_params[6], grad_params[7], grad_params[8], grad_params[9], grad_params[10], grad_params[11], grad_params[12])
```

```python
import functools
import math

import jax
import jax.numpy as jnp
import numpy as np
from jax import lax
from jax.experimental import pallas as pl
from jax.experimental.pallas import tpu as pltpu
from jax.sharding import PartitionSpec as P

bf = jnp.bfloat16
f32 = jnp.float32
NN = (((1,), (0,)), ((), ()))
NT = (((1,), (1,)), ((), ()))
TN = (((0,), (0,)), ((), ()))
D = 1024
HEADS = 16
HEAD_DIM = 64
GRID = 7
UNIT = GRID * GRID
UNITS_MB = 8
BUF = UNIT * UNITS_MB
PAIR = 2 * BUF
QUADS = 4
QW = 256
FC = 512
CW = 1024
EPS = 1e-6
SCALE = 0.125
NEG = -1e30
VMEM_LIMIT = 60 << 20
KEYS = 384
WINDOWS = ((0, ((0, 192, 0), (192, 208, 16))), (384, ((0, 192, 0), (192, 208, 16))))
QMAX = 208


def dot(a, b, dims=NN):
    return lax.dot_general(a, b, dims, preferred_element_type=f32)


def any_spec():
    return pl.BlockSpec(memory_space=pl.ANY)


def vmem_spec():
    return pl.BlockSpec(memory_space=pltpu.VMEM)


def sds(shape, kind):
    return jax.ShapeDtypeStruct(shape, kind)


def norm_parts(v):
    center = v - jnp.mean(v, axis=-1, keepdims=True)
    inv = lax.rsqrt(jnp.mean(center * center, axis=-1, keepdims=True) + EPS)
    return center * inv, inv


def transpose_rows(src, dst, rows):
    full = rows // 128

    def one(i, carry):
        o = pl.multiple_of(i * 128, 128)
        dst[:, pl.ds(o, 128)] = src[pl.ds(o, 128), :].T
        return carry

    lax.fori_loop(0, full, one, 0)
    if rows % 128:
        dst[:, full * 128 : rows] = src[full * 128 : rows, :].T


def fill_bias(bias, lab_col, lab_row, q_units, k_units):
    same = jnp.where(lab_col[...] == lab_row[...], 1.0, 0.0).astype(bf)

    def one(i, carry):
        reach = dot(q_units[i], same).astype(bf)
        bias[i] = (dot(reach, k_units[i]) - 1.0) * -NEG
        return carry

    lax.fori_loop(0, bias.shape[0], one, 0)


def half_mask(rows, second):
    lane = lax.broadcasted_iota(jnp.int32, (rows, 128), 1)
    return lane >= 64 if second else lane < 64


def attention_forward(pairs, mixed, bias, attended, lse, quad, hook):
    def one(i, carry):
        p, hp = i // 2, lax.rem(i, 2)
        base = pl.multiple_of(p * PAIR, 16)
        lane0 = pl.multiple_of(hp * 128, 128)
        tail = None
        for w, (start, halves) in enumerate(WINDOWS):
            for n, (q0, qn, k0) in enumerate(halves):
                row = pl.multiple_of(base + start + q0, 16)
                keys = pl.ds(pl.multiple_of(base + start + k0, 16), KEYS)
                q2 = mixed[pl.ds(row, qn), pl.ds(lane0, 128)] * jnp.asarray(SCALE, bf)
                k2 = mixed[keys, pl.ds(pl.multiple_of(lane0 + QW, 128), 128)]
                v2 = mixed[keys, pl.ds(pl.multiple_of(lane0 + 2 * QW, 128), 128)]
                idx = p * 4 + w * 2 + n
                out = None
                lse_new = jnp.zeros((qn, 128), f32)
                lane = lax.broadcasted_iota(jnp.int32, (qn, 128), 1)
                for h in range(2):
                    qm = jnp.where(half_mask(qn, h == 1), q2, jnp.zeros_like(q2))
                    s = dot(qm, k2, NT) + bias[idx, 0:qn, :]
                    m = jnp.max(s, axis=-1, keepdims=True)
                    e = jnp.exp(s - m)
                    total = jnp.sum(e, axis=-1, keepdims=True)
                    probs = (e * (1.0 / total)).astype(bf)
                    o = dot(probs, v2)
                    out = o if h == 0 else jnp.where(half_mask(qn, True), o, out)
                    head = quad * 4 + hp * 2 + h
                    lse_new = jnp.where(lane == head, m + jnp.log(total), lse_new)
                if w == 0 and n == 1:
                    tail = (out[qn - 16 :], lse_new[qn - 16 :])
                if w == 1 and n == 0:
                    first = lax.broadcasted_iota(jnp.int32, (16, 128), 0) < 8
                    out = jnp.concatenate([jnp.where(first, tail[0], out[0:16]), out[16:]], axis=0)
                    lse_new = jnp.concatenate([jnp.where(first, tail[1], lse_new[0:16]), lse_new[16:]], axis=0)
                attended[pl.ds(row, qn), pl.ds(lane0, 128)] = out.astype(bf)
                head0 = quad * 4 + hp * 2
                keep = (lane == head0) | (lane == head0 + 1)
                lse[pl.ds(row, qn), :] = jnp.where(keep, lse_new, lse[pl.ds(row, qn), :])
        hook(i)
        return carry

    lax.fori_loop(0, pairs * 2, one, 0)


MESH = pl.DeviceIdType.MESH


class Place:
    def __init__(self):
        self.d = lax.axis_index("dp")
        self.f = lax.axis_index("fsdp")
        self.z = lax.div(self.f, 2)
        self.c = lax.rem(self.f, 2)
        self.dx = self.d + 1 - 2 * lax.rem(self.d, 2)
        self.dy = lax.rem(self.d + 2, 4)
        self.dd = 3 - self.d
        self.sib = self.f + 1 - 2 * self.c
        self.zs = [lax.rem(self.z + n, 4) for n in (1, 2, 3)]
        self.x_dev = (self.dx, self.f)
        self.y_dev = (self.dy, self.f)
        self.sib_dev = (self.d, self.sib)
        self.z_devs = [(self.d, 2 * zz + self.c) for zz in self.zs]

    def barrier(self):
        sem = pltpu.get_barrier_semaphore()
        for dev in [self.x_dev, self.y_dev, self.sib_dev] + self.z_devs:
            pl.semaphore_signal(sem, inc=1, device_id=dev, device_id_type=MESH)
        pl.semaphore_wait(sem, 6)


def remote(src, dst, send, recv, dev):
    return pltpu.make_async_remote_copy(src, dst, send, recv, device_id=dev, device_id_type=MESH)


class Gather:
    def __init__(self, at, shard, whole, send, recv):
        self.at, self.shard, self.whole, self.send, self.recv = at, shard, whole, send, recv
        self.chunks = whole.shape[0]

    def rows(self, zz, q, first, count):
        return pl.ds(pl.multiple_of((2 * zz + self.at.c) * 128 + 32 * q + first, 16), count)

    def push(self, k, rows, stage, dev, src=None):
        dst = self.whole.at[k, rows]
        remote(dst if src is None else src, dst, self.send.at[k], self.recv.at[k, stage], dev).start()

    def landed(self, k, stage, count):
        part = self.whole.at[k, pl.ds(0, count)]
        remote(part, part, self.send.at[k], self.recv.at[k, stage], self.at.x_dev).wait_recv()

    def begin(self, k):
        at = self.at
        quarter = self.shard.at[k, pl.ds(pl.multiple_of(32 * at.d, 16), 32)]
        for dev in at.z_devs:
            self.push(k, self.rows(at.z, at.d, 0, 32), 0, dev, quarter)
        self.push(k, self.rows(at.z, 0, 0, 128), 5, at.sib_dev, self.shard.at[k])

    def spread(self, k):
        at = self.at
        self.landed(k, 0, 96)
        for zz in at.zs:
            self.push(k, self.rows(zz, at.d, 0, 32), 1, at.x_dev)
            self.push(k, self.rows(zz, at.d, 0, 32), 2, at.y_dev)

    def diagonal(self, k):
        at = self.at
        self.landed(k, 1, 96)
        self.landed(k, 2, 96)
        for zz in at.zs:
            self.push(k, self.rows(zz, at.dx, 0, 16), 3, at.y_dev)
            self.push(k, self.rows(zz, at.dy, 16, 16), 4, at.x_dev)

    def pair(self, k):
        at = self.at
        self.landed(k, 3, 48)
        self.landed(k, 4, 48)
        for zz in at.zs:
            self.push(k, self.rows(zz, 0, 0, 128), 5, at.sib_dev)

    def ready(self, k):
        self.landed(k, 5, 512)

    def tick(self, t):
        if t + 3 < self.chunks:
            self.begin(t + 3)
        if 0 <= t - 2 < self.chunks:
            self.pair(t - 2)
        if 0 <= t - 1 < self.chunks:
            self.diagonal(t - 1)
        if 0 <= t < self.chunks:
            self.spread(t)

    def finish(self, k):
        part = self.whole.at[k, pl.ds(0, 896)]
        remote(part, part, self.send.at[k], self.recv.at[k, 0], self.at.x_dev).wait_send()


def spread_vectors(shards, vec, b_up):
    n = vec.shape[1] // 128
    for f in range(n):
        vec[:, 128 * f : 128 * (f + 1)] = shards[f, 0:8, :].astype(f32)
        for i in range(4):
            b_up[f : f + 1, 128 * i : 128 * (i + 1)] = shards[f, 8 + i : 9 + i, :].astype(f32)


def f1_kernel(rows, comm, *refs):
    if comm:
        (tok_h, ohy, ohx, tab, lab_col, lab_row, q_units, k_units, small, ws_h,
         x_h, normed_h, mixed_h, att_h, lse, mid_h, n2_h, vec, b_up, w_h,
         tok, acc, normed, w, mixed, att, bias, n2, lsem, wsem, osem, smalls, ssem, gsend, grecv) = refs
        at = Place()
        gather = Gather(at, ws_h, w_h, gsend, grecv)
        tick = gather.tick
    else:
        (tok_h, ohy, ohx, tab, lab_col, lab_row, q_units, k_units, vec_in, b_up_in, w_h,
         x_h, normed_h, mixed_h, att_h, lse, mid_h, n2_h, vec, b_up,
         tok, acc, normed, w, mixed, att, bias, n2, lsem, wsem, osem) = refs
        tick = lambda t: None
    pairs = rows // PAIR
    RB = PAIR // 7
    blocks = rows // RB

    def wcopy(k, s):
        return pltpu.make_async_copy(w_h.at[k], w.at[s], wsem.at[s])

    load = pltpu.make_async_copy(tok_h, tok, lsem.at[0])
    load.start()
    if comm:
        at.barrier()
        own = smalls.at[at.f]
        smalls[at.f] = small[...]
        for dev in at.z_devs:
            remote(own, own, ssem.at[0], ssem.at[1], dev).start()
        for k in range(3):
            gather.begin(k)
        keep = pltpu.make_async_copy(ws_h, w_h.at[:, pl.ds(pl.multiple_of(at.f * 128, 16), 128)], lsem.at[1])
        keep.start()
    else:
        wcopy(0, 0).start()
        vec[...] = vec_in[...]
        b_up[...] = b_up_in[...]
    fill_bias(bias, lab_col, lab_row, q_units, k_units)
    lse[...] = jnp.zeros_like(lse)
    load.wait()

    def place(r, carry):
        sl = pl.ds(pl.multiple_of(r * RB, 16), RB)
        py = dot(ohy[sl, :], tab[0]) + dot(ohy[sl, :], tab[1]) + dot(ohy[sl, :], tab[2])
        px = dot(ohx[sl, :], tab[0]) + dot(ohx[sl, :], tab[1]) + dot(ohx[sl, :], tab[2])
        acc[sl, :] = tok[sl, :].astype(f32) + jnp.concatenate([py, px], axis=1)
        return carry

    def norm_one(r, carry):
        sl = pl.ds(pl.multiple_of(r * RB, 16), RB)
        xhat, _ = norm_parts(acc[sl, :])
        normed[sl, :] = (xhat * vec[0:1, :] + vec[1:2, :]).astype(bf)
        return carry

    if comm:
        lax.fori_loop(0, blocks // 2, place, 0)
        three = smalls.at[pl.ds(0, 3)]
        remote(three, three, ssem.at[0], ssem.at[1], at.x_dev).wait()
        for zz in [at.z] + at.zs:
            slab = smalls.at[2 * zz + at.c]
            remote(slab, slab, ssem.at[2], ssem.at[3], at.sib_dev).start()
        tick(0)
        lax.fori_loop(blocks // 2, blocks, place, 0)
        four = smalls.at[pl.ds(0, 4)]
        remote(four, four, ssem.at[2], ssem.at[3], at.sib_dev).wait()
        spread_vectors(smalls, vec, b_up)
    else:
        lax.fori_loop(0, blocks, place, 0)
    x_out = pltpu.make_async_copy(acc, x_h, osem.at[0])
    x_out.start()
    tick(1)
    lax.fori_loop(0, blocks, norm_one, 0)
    tick(2)
    n_out = pltpu.make_async_copy(normed, normed_h, osem.at[1])
    n_out.start()
    if comm:
        keep.wait()

    for k in range(QUADS):
        s = k % 2
        if comm:
            gather.ready(k)
            wcopy(k, s).start()
        wcopy(k, s).wait()
        if not comm and k + 1 < QUADS:
            wcopy(k + 1, 1 - s).start()
        if k > 0:
            pltpu.make_async_copy(mixed, mixed_h.at[k - 1], osem.at[2]).wait()
            pltpu.make_async_copy(att, att_h.at[k - 1], osem.at[3]).wait()
        cols = slice(QW * k, QW * (k + 1))
        b_qkv = jnp.concatenate([vec[2:3, cols], jnp.zeros((1, QW), f32), vec[3:4, cols]], axis=1)

        def project(r, carry):
            sl = pl.ds(pl.multiple_of(r * PAIR, 16), PAIR)
            mixed[sl, :] = (dot(normed[sl, :], w[s, :, 0 : 3 * QW]) + b_qkv).astype(bf)
            return carry

        lax.fori_loop(0, pairs, project, 0)
        pltpu.make_async_copy(mixed, mixed_h.at[k], osem.at[2]).start()
        tick(3 + 3 * k)

        def hook(i):
            if comm:
                @pl.when(i == pairs - 1)
                def _():
                    tick(4 + 3 * k)

                @pl.when(i == 2 * pairs - 1)
                def _():
                    tick(5 + 3 * k)

        attention_forward(pairs, mixed, bias, att, lse, k, hook)
        pltpu.make_async_copy(att, att_h.at[k], osem.at[3]).start()
        if k == 0:
            x_out.wait()

        def project_out(r, carry):
            sl = pl.ds(pl.multiple_of(r * PAIR, 16), PAIR)
            extra = vec[4:5, :] if k == 0 else 0.0
            acc[sl, :] += dot(att[sl, :], w[s, :, 3 * QW : CW], NT) + extra
            return carry

        lax.fori_loop(0, pairs, project_out, 0)
    m_out = pltpu.make_async_copy(acc, mid_h, osem.at[0])
    m_out.start()

    def second(r, carry):
        sl = pl.ds(pl.multiple_of(r * RB, 16), RB)
        xhat, _ = norm_parts(acc[sl, :])
        n2[sl, :] = (xhat * vec[5:6, :] + vec[6:7, :]).astype(bf)
        return carry

    lax.fori_loop(0, blocks, second, 0)
    n2_out = pltpu.make_async_copy(n2, n2_h, osem.at[4])
    n2_out.start()
    pltpu.make_async_copy(mixed, mixed_h.at[QUADS - 1], osem.at[2]).wait()
    pltpu.make_async_copy(att, att_h.at[QUADS - 1], osem.at[3]).wait()
    n_out.wait()
    m_out.wait()
    n2_out.wait()
    if comm:
        for k in range(QUADS, gather.chunks):
            gather.ready(k)
        for k in range(gather.chunks):
            gather.finish(k)


def f1(rows, comm, chunks, *args):
    A, V = any_spec(), vmem_spec()
    out_shape = (sds((rows, D), f32), sds((rows, D), bf), sds((QUADS, rows, 3 * QW), bf), sds((QUADS, rows, QW), bf),
                 sds((rows, 128), f32), sds((rows, D), f32), sds((rows, D), bf), sds((8, D), f32), sds((8, FC), f32))
    out_specs = (A, A, A, A, V, A, A, V, V)
    scratch = [
        pltpu.VMEM((rows, D), bf), pltpu.VMEM((rows, D), f32), pltpu.VMEM((rows, D), bf), pltpu.VMEM((2, D, CW), bf),
        pltpu.VMEM((rows, 3 * QW), bf), pltpu.VMEM((rows, QW), bf), pltpu.VMEM((rows // PAIR * 4, QMAX, KEYS), f32),
        pltpu.VMEM((rows, D), bf),
        pltpu.SemaphoreType.DMA((2,)), pltpu.SemaphoreType.DMA((2,)), pltpu.SemaphoreType.DMA((5,)),
    ]
    in_specs = [A, V, V, V, V, V, V, V]
    if comm:
        in_specs += [V, A]
        out_shape += (sds((chunks, D, CW), bf),)
        out_specs += (A,)
        scratch += [pltpu.VMEM((8, 16, 128), bf), pltpu.SemaphoreType.DMA((4,)), pltpu.SemaphoreType.DMA((chunks,)),
                    pltpu.SemaphoreType.DMA((chunks, 6))]
        params = pltpu.CompilerParams(vmem_limit_bytes=VMEM_LIMIT, collective_id=0, has_side_effects=True)
    else:
        in_specs += [V, V, A]
        params = pltpu.CompilerParams(vmem_limit_bytes=VMEM_LIMIT)
    return pl.pallas_call(
        functools.partial(f1_kernel, rows, comm), out_shape=out_shape, in_specs=in_specs, out_specs=out_specs,
        scratch_shapes=scratch, compiler_params=params, name="attention_forward",
    )(*args)


def f2_kernel(rows, n2_h, g_h, mid_h, w_h, b_up, b_down, g2,
              out_h, gm_h, gb_h, gw_h, db_up, db_down, dg2, db2,
              n2, g, n2t, gt, w, act, dhid, acc_o, acc_d, gp, mid, ob, gb, lsem, wsem, osem, msem):
    KP = n2t.shape[1]
    NR = rows // PAIR
    first = QUADS
    chunks = w_h.shape[0] - QUADS

    def wcopy(j, s):
        return pltpu.make_async_copy(w_h.at[first + j], w.at[s], wsem.at[s])

    c1 = pltpu.make_async_copy(n2_h, n2, lsem.at[0])
    c1.start()
    c2 = pltpu.make_async_copy(g_h, g, lsem.at[1])
    c2.start()
    wcopy(0, 0).start()
    n2t[:, rows:KP] = jnp.zeros((D, KP - rows), bf)
    gt[:, rows:KP] = jnp.zeros((D, KP - rows), bf)
    act[rows:KP, :] = jnp.zeros((KP - rows, FC), bf)
    dhid[rows:KP, :] = jnp.zeros((KP - rows, FC), bf)
    acc_o[...] = jnp.zeros_like(acc_o)
    acc_d[...] = jnp.zeros_like(acc_d)
    c1.wait()
    c2.wait()
    transpose_rows(n2, n2t, rows)
    transpose_rows(g, gt, rows)

    def chunk(j, carry):
        s = lax.rem(j, 2)
        wcopy(j, s).wait()

        @pl.when(j + 1 < chunks)
        def _():
            wcopy(j + 1, 1 - s).start()

        def block(r, inner):
            sl = pl.ds(pl.multiple_of(r * PAIR, 16), PAIR)
            h = dot(n2[sl, :], w[s, :, 0:FC]) + b_up[pl.ds(j, 1), :]
            da = dot(g[sl, :], w[s, :, FC:CW])
            phi = 0.5 * (1.0 + lax.erf(h * 0.7071067811865476))
            slope = phi + h * (jnp.exp(-0.5 * h * h) * 0.3989422804014327)
            a = (h * phi).astype(bf)
            dh = (da * slope).astype(bf)
            act[sl, :] = a
            dhid[sl, :] = dh
            acc_o[sl, :] += dot(a, w[s, :, FC:CW], NT)
            acc_d[sl, :] += dot(dh, w[s, :, 0:FC], NT)
            return inner

        lax.fori_loop(0, NR, block, 0)
        db_up[pl.ds(j, 1), :] = dot(jnp.ones((8, KP), bf), dhid[...])[0:1]

        @pl.when(j > 0)
        def _():
            pltpu.make_async_copy(gp, gw_h.at[j - 1], osem.at[0]).wait()

        def grads(m, inner):
            sl = pl.ds(pl.multiple_of(m * 512, 512), 512)
            gp[sl, 0:FC] = dot(n2t[sl, :], dhid[...]).astype(bf)
            gp[sl, FC:CW] = dot(gt[sl, :], act[...]).astype(bf)
            return inner

        lax.fori_loop(0, D // 512, grads, 0)
        pltpu.make_async_copy(gp, gw_h.at[j], osem.at[0]).start()
        return carry

    lax.fori_loop(0, chunks, chunk, 0)
    RB = PAIR // 7
    blocks = rows // RB

    def mcopy(r, s):
        return pltpu.make_async_copy(mid_h.at[pl.ds(pl.multiple_of(r * RB, 16), RB)], mid.at[s], msem.at[s])

    mcopy(0, 0).start()
    dg2[...] = jnp.zeros_like(dg2)
    db2[...] = jnp.zeros_like(db2)
    db_down[...] = jnp.zeros_like(db_down)

    def last(r, carry):
        s = lax.rem(r, 2)
        sl = pl.ds(pl.multiple_of(r * RB, 16), RB)
        mcopy(r, s).wait()

        @pl.when(r + 1 < blocks)
        def _():
            mcopy(r + 1, 1 - s).start()

        middle = mid[s]
        ob[sl, :] = (middle + acc_o[sl, :] + b_down[...]).astype(bf)
        xhat, inv = norm_parts(middle)
        dn = acc_d[sl, :]
        cot = g[sl, :].astype(f32)
        e = dn * g2[...]
        gm = cot + (e - jnp.mean(e, axis=-1, keepdims=True) - xhat * jnp.mean(e * xhat, axis=-1, keepdims=True)) * inv
        acc_d[sl, :] = gm
        gb[sl, :] = gm.astype(bf)
        dg2[...] += jnp.sum(dn * xhat, axis=0, keepdims=True)
        db2[...] += jnp.sum(dn, axis=0, keepdims=True)
        db_down[...] += jnp.sum(cot, axis=0, keepdims=True)
        return carry

    lax.fori_loop(0, blocks, last, 0)
    outs = [pltpu.make_async_copy(acc_d, gm_h, osem.at[1]), pltpu.make_async_copy(ob, out_h, osem.at[2]),
            pltpu.make_async_copy(gb, gb_h, osem.at[3])]
    for o in outs:
        o.start()
    pltpu.make_async_copy(gp, gw_h.at[chunks - 1], osem.at[0]).wait()
    for o in outs:
        o.wait()


def f2(rows, n2, g, mid, w, b_up, b_down, g2):
    A, V = any_spec(), vmem_spec()
    KP = -(-rows // 256) * 256
    chunks = w.shape[0] - QUADS
    RB = PAIR // 7
    return pl.pallas_call(
        functools.partial(f2_kernel, rows),
        out_shape=(sds((rows, D), bf), sds((rows, D), f32), sds((rows, D), bf), sds((chunks, D, CW), bf), sds((chunks, FC), f32),
                   sds((1, D), f32), sds((1, D), f32), sds((1, D), f32)),
        in_specs=[A, A, A, A, V, V, V],
        out_specs=(A, A, A, A, V, V, V, V),
        scratch_shapes=[
            pltpu.VMEM((rows, D), bf), pltpu.VMEM((rows, D), bf), pltpu.VMEM((D, KP), bf), pltpu.VMEM((D, KP), bf),
            pltpu.VMEM((2, D, CW), bf), pltpu.VMEM((KP, FC), bf), pltpu.VMEM((KP, FC), bf),
            pltpu.VMEM((rows, D), f32), pltpu.VMEM((rows, D), f32), pltpu.VMEM((D, CW), bf),
            pltpu.VMEM((2, RB, D), f32), pltpu.VMEM((rows, D), bf), pltpu.VMEM((rows, D), bf),
            pltpu.SemaphoreType.DMA((2,)), pltpu.SemaphoreType.DMA((2,)), pltpu.SemaphoreType.DMA((4,)),
            pltpu.SemaphoreType.DMA((2,)),
        ],
        compiler_params=pltpu.CompilerParams(vmem_limit_bytes=VMEM_LIMIT),
        name="feed_forward",
    )(n2, g, mid, w, b_up, b_down, g2)


def attention_backward(pairs, mixed, datt, bias, lse, dmixed, dq, dk, dv, quad):
    def one(i, carry):
        p, hp = i // 2, lax.rem(i, 2)
        base = pl.multiple_of(p * PAIR, 16)
        lane0 = pl.multiple_of(hp * 128, 128)
        dq[...] = jnp.zeros_like(dq)
        dk[...] = jnp.zeros_like(dk)
        dv[...] = jnp.zeros_like(dv)
        for w, (start, halves) in enumerate(WINDOWS):
            for n, (q0, qn, k0) in enumerate(halves):
                at = start + q0
                row = pl.multiple_of(base + at, 16)
                kat = start + k0
                keys = pl.ds(pl.multiple_of(base + kat, 16), KEYS)
                q2 = mixed[pl.ds(row, qn), pl.ds(lane0, 128)] * jnp.asarray(SCALE, bf)
                k2 = mixed[keys, pl.ds(pl.multiple_of(lane0 + QW, 128), 128)]
                v2 = mixed[keys, pl.ds(pl.multiple_of(lane0 + 2 * QW, 128), 128)]
                do2 = datt[pl.ds(row, qn), pl.ds(lane0, 128)]
                lse_rows = lse[pl.ds(row, qn), :]
                lane = lax.broadcasted_iota(jnp.int32, (qn, 128), 1)
                idx = p * 4 + w * 2 + n
                dqs = None
                for h in range(2):
                    mask = half_mask(qn, h == 1)
                    kmask = half_mask(KEYS, h == 1)
                    qm = jnp.where(mask, q2, jnp.zeros_like(q2))
                    dom = jnp.where(mask, do2, jnp.zeros_like(do2))
                    head = quad * 4 + hp * 2 + h
                    row_lse = jnp.sum(jnp.where(lane == head, lse_rows, 0.0), axis=-1, keepdims=True)
                    s = dot(qm, k2, NT) + bias[idx, 0:qn, :]
                    probs = jnp.exp(s - row_lse)
                    dp = dot(dom, v2, NT)
                    inner = jnp.sum(probs * dp, axis=-1, keepdims=True)
                    ds = (probs * (dp - inner)).astype(bf)
                    dv[kat : kat + KEYS, :] += dot(probs.astype(bf), dom, TN)
                    dk[kat : kat + KEYS, :] += dot(ds, qm, TN)
                    part = dot(ds, k2)
                    dqs = part if h == 0 else jnp.where(mask, part, dqs)
                dq[at : at + qn, :] += dqs
        rows = pl.ds(base, PAIR)
        dmixed[rows, pl.ds(lane0, 128)] = (dq[...] * SCALE).astype(bf)
        dmixed[rows, pl.ds(pl.multiple_of(lane0 + QW, 128), 128)] = dk[...].astype(bf)
        dmixed[rows, pl.ds(pl.multiple_of(lane0 + 2 * QW, 128), 128)] = dv[...].astype(bf)
        return carry

    lax.fori_loop(0, pairs * 2, one, 0)


def f3_kernel(rows, gb_h, normed_h, w_h, mixed_h, att_h, lse, x_h, gm_h, g1, lab_col, lab_row, q_units, k_units,
              gt_h, gw_h, db_qkv, db_out, dg1, db1,
              gb, normed, gbt, normedt, w, mixed, att, datt, dmixed, bias, acc, dq, dk, dv, gp, xb, gmb, ob,
              lsem, wsem, isem, osem, xsem, gsem, tsem):
    KP = gbt.shape[1]
    pairs = rows // PAIR

    def inputs(k, s):
        return (pltpu.make_async_copy(w_h.at[k], w.at[s], wsem.at[s]),
                pltpu.make_async_copy(mixed_h.at[k], mixed.at[s], isem.at[s, 0]),
                pltpu.make_async_copy(att_h.at[k], att.at[s, pl.ds(0, rows)], isem.at[s, 1]))

    c1 = pltpu.make_async_copy(gb_h, gb, lsem.at[0])
    c1.start()
    c2 = pltpu.make_async_copy(normed_h, normed, lsem.at[1])
    c2.start()
    for c in inputs(0, 0):
        c.start()
    gbt[:, rows:KP] = jnp.zeros((D, KP - rows), bf)
    normedt[:, rows:KP] = jnp.zeros((D, KP - rows), bf)
    dmixed[rows:KP, :] = jnp.zeros((KP - rows, 3 * QW), bf)
    for s in range(2):
        att[s, rows:KP, :] = jnp.zeros((KP - rows, QW), bf)
    fill_bias(bias, lab_col, lab_row, q_units, k_units)
    c1.wait()
    c2.wait()
    transpose_rows(gb, gbt, rows)
    transpose_rows(normed, normedt, rows)
    db_out[...] = dot(jnp.ones((8, rows), bf), gb[...])[0:1]

    def quad(k, carry):
        s = lax.rem(k, 2)
        for c in inputs(k, s):
            c.wait()

        @pl.when(k + 1 < QUADS)
        def _():
            for c in inputs(k + 1, 1 - s):
                c.start()

        def back(r, inner):
            sl = pl.ds(pl.multiple_of(r * PAIR, 16), PAIR)
            datt[sl, :] = dot(gb[sl, :], w[s, :, 3 * QW : CW]).astype(bf)
            return inner

        lax.fori_loop(0, pairs, back, 0)
        attention_backward(pairs, mixed.at[s], datt, bias, lse, dmixed, dq, dk, dv, k)
        db_qkv[pl.ds(k, 1), :] = dot(jnp.ones((8, KP), bf), dmixed[...])[0:1]

        @pl.when(k > 0)
        def _():
            pltpu.make_async_copy(gp, gw_h.at[k - 1], osem.at[0]).wait()

        def grads(m, inner):
            sl = pl.ds(pl.multiple_of(m * 512, 512), 512)
            gp[sl, 0 : 3 * QW] = dot(normedt[sl, :], dmixed[...]).astype(bf)
            gp[sl, 3 * QW : CW] = dot(gbt[sl, :], att[s]).astype(bf)
            return inner

        lax.fori_loop(0, D // 512, grads, 0)
        pltpu.make_async_copy(gp, gw_h.at[k], osem.at[0]).start()

        def back_in(r, inner):
            sl = pl.ds(pl.multiple_of(r * PAIR, 16), PAIR)
            new = dot(dmixed[sl, :], w[s, :, 0 : 3 * QW], NT)
            acc[sl, :] = jnp.where(k == 0, new, acc[sl, :] + new)
            return inner

        lax.fori_loop(0, pairs, back_in, 0)
        return carry

    lax.fori_loop(0, QUADS, quad, 0)
    RB = PAIR // 7
    blocks = rows // RB

    def part(r):
        return pl.ds(pl.multiple_of(r * RB, 16), RB)

    def rcopies(r, s):
        return (pltpu.make_async_copy(x_h.at[part(r)], xb.at[s], xsem.at[s]),
                pltpu.make_async_copy(gm_h.at[part(r)], gmb.at[s], gsem.at[s]))

    for c in rcopies(0, 0):
        c.start()
    dg1[...] = jnp.zeros_like(dg1)
    db1[...] = jnp.zeros_like(db1)

    def last(r, carry):
        s = lax.rem(r, 2)
        for c in rcopies(r, s):
            c.wait()

        @pl.when(r + 1 < blocks)
        def _():
            for c in rcopies(r + 1, 1 - s):
                c.start()

        @pl.when(r >= 2)
        def _():
            pltpu.make_async_copy(ob.at[s], gt_h.at[part(r - 2)], tsem.at[s]).wait()

        xhat, inv = norm_parts(xb[s])
        dn = acc[part(r), :]
        e = dn * g1[...]
        ob[s] = gmb[s] + (e - jnp.mean(e, axis=-1, keepdims=True) - xhat * jnp.mean(e * xhat, axis=-1, keepdims=True)) * inv
        pltpu.make_async_copy(ob.at[s], gt_h.at[part(r)], tsem.at[s]).start()
        dg1[...] += jnp.sum(dn * xhat, axis=0, keepdims=True)
        db1[...] += jnp.sum(dn, axis=0, keepdims=True)
        return carry

    lax.fori_loop(0, blocks, last, 0)
    for r in (blocks - 2, blocks - 1):
        pltpu.make_async_copy(ob.at[r % 2], gt_h.at[part(r)], tsem.at[r % 2]).wait()
    pltpu.make_async_copy(gp, gw_h.at[QUADS - 1], osem.at[0]).wait()


def f3(rows, gb, normed, w, mixed, att, lse, x, gm, g1, lab_col, lab_row, q_units, k_units):
    A, V = any_spec(), vmem_spec()
    KP = -(-rows // 256) * 256
    RB = PAIR // 7
    return pl.pallas_call(
        functools.partial(f3_kernel, rows),
        out_shape=(sds((rows, D), f32), sds((QUADS, D, CW), bf), sds((QUADS, 3 * QW), f32), sds((1, D), f32), sds((1, D), f32),
                   sds((1, D), f32)),
        in_specs=[A, A, A, A, A, V, A, A, V, V, V, V, V],
        out_specs=(A, A, V, V, V, V),
        scratch_shapes=[
            pltpu.VMEM((rows, D), bf), pltpu.VMEM((rows, D), bf), pltpu.VMEM((D, KP), bf), pltpu.VMEM((D, KP), bf),
            pltpu.VMEM((2, D, CW), bf), pltpu.VMEM((2, rows, 3 * QW), bf), pltpu.VMEM((2, KP, QW), bf), pltpu.VMEM((rows, QW), bf),
            pltpu.VMEM((KP, 3 * QW), bf), pltpu.VMEM((rows // PAIR * 4, QMAX, KEYS), f32), pltpu.VMEM((rows, D), f32),
            pltpu.VMEM((PAIR, 128), f32), pltpu.VMEM((PAIR, 128), f32), pltpu.VMEM((PAIR, 128), f32), pltpu.VMEM((D, CW), bf),
            pltpu.VMEM((2, RB, D), f32), pltpu.VMEM((2, RB, D), f32), pltpu.VMEM((2, RB, D), f32),
            pltpu.SemaphoreType.DMA((2,)), pltpu.SemaphoreType.DMA((2,)), pltpu.SemaphoreType.DMA((2, 2)),
            pltpu.SemaphoreType.DMA((1,)), pltpu.SemaphoreType.DMA((2,)), pltpu.SemaphoreType.DMA((2,)),
            pltpu.SemaphoreType.DMA((2,)),
        ],
        compiler_params=pltpu.CompilerParams(vmem_limit_bytes=VMEM_LIMIT),
        name="attention_backward",
    )(gb, normed, w, mixed, att, lse, x, gm, g1, lab_col, lab_row, q_units, k_units)


def unit_labels(band_code):
    units = band_code.reshape(-1, UNITS_MB)
    labels = jnp.cumsum((units <= 1).astype(jnp.int32), axis=1) + 16 * jnp.arange(units.shape[0], dtype=jnp.int32)[:, None]
    return labels.reshape(-1).astype(f32)


def window_units(rows):
    units = rows // UNIT
    queries, keys = [], []
    for p in range(rows // PAIR):
        for w, (start, halves) in enumerate(WINDOWS):
            for q0, qn, k0 in halves:
                q = p * PAIR + start + q0 + np.arange(QMAX)
                inside = (q >= p * PAIR + w * BUF) & (q < p * PAIR + (w + 1) * BUF)
                queries.append((q[:, None] // UNIT == np.arange(units)) & inside[:, None])
                k = p * PAIR + start + k0 + np.arange(KEYS)
                keys.append(np.arange(units)[:, None] == k // UNIT)
    return jnp.asarray(np.stack(queries), bf), jnp.asarray(np.stack(keys), bf)


def place_table(gsd_code):
    ratio = jnp.exp2((gsd_code.astype(f32) - 3.0) * 0.5)
    quarter = D // 4
    freq = jnp.exp2(jnp.arange(quarter, dtype=f32) * (-math.log2(10000.0) / quarter))
    a = jnp.arange(GRID, dtype=f32)
    angle = (a[None, :] * ratio[:, None]).reshape(-1)[:, None] * freq[None, :]
    tab = jnp.concatenate([jnp.sin(angle), jnp.cos(angle)], axis=1)
    n = tab.shape[0]
    pad = -(-n // 256) * 256
    tab = jnp.pad(tab, ((0, pad - n), (0, 0)))
    hi = lax.reduce_precision(tab, 8, 7)
    rest = tab - hi
    mid = lax.reduce_precision(rest, 8, 7)
    return jnp.stack([hi, mid, rest - mid]).astype(bf)


def one_hots(rows, width):
    r = np.arange(rows)
    col = np.arange(width)
    ohy = (r[:, None] // GRID == col[None, :])
    ohx = ((r // UNIT * GRID + r % GRID)[:, None] == col[None, :])
    return jnp.asarray(ohy, bf), jnp.asarray(ohx, bf)


def pack_weights(qkv, out, up, down):
    n = qkv.shape[0]
    att = jnp.concatenate([qkv.reshape(n, 3, QUADS, QW).transpose(2, 0, 1, 3).reshape(QUADS, n, 3 * QW),
                           out.T.reshape(n, QUADS, QW).transpose(1, 0, 2)], axis=2)
    ff = up.shape[1] // FC
    feed = jnp.concatenate([up.reshape(n, ff, FC).transpose(1, 0, 2), down.T.reshape(n, ff, FC).transpose(1, 0, 2)], axis=2)
    return jnp.concatenate([att, feed], axis=0)


def local(dp, fsdp, tokens, band_code, gsd_code, norm1_gain, norm1_bias, qkv_weight, bias_q, bias_v, out_weight, bias_out,
          norm2_gain, norm2_bias, up_weight, bias_up, down_weight, bias_down, grad_out):
    rows = tokens.shape[0]
    comm = dp == 4 and fsdp == 8
    shard = pack_weights(qkv_weight, out_weight, up_weight, down_weight)
    n = shard.shape[1]
    chunks = shard.shape[0]
    vectors = (norm1_gain, norm1_bias, bias_q, bias_v, bias_out, norm2_gain, norm2_bias, bias_down)
    labels = unit_labels(band_code)
    tab = place_table(gsd_code)
    ohy, ohx = one_hots(rows, tab.shape[1])
    q_units, k_units = window_units(rows)
    lab = (labels.reshape(-1, 1), labels.reshape(1, -1), q_units, k_units)
    if comm:
        small = jnp.concatenate([jnp.stack(vectors), bias_up.reshape(4, 128), jnp.zeros((4, 128), bf)])
        x, normed, mixed, att, lse, mid, n2, vec, b_up, w = f1(rows, True, chunks, tokens, ohy, ohx, tab, *lab, small, shard)
    else:
        gathered = lax.all_gather(jnp.stack(vectors), "fsdp", axis=1, tiled=True).astype(f32)
        up_bias = lax.all_gather(bias_up, "fsdp", axis=0, tiled=True).astype(f32).reshape(-1, FC)
        w = lax.all_gather(shard, "fsdp", axis=1, tiled=True)
        x, normed, mixed, att, lse, mid, n2, vec, b_up = f1(rows, False, chunks, tokens, ohy, ohx, tab, *lab, gathered, up_bias, w)
    out, gm, gb, gw_ff, db_up, db_down, dg2, db2 = f2(rows, n2, grad_out, mid, w, b_up, vec[7:8], vec[5:6])
    grad_tokens, gw_att, db_qkv, db_out, dg1, db1 = f3(rows, gb, normed, w, mixed, att, lse, x, gm, vec[0:1], *lab)
    small_grads = jnp.concatenate([dg1, db1, db_qkv[:, 0:QW].reshape(1, D), db_qkv[:, 2 * QW :].reshape(1, D), db_out, dg2, db2,
                                   db_down], axis=0)
    small_grads = jnp.concatenate([small_grads.reshape(8, fsdp, n).transpose(1, 0, 2).reshape(fsdp, 8 * n),
                                   db_up.reshape(fsdp, 4 * n)], axis=1)
    gw = jnp.concatenate([gw_att, gw_ff], axis=0)
    gw = lax.psum(lax.psum_scatter(gw, "fsdp", scatter_dimension=1, tiled=True), "dp").astype(f32)
    sg = lax.psum(lax.psum_scatter(small_grads, "fsdp", scatter_dimension=0, tiled=True), "dp").reshape(12, n)
    g_att, g_ff = gw[:QUADS], gw[QUADS:]
    g_qkv = g_att[:, :, : 3 * QW].reshape(QUADS, n, 3, QW).transpose(1, 2, 0, 3).reshape(n, 3 * D)
    g_out = g_att[:, :, 3 * QW :].transpose(0, 2, 1).reshape(D, n)
    g_up = g_ff[:, :, :FC].transpose(1, 0, 2).reshape(n, -1)
    g_down = g_ff[:, :, FC:].transpose(0, 2, 1).reshape(-1, n)
    return (out, grad_tokens, sg[0], sg[1], g_qkv, sg[2], sg[3], g_out, sg[4], sg[5], sg[6], g_up, sg[8:12].reshape(4 * n), g_down, sg[7])


def solution(mesh):
    rows, vec, first, second = P(("dp", "fsdp"), None), P("fsdp"), P("fsdp", None), P(None, "fsdp")
    codes = P(("dp", "fsdp"))
    return jax.shard_map(
        functools.partial(local, mesh.shape["dp"], mesh.shape["fsdp"]),
        mesh=mesh,
        in_specs=(rows, codes, codes, vec, vec, first, vec, vec, second, vec, vec, vec, first, vec, second, vec, rows),
        out_specs=(rows, rows, vec, vec, first, vec, vec, second, vec, vec, vec, first, vec, second, vec),
        check_vma=False,
    )
```

```python
import functools
import math

import jax
import jax.numpy as jnp
import numpy as np
from jax import lax
from jax.experimental import pallas as pl
from jax.experimental.pallas import tpu as pltpu
from jax.sharding import PartitionSpec as P

bf = jnp.bfloat16
f32 = jnp.float32
NN = (((1,), (0,)), ((), ()))
NT = (((1,), (1,)), ((), ()))
TN = (((0,), (0,)), ((), ()))
D = 1024
HEADS = 16
HEAD_DIM = 64
GRID = 7
UNIT = GRID * GRID
UNITS_MB = 8
BUF = UNIT * UNITS_MB
PAIR = 2 * BUF
QUADS = 4
QW = 256
FC = 512
CW = 1024
EPS = 1e-6
SCALE = 0.125
NEG = -1e30
VMEM_LIMIT = 60 << 20
KEYS = 384
WINDOWS = ((0, ((0, 192, 0), (192, 208, 16))), (384, ((0, 192, 0), (192, 208, 16))))
QMAX = 208


def dot(a, b, dims=NN):
    return lax.dot_general(a, b, dims, preferred_element_type=f32)


def any_spec():
    return pl.BlockSpec(memory_space=pl.ANY)


def vmem_spec():
    return pl.BlockSpec(memory_space=pltpu.VMEM)


def sds(shape, kind):
    return jax.ShapeDtypeStruct(shape, kind)


def norm_parts(v):
    center = v - jnp.mean(v, axis=-1, keepdims=True)
    inv = lax.rsqrt(jnp.mean(center * center, axis=-1, keepdims=True) + EPS)
    return center * inv, inv


def transpose_rows(src, dst, rows):
    full = rows // 128

    def one(i, carry):
        o = pl.multiple_of(i * 128, 128)
        dst[:, pl.ds(o, 128)] = src[pl.ds(o, 128), :].T
        return carry

    lax.fori_loop(0, full, one, 0)
    if rows % 128:
        dst[:, full * 128 : rows] = src[full * 128 : rows, :].T


def fill_bias(bias, lab_col, lab_row, q_units, k_units):
    same = jnp.where(lab_col[...] == lab_row[...], 1.0, 0.0).astype(bf)

    def one(i, carry):
        reach = dot(q_units[i], same).astype(bf)
        bias[i] = (dot(reach, k_units[i]) - 1.0) * -NEG
        return carry

    lax.fori_loop(0, bias.shape[0], one, 0)


def half_mask(rows, second):
    lane = lax.broadcasted_iota(jnp.int32, (rows, 128), 1)
    return lane >= 64 if second else lane < 64


def attention_forward(pairs, mixed, bias, attended, lse, quad, hook):
    def one(i, carry):
        p, hp = i // 2, lax.rem(i, 2)
        base = pl.multiple_of(p * PAIR, 16)
        lane0 = pl.multiple_of(hp * 128, 128)
        tail = None
        for w, (start, halves) in enumerate(WINDOWS):
            for n, (q0, qn, k0) in enumerate(halves):
                row = pl.multiple_of(base + start + q0, 16)
                keys = pl.ds(pl.multiple_of(base + start + k0, 16), KEYS)
                q2 = mixed[pl.ds(row, qn), pl.ds(lane0, 128)] * jnp.asarray(SCALE, bf)
                k2 = mixed[keys, pl.ds(pl.multiple_of(lane0 + QW, 128), 128)]
                v2 = mixed[keys, pl.ds(pl.multiple_of(lane0 + 2 * QW, 128), 128)]
                idx = p * 4 + w * 2 + n
                out = None
                lse_new = jnp.zeros((qn, 128), f32)
                lane = lax.broadcasted_iota(jnp.int32, (qn, 128), 1)
                for h in range(2):
                    qm = jnp.where(half_mask(qn, h == 1), q2, jnp.zeros_like(q2))
                    s = dot(qm, k2, NT) + bias[idx, 0:qn, :]
                    m = jnp.max(s, axis=-1, keepdims=True)
                    e = jnp.exp(s - m)
                    total = jnp.sum(e, axis=-1, keepdims=True)
                    probs = (e * (1.0 / total)).astype(bf)
                    o = dot(probs, v2)
                    out = o if h == 0 else jnp.where(half_mask(qn, True), o, out)
                    head = quad * 4 + hp * 2 + h
                    lse_new = jnp.where(lane == head, m + jnp.log(total), lse_new)
                if w == 0 and n == 1:
                    tail = (out[qn - 16 :], lse_new[qn - 16 :])
                if w == 1 and n == 0:
                    first = lax.broadcasted_iota(jnp.int32, (16, 128), 0) < 8
                    out = jnp.concatenate([jnp.where(first, tail[0], out[0:16]), out[16:]], axis=0)
                    lse_new = jnp.concatenate([jnp.where(first, tail[1], lse_new[0:16]), lse_new[16:]], axis=0)
                attended[pl.ds(row, qn), pl.ds(lane0, 128)] = out.astype(bf)
                head0 = quad * 4 + hp * 2
                keep = (lane == head0) | (lane == head0 + 1)
                lse[pl.ds(row, qn), :] = jnp.where(keep, lse_new, lse[pl.ds(row, qn), :])
        hook(i)
        return carry

    lax.fori_loop(0, pairs * 2, one, 0)


MESH = pl.DeviceIdType.MESH


def kernel_params(comm, number):
    if comm:
        return pltpu.CompilerParams(vmem_limit_bytes=VMEM_LIMIT, collective_id=number, has_side_effects=True)
    return pltpu.CompilerParams(vmem_limit_bytes=VMEM_LIMIT)


def grad_shape(comm, chunks):
    return sds((chunks, 128, CW) if comm else (chunks, 4, 256, CW), bf)


class Place:
    def __init__(self):
        self.d = lax.axis_index("dp")
        self.f = lax.axis_index("fsdp")
        self.z = lax.div(self.f, 2)
        self.c = lax.rem(self.f, 2)
        self.dx = self.d + 1 - 2 * lax.rem(self.d, 2)
        self.dy = lax.rem(self.d + 2, 4)
        self.dd = 3 - self.d
        self.sib = self.f + 1 - 2 * self.c
        self.zs = [lax.rem(self.z + n, 4) for n in (1, 2, 3)]
        self.x_dev = (self.dx, self.f)
        self.y_dev = (self.dy, self.f)
        self.sib_dev = (self.d, self.sib)
        self.z_devs = [(self.d, 2 * zz + self.c) for zz in self.zs]

    def barrier(self):
        sem = pltpu.get_barrier_semaphore()
        for dev in [self.x_dev, self.y_dev, self.sib_dev] + self.z_devs:
            pl.semaphore_signal(sem, inc=1, device_id=dev, device_id_type=MESH)
        pl.semaphore_wait(sem, 6)


def remote(src, dst, send, recv, dev):
    return pltpu.make_async_remote_copy(src, dst, send, recv, device_id=dev, device_id_type=MESH)


class Gather:
    def __init__(self, at, shard, whole, send, recv):
        self.at, self.shard, self.whole, self.send, self.recv = at, shard, whole, send, recv
        self.chunks = whole.shape[0]

    def rows(self, zz, q, first, count):
        return pl.ds(pl.multiple_of((2 * zz + self.at.c) * 128 + 32 * q + first, 16), count)

    def push(self, k, rows, stage, dev, src=None):
        dst = self.whole.at[k, rows]
        remote(dst if src is None else src, dst, self.send.at[k], self.recv.at[k, stage], dev).start()

    def landed(self, k, stage, count):
        part = self.whole.at[k, pl.ds(0, count)]
        remote(part, part, self.send.at[k], self.recv.at[k, stage], self.at.x_dev).wait_recv()

    def begin(self, k):
        at = self.at
        quarter = self.shard.at[k, pl.ds(pl.multiple_of(32 * at.d, 16), 32)]
        for dev in at.z_devs:
            self.push(k, self.rows(at.z, at.d, 0, 32), 0, dev, quarter)
        self.push(k, self.rows(at.z, 0, 0, 128), 5, at.sib_dev, self.shard.at[k])

    def spread(self, k):
        at = self.at
        self.landed(k, 0, 96)
        for zz in at.zs:
            self.push(k, self.rows(zz, at.d, 0, 32), 1, at.x_dev)
            self.push(k, self.rows(zz, at.d, 0, 32), 2, at.y_dev)

    def diagonal(self, k):
        at = self.at
        self.landed(k, 1, 96)
        self.landed(k, 2, 96)
        for zz in at.zs:
            self.push(k, self.rows(zz, at.dx, 0, 16), 3, at.y_dev)
            self.push(k, self.rows(zz, at.dy, 16, 16), 4, at.x_dev)

    def pair(self, k):
        at = self.at
        self.landed(k, 3, 48)
        self.landed(k, 4, 48)
        for zz in at.zs:
            self.push(k, self.rows(zz, 0, 0, 128), 5, at.sib_dev)

    def ready(self, k):
        self.landed(k, 5, 512)

    def tick(self, t):
        if t + 3 < self.chunks:
            self.begin(t + 3)
        if 0 <= t - 2 < self.chunks:
            self.pair(t - 2)
        if 0 <= t - 1 < self.chunks:
            self.diagonal(t - 1)
        if 0 <= t < self.chunks:
            self.spread(t)

    def finish(self, k):
        part = self.whole.at[k, pl.ds(0, 896)]
        remote(part, part, self.send.at[k], self.recv.at[k, 0], self.at.x_dev).wait_send()


def spread_vectors(shards, vec, b_up):
    n = vec.shape[1] // 128
    for f in range(n):
        vec[:, 128 * f : 128 * (f + 1)] = shards[f, 0:8, :].astype(f32)
        for i in range(4):
            b_up[f : f + 1, 128 * i : 128 * (i + 1)] = shards[f, 8 + i : 9 + i, :].astype(f32)


def f1_kernel(rows, comm, *refs):
    if comm:
        (tok_h, ohy, ohx, tab, lab_col, lab_row, q_units, k_units, small, ws_h,
         x_h, normed_h, mixed_h, att_h, lse, mid_h, n2_h, vec, b_up, w_h,
         tok, acc, normed, w, mixed, att, bias, n2, lsem, wsem, osem, smalls, ssem, gsend, grecv) = refs
        at = Place()
        gather = Gather(at, ws_h, w_h, gsend, grecv)
        tick = gather.tick
    else:
        (tok_h, ohy, ohx, tab, lab_col, lab_row, q_units, k_units, vec_in, b_up_in, w_h,
         x_h, normed_h, mixed_h, att_h, lse, mid_h, n2_h, vec, b_up,
         tok, acc, normed, w, mixed, att, bias, n2, lsem, wsem, osem) = refs
        tick = lambda t: None
    pairs = rows // PAIR
    RB = PAIR // 7
    blocks = rows // RB

    def wcopy(k, s):
        return pltpu.make_async_copy(w_h.at[k], w.at[s], wsem.at[s])

    load = pltpu.make_async_copy(tok_h, tok, lsem.at[0])
    load.start()
    if comm:
        at.barrier()
        own = smalls.at[at.f]
        smalls[at.f] = small[...]
        for dev in at.z_devs:
            remote(own, own, ssem.at[0], ssem.at[1], dev).start()
        for k in range(3):
            gather.begin(k)
        keep = pltpu.make_async_copy(ws_h, w_h.at[:, pl.ds(pl.multiple_of(at.f * 128, 16), 128)], lsem.at[1])
        keep.start()
    else:
        wcopy(0, 0).start()
        vec[...] = vec_in[...]
        b_up[...] = b_up_in[...]
    fill_bias(bias, lab_col, lab_row, q_units, k_units)
    lse[...] = jnp.zeros_like(lse)
    load.wait()

    def place(r, carry):
        sl = pl.ds(pl.multiple_of(r * RB, 16), RB)
        py = dot(ohy[sl, :], tab[0]) + dot(ohy[sl, :], tab[1]) + dot(ohy[sl, :], tab[2])
        px = dot(ohx[sl, :], tab[0]) + dot(ohx[sl, :], tab[1]) + dot(ohx[sl, :], tab[2])
        acc[sl, :] = tok[sl, :].astype(f32) + jnp.concatenate([py, px], axis=1)
        return carry

    def norm_one(r, carry):
        sl = pl.ds(pl.multiple_of(r * RB, 16), RB)
        xhat, _ = norm_parts(acc[sl, :])
        normed[sl, :] = (xhat * vec[0:1, :] + vec[1:2, :]).astype(bf)
        return carry

    if comm:
        lax.fori_loop(0, blocks // 2, place, 0)
        three = smalls.at[pl.ds(0, 3)]
        remote(three, three, ssem.at[0], ssem.at[1], at.x_dev).wait()
        for zz in [at.z] + at.zs:
            slab = smalls.at[2 * zz + at.c]
            remote(slab, slab, ssem.at[2], ssem.at[3], at.sib_dev).start()
        tick(0)
        lax.fori_loop(blocks // 2, blocks, place, 0)
        four = smalls.at[pl.ds(0, 4)]
        remote(four, four, ssem.at[2], ssem.at[3], at.sib_dev).wait()
        spread_vectors(smalls, vec, b_up)
    else:
        lax.fori_loop(0, blocks, place, 0)
    x_out = pltpu.make_async_copy(acc, x_h, osem.at[0])
    x_out.start()
    tick(1)
    lax.fori_loop(0, blocks, norm_one, 0)
    tick(2)
    n_out = pltpu.make_async_copy(normed, normed_h, osem.at[1])
    n_out.start()
    if comm:
        keep.wait()

    for k in range(QUADS):
        s = k % 2
        if comm:
            gather.ready(k)
            wcopy(k, s).start()
        wcopy(k, s).wait()
        if not comm and k + 1 < QUADS:
            wcopy(k + 1, 1 - s).start()
        if k > 0:
            pltpu.make_async_copy(mixed, mixed_h.at[k - 1], osem.at[2]).wait()
            pltpu.make_async_copy(att, att_h.at[k - 1], osem.at[3]).wait()
        cols = slice(QW * k, QW * (k + 1))
        b_qkv = jnp.concatenate([vec[2:3, cols], jnp.zeros((1, QW), f32), vec[3:4, cols]], axis=1)

        def project(r, carry):
            sl = pl.ds(pl.multiple_of(r * PAIR, 16), PAIR)
            mixed[sl, :] = (dot(normed[sl, :], w[s, :, 0 : 3 * QW]) + b_qkv).astype(bf)
            return carry

        lax.fori_loop(0, pairs, project, 0)
        pltpu.make_async_copy(mixed, mixed_h.at[k], osem.at[2]).start()
        tick(3 + 3 * k)

        def hook(i):
            if comm:
                @pl.when(i == pairs - 1)
                def _():
                    tick(4 + 3 * k)

                @pl.when(i == 2 * pairs - 1)
                def _():
                    tick(5 + 3 * k)

        attention_forward(pairs, mixed, bias, att, lse, k, hook)
        pltpu.make_async_copy(att, att_h.at[k], osem.at[3]).start()
        if k == 0:
            x_out.wait()

        def project_out(r, carry):
            sl = pl.ds(pl.multiple_of(r * PAIR, 16), PAIR)
            extra = vec[4:5, :] if k == 0 else 0.0
            acc[sl, :] += dot(att[sl, :], w[s, :, 3 * QW : CW], NT) + extra
            return carry

        lax.fori_loop(0, pairs, project_out, 0)
    m_out = pltpu.make_async_copy(acc, mid_h, osem.at[0])
    m_out.start()

    def second(r, carry):
        sl = pl.ds(pl.multiple_of(r * RB, 16), RB)
        xhat, _ = norm_parts(acc[sl, :])
        n2[sl, :] = (xhat * vec[5:6, :] + vec[6:7, :]).astype(bf)
        return carry

    lax.fori_loop(0, blocks, second, 0)
    n2_out = pltpu.make_async_copy(n2, n2_h, osem.at[4])
    n2_out.start()
    pltpu.make_async_copy(mixed, mixed_h.at[QUADS - 1], osem.at[2]).wait()
    pltpu.make_async_copy(att, att_h.at[QUADS - 1], osem.at[3]).wait()
    n_out.wait()
    m_out.wait()
    n2_out.wait()
    if comm:
        for k in range(QUADS, gather.chunks):
            gather.ready(k)
        for k in range(gather.chunks):
            gather.finish(k)


def f1(rows, comm, chunks, *args):
    A, V = any_spec(), vmem_spec()
    out_shape = (sds((rows, D), f32), sds((rows, D), bf), sds((QUADS, rows, 3 * QW), bf), sds((QUADS, rows, QW), bf),
                 sds((rows, 128), f32), sds((rows, D), f32), sds((rows, D), bf), sds((8, D), f32), sds((8, FC), f32))
    out_specs = (A, A, A, A, V, A, A, V, V)
    scratch = [
        pltpu.VMEM((rows, D), bf), pltpu.VMEM((rows, D), f32), pltpu.VMEM((rows, D), bf), pltpu.VMEM((2, D, CW), bf),
        pltpu.VMEM((rows, 3 * QW), bf), pltpu.VMEM((rows, QW), bf), pltpu.VMEM((rows // PAIR * 4, QMAX, KEYS), f32),
        pltpu.VMEM((rows, D), bf),
        pltpu.SemaphoreType.DMA((2,)), pltpu.SemaphoreType.DMA((2,)), pltpu.SemaphoreType.DMA((5,)),
    ]
    in_specs = [A, V, V, V, V, V, V, V]
    if comm:
        in_specs += [V, A]
        out_shape += (sds((chunks, D, CW), bf),)
        out_specs += (A,)
        scratch += [pltpu.VMEM((8, 16, 128), bf), pltpu.SemaphoreType.DMA((4,)), pltpu.SemaphoreType.DMA((chunks,)),
                    pltpu.SemaphoreType.DMA((chunks, 6))]
    else:
        in_specs += [V, V, A]
    return pl.pallas_call(
        functools.partial(f1_kernel, rows, comm), out_shape=out_shape, in_specs=in_specs, out_specs=out_specs,
        scratch_shapes=scratch, compiler_params=kernel_params(comm, 0), name="attention_forward",
    )(*args)


class Reduce:
    SLOTS = 3
    STEPS = ((12, "done"), (10, "share"), (9, "total"), (7, "planes"), (4, "relay"), (1, "cross"), (0, "pair"))

    def __init__(self, at, count, gp, r1, rx, ry, rz, fin, out, send, recv, osem, sizes):
        self.at, self.count, self.gp, self.r1, self.rx, self.ry, self.rz = at, count, gp, r1, rx, ry, rz
        self.fin, self.out, self.send, self.recv, self.osem, self.sizes = fin, out, send, recv, osem, sizes

    @classmethod
    def scratch(cls, count):
        s = cls.SLOTS
        return [pltpu.VMEM((s, 4, 256, CW), bf), pltpu.VMEM((s, 4, 128, CW), bf), pltpu.VMEM((s, 3, 4, 16, CW), bf),
                pltpu.VMEM((s, 3, 4, 16, CW), bf), pltpu.VMEM((s, 3, 32, CW), bf), pltpu.VMEM((count, 32, CW), bf),
                pltpu.SemaphoreType.DMA((count, 2)), pltpu.SemaphoreType.DMA((count, 6)), pltpu.SemaphoreType.DMA((count,))]

    def slot(self, t):
        return lax.rem(t, self.SLOTS)

    def rows(self, q, first, count):
        return pl.ds(pl.multiple_of(self.at.c * 128 + q * 32 + first, 16), count)

    def push(self, t, src, dst, stage, dev, group=0):
        remote(src, dst, self.send.at[t, group], self.recv.at[t, stage], dev).start()

    def landed(self, t, stage, rows):
        part = self.sizes.at[0, pl.ds(0, rows)]
        remote(part, part, self.send.at[t, 0], self.recv.at[t, stage], self.at.x_dev).wait_recv()

    def left(self, t, group, rows):
        part = self.sizes.at[0, pl.ds(0, rows)]
        remote(part, part, self.send.at[t, group], self.recv.at[t, 0], self.at.x_dev).wait_send()

    def add(self, t, q, first, *parts):
        s, sl = self.slot(t), self.rows(q, first, 16)
        total = self.gp[s, :, sl, :].astype(f32)
        for p in parts:
            total = total + p.astype(f32)
        self.gp[s, :, sl, :] = total.astype(bf)

    def pair(self, t):
        s = self.slot(t)
        other = pl.ds(pl.multiple_of((1 - self.at.c) * 128, 128), 128)
        self.push(t, self.gp.at[s, :, other], self.r1.at[s], 0, self.at.sib_dev)

    def cross(self, t):
        at, s = self.at, self.slot(t)
        self.landed(t, 0, 512)
        own = pl.ds(pl.multiple_of(at.c * 128, 128), 128)

        def plane(zz, carry):
            self.gp[s, zz, own, :] = (self.gp[s, zz, own, :].astype(f32) + self.r1[s, zz].astype(f32)).astype(bf)
            return carry

        lax.fori_loop(0, 4, plane, 0)
        gp = self.gp
        self.push(t, gp.at[s, :, self.rows(at.dd, 0, 16)], self.rx.at[s, 0], 1, at.x_dev)
        self.push(t, gp.at[s, :, self.rows(at.dd, 16, 16)], self.ry.at[s, 0], 1, at.y_dev)
        self.push(t, gp.at[s, :, self.rows(at.dx, 0, 16)], self.rx.at[s, 1], 2, at.x_dev)
        self.push(t, gp.at[s, :, self.rows(at.dy, 16, 16)], self.ry.at[s, 1], 2, at.y_dev)

    def relay(self, t):
        at, s = self.at, self.slot(t)
        self.landed(t, 1, 128)
        self.add(t, at.dy, 0, self.rx[s, 0])
        self.add(t, at.dx, 16, self.ry[s, 0])
        self.push(t, self.gp.at[s, :, self.rows(at.dy, 0, 16)], self.ry.at[s, 2], 2, at.y_dev)
        self.push(t, self.gp.at[s, :, self.rows(at.dx, 16, 16)], self.rx.at[s, 2], 2, at.x_dev)

    def planes(self, t):
        at, s = self.at, self.slot(t)
        self.landed(t, 2, 256)
        self.add(t, at.d, 0, self.rx[s, 1], self.ry[s, 2])
        self.add(t, at.d, 16, self.ry[s, 1], self.rx[s, 2])
        for n, (zz, dev) in enumerate(zip(at.zs, at.z_devs)):
            self.push(t, self.gp.at[s, zz, self.rows(at.d, 0, 32)], self.rz.at[s, n], 3, dev)

    def quarter(self, t, q, first=0, count=32):
        return self.out.at[t, pl.ds(pl.multiple_of(q * 32 + first, 16), count)]

    def total(self, t):
        at, s = self.at, self.slot(t)
        self.landed(t, 3, 96)
        total = self.gp[s, at.z, self.rows(at.d, 0, 32), :].astype(f32)
        for n in range(3):
            total = total + self.rz[s, n].astype(f32)
        self.fin[t] = total.astype(bf)
        pltpu.make_async_copy(self.fin.at[t], self.quarter(t, at.d), self.osem.at[t]).start()
        self.push(t, self.fin.at[t], self.quarter(t, at.d), 4, at.x_dev, 1)
        self.push(t, self.fin.at[t], self.quarter(t, at.d), 4, at.y_dev, 1)

    def share(self, t):
        at = self.at
        self.landed(t, 4, 64)
        self.push(t, self.quarter(t, at.dx, 0, 16), self.quarter(t, at.dx, 0, 16), 5, at.y_dev, 1)
        self.push(t, self.quarter(t, at.dy, 16, 16), self.quarter(t, at.dy, 16, 16), 5, at.x_dev, 1)

    def done(self, t):
        self.landed(t, 5, 32)
        self.left(t, 1, 96)
        pltpu.make_async_copy(self.fin.at[t], self.quarter(t, self.at.d), self.osem.at[t]).wait()

    def release(self, t):
        self.left(t, 0, 992)

    def tick(self, j, i):
        for offset, name in self.STEPS:
            if offset % 4 == i:
                t = j - offset // 4
                if isinstance(t, int):
                    if 0 <= t < self.count:
                        getattr(self, name)(t)
                else:
                    pl.when((t >= 0) & (t < self.count))(functools.partial(getattr(self, name), t))

    def drain(self, j, i, last):
        for k in range(4 * j + i, 4 * (last + 3) + 1):
            self.tick(k // 4, k % 4)


class Keep:
    SLOTS = 3

    def __init__(self, count, gp, out, sem):
        self.count, self.gp, self.out, self.sem = count, gp, out, sem

    @classmethod
    def scratch(cls, count):
        return [pltpu.VMEM((cls.SLOTS, 4, 256, CW), bf), pltpu.SemaphoreType.DMA((count,))]

    def slot(self, t):
        return lax.rem(t, self.SLOTS)

    def copy(self, t):
        return pltpu.make_async_copy(self.gp.at[self.slot(t)], self.out.at[t], self.sem.at[t])

    def tick(self, j, i):
        if i == 0:
            pl.when((j >= 0) & (j < self.count))(lambda: self.copy(j).start())

    def release(self, t):
        self.copy(t).wait()


def reducer(comm, count, out, sizes, scratch):
    if not comm:
        return Keep(count, scratch[0], out, scratch[1])
    at = Place()
    at.barrier()
    return Reduce(at, count, *scratch[:6], out, *scratch[6:], sizes)


def put_chunk(red, j, m, left, right):
    s, n = red.slot(j), left.shape[1]
    for i in range(2):
        red.gp[s, 2 * m + i, :, 0:n] = left[256 * i : 256 * (i + 1)].astype(bf)
        red.gp[s, 2 * m + i, :, n:CW] = right[256 * i : 256 * (i + 1)].astype(bf)


def f2_kernel(rows, comm, n2_h, g_h, mid_h, w_h, b_up, b_down, g2,
              out_h, gm_h, gb_h, gw_h, db_up, db_down, dg2, db2,
              n2, g, n2t, gt, w, act, dhid, acc_o, acc_d, mid, ob, gb, lsem, wsem, osem, msem, *scratch):
    KP = n2t.shape[1]
    NR = rows // PAIR
    first = QUADS
    chunks = w_h.shape[0] - QUADS

    def wcopy(j, s):
        return pltpu.make_async_copy(w_h.at[first + j], w.at[s], wsem.at[s])

    c1 = pltpu.make_async_copy(n2_h, n2, lsem.at[0])
    c1.start()
    c2 = pltpu.make_async_copy(g_h, g, lsem.at[1])
    c2.start()
    wcopy(0, 0).start()
    red = reducer(comm, chunks, gw_h, w_h, scratch)
    n2t[:, rows:KP] = jnp.zeros((D, KP - rows), bf)
    gt[:, rows:KP] = jnp.zeros((D, KP - rows), bf)
    act[rows:KP, :] = jnp.zeros((KP - rows, FC), bf)
    dhid[rows:KP, :] = jnp.zeros((KP - rows, FC), bf)
    acc_o[...] = jnp.zeros_like(acc_o)
    acc_d[...] = jnp.zeros_like(acc_d)
    c1.wait()
    c2.wait()
    transpose_rows(n2, n2t, rows)
    transpose_rows(g, gt, rows)

    def chunk(j, carry):
        s = lax.rem(j, 2)
        wcopy(j, s).wait()

        @pl.when(j + 1 < chunks)
        def _():
            wcopy(j + 1, 1 - s).start()

        def block(r, inner):
            sl = pl.ds(pl.multiple_of(r * PAIR, 16), PAIR)
            h = dot(n2[sl, :], w[s, :, 0:FC]) + b_up[pl.ds(j, 1), :]
            da = dot(g[sl, :], w[s, :, FC:CW])
            phi = 0.5 * (1.0 + lax.erf(h * 0.7071067811865476))
            slope = phi + h * (jnp.exp(-0.5 * h * h) * 0.3989422804014327)
            a = (h * phi).astype(bf)
            dh = (da * slope).astype(bf)
            act[sl, :] = a
            dhid[sl, :] = dh
            acc_o[sl, :] += dot(a, w[s, :, FC:CW], NT)
            acc_d[sl, :] += dot(dh, w[s, :, 0:FC], NT)
            return inner

        red.tick(j - 1, 0)
        for r in range(NR):
            block(r, 0)
            red.tick(j - 1, r + 1)
        db_up[pl.ds(j, 1), :] = dot(jnp.ones((8, KP), bf), dhid[...])[0:1]

        @pl.when(j >= red.SLOTS)
        def _():
            red.release(j - red.SLOTS)

        def grads(m, inner):
            sl = pl.ds(pl.multiple_of(m * 512, 512), 512)
            put_chunk(red, j, m, dot(n2t[sl, :], dhid[...]), dot(gt[sl, :], act[...]))

            @pl.when(m == 0)
            def _():
                red.tick(j - 1, 3)

            return inner

        lax.fori_loop(0, D // 512, grads, 0)
        return carry

    lax.fori_loop(0, chunks, chunk, 0)
    RB = PAIR // 7
    blocks = rows // RB

    def mcopy(r, s):
        return pltpu.make_async_copy(mid_h.at[pl.ds(pl.multiple_of(r * RB, 16), RB)], mid.at[s], msem.at[s])

    mcopy(0, 0).start()
    dg2[...] = jnp.zeros_like(dg2)
    db2[...] = jnp.zeros_like(db2)
    db_down[...] = jnp.zeros_like(db_down)

    def last(r, carry):
        s = lax.rem(r, 2)
        sl = pl.ds(pl.multiple_of(r * RB, 16), RB)
        mcopy(r, s).wait()

        @pl.when(r + 1 < blocks)
        def _():
            mcopy(r + 1, 1 - s).start()

        middle = mid[s]
        ob[sl, :] = (middle + acc_o[sl, :] + b_down[...]).astype(bf)
        xhat, inv = norm_parts(middle)
        dn = acc_d[sl, :]
        cot = g[sl, :].astype(f32)
        e = dn * g2[...]
        gm = cot + (e - jnp.mean(e, axis=-1, keepdims=True) - xhat * jnp.mean(e * xhat, axis=-1, keepdims=True)) * inv
        acc_d[sl, :] = gm
        gb[sl, :] = gm.astype(bf)
        dg2[...] += jnp.sum(dn * xhat, axis=0, keepdims=True)
        db2[...] += jnp.sum(dn, axis=0, keepdims=True)
        db_down[...] += jnp.sum(cot, axis=0, keepdims=True)
        end_tick(red, chunks - 1, r)
        return carry

    lax.fori_loop(0, blocks, last, 0)
    outs = [pltpu.make_async_copy(acc_d, gm_h, osem.at[1]), pltpu.make_async_copy(ob, out_h, osem.at[2]),
            pltpu.make_async_copy(gb, gb_h, osem.at[3])]
    for o in outs:
        o.start()
    finish(red, comm, blocks)
    for o in outs:
        o.wait()


def end_tick(red, last, r):
    for i in range(4):
        pl.when(lax.rem(r, 4) == i)(functools.partial(red.tick, last + lax.div(r, 4), i))


def finish(red, comm, done):
    last = red.count - 1
    if comm:
        red.drain(last + done // 4, done % 4, last)
    for t in range(max(0, red.count - red.SLOTS), red.count):
        red.release(t)


def f2(rows, comm, n2, g, mid, w, b_up, b_down, g2):
    A, V = any_spec(), vmem_spec()
    KP = -(-rows // 256) * 256
    chunks = w.shape[0] - QUADS
    RB = PAIR // 7
    return pl.pallas_call(
        functools.partial(f2_kernel, rows, comm),
        out_shape=(sds((rows, D), bf), sds((rows, D), f32), sds((rows, D), bf), grad_shape(comm, chunks), sds((chunks, FC), f32),
                   sds((1, D), f32), sds((1, D), f32), sds((1, D), f32)),
        in_specs=[A, A, A, A, V, V, V],
        out_specs=(A, A, A, A, V, V, V, V),
        scratch_shapes=[
            pltpu.VMEM((rows, D), bf), pltpu.VMEM((rows, D), bf), pltpu.VMEM((D, KP), bf), pltpu.VMEM((D, KP), bf),
            pltpu.VMEM((2, D, CW), bf), pltpu.VMEM((KP, FC), bf), pltpu.VMEM((KP, FC), bf),
            pltpu.VMEM((rows, D), f32), pltpu.VMEM((rows, D), f32),
            pltpu.VMEM((2, RB, D), f32), pltpu.VMEM((rows, D), bf), pltpu.VMEM((rows, D), bf),
            pltpu.SemaphoreType.DMA((2,)), pltpu.SemaphoreType.DMA((2,)), pltpu.SemaphoreType.DMA((4,)),
            pltpu.SemaphoreType.DMA((2,)),
        ] + (Reduce if comm else Keep).scratch(chunks),
        compiler_params=kernel_params(comm, 1),
        name="feed_forward",
    )(n2, g, mid, w, b_up, b_down, g2)


def attention_backward(pairs, mixed, datt, bias, lse, dmixed, dq, dk, dv, quad, hook):
    def one(i, carry):
        p, hp = i // 2, lax.rem(i, 2)
        base = pl.multiple_of(p * PAIR, 16)
        lane0 = pl.multiple_of(hp * 128, 128)
        dq[...] = jnp.zeros_like(dq)
        dk[...] = jnp.zeros_like(dk)
        dv[...] = jnp.zeros_like(dv)
        for w, (start, halves) in enumerate(WINDOWS):
            for n, (q0, qn, k0) in enumerate(halves):
                at = start + q0
                row = pl.multiple_of(base + at, 16)
                kat = start + k0
                keys = pl.ds(pl.multiple_of(base + kat, 16), KEYS)
                q2 = mixed[pl.ds(row, qn), pl.ds(lane0, 128)] * jnp.asarray(SCALE, bf)
                k2 = mixed[keys, pl.ds(pl.multiple_of(lane0 + QW, 128), 128)]
                v2 = mixed[keys, pl.ds(pl.multiple_of(lane0 + 2 * QW, 128), 128)]
                do2 = datt[pl.ds(row, qn), pl.ds(lane0, 128)]
                lse_rows = lse[pl.ds(row, qn), :]
                lane = lax.broadcasted_iota(jnp.int32, (qn, 128), 1)
                idx = p * 4 + w * 2 + n
                dqs = None
                for h in range(2):
                    mask = half_mask(qn, h == 1)
                    kmask = half_mask(KEYS, h == 1)
                    qm = jnp.where(mask, q2, jnp.zeros_like(q2))
                    dom = jnp.where(mask, do2, jnp.zeros_like(do2))
                    head = quad * 4 + hp * 2 + h
                    row_lse = jnp.sum(jnp.where(lane == head, lse_rows, 0.0), axis=-1, keepdims=True)
                    s = dot(qm, k2, NT) + bias[idx, 0:qn, :]
                    probs = jnp.exp(s - row_lse)
                    dp = dot(dom, v2, NT)
                    inner = jnp.sum(probs * dp, axis=-1, keepdims=True)
                    ds = (probs * (dp - inner)).astype(bf)
                    dv[kat : kat + KEYS, :] += dot(probs.astype(bf), dom, TN)
                    dk[kat : kat + KEYS, :] += dot(ds, qm, TN)
                    part = dot(ds, k2)
                    dqs = part if h == 0 else jnp.where(mask, part, dqs)
                dq[at : at + qn, :] += dqs
        rows = pl.ds(base, PAIR)
        dmixed[rows, pl.ds(lane0, 128)] = (dq[...] * SCALE).astype(bf)
        dmixed[rows, pl.ds(pl.multiple_of(lane0 + QW, 128), 128)] = dk[...].astype(bf)
        dmixed[rows, pl.ds(pl.multiple_of(lane0 + 2 * QW, 128), 128)] = dv[...].astype(bf)
        hook(i)
        return carry

    lax.fori_loop(0, pairs * 2, one, 0)


def f3_kernel(rows, comm, gb_h, normed_h, w_h, mixed_h, att_h, lse, x_h, gm_h, g1, lab_col, lab_row, q_units, k_units,
              gt_h, gw_h, db_qkv, db_out, dg1, db1,
              gb, normed, gbt, normedt, w, mixed, att, datt, dmixed, bias, acc, dq, dk, dv, xb, gmb, ob,
              lsem, wsem, isem, xsem, gsem, tsem, *scratch):
    KP = gbt.shape[1]
    pairs = rows // PAIR

    def inputs(k, s):
        return (pltpu.make_async_copy(w_h.at[k], w.at[s], wsem.at[s]),
                pltpu.make_async_copy(mixed_h.at[k], mixed.at[s], isem.at[s, 0]),
                pltpu.make_async_copy(att_h.at[k], att.at[s, pl.ds(0, rows)], isem.at[s, 1]))

    c1 = pltpu.make_async_copy(gb_h, gb, lsem.at[0])
    c1.start()
    c2 = pltpu.make_async_copy(normed_h, normed, lsem.at[1])
    c2.start()
    for c in inputs(0, 0):
        c.start()
    red = reducer(comm, QUADS, gw_h, w_h, scratch)
    gbt[:, rows:KP] = jnp.zeros((D, KP - rows), bf)
    normedt[:, rows:KP] = jnp.zeros((D, KP - rows), bf)
    dmixed[rows:KP, :] = jnp.zeros((KP - rows, 3 * QW), bf)
    for s in range(2):
        att[s, rows:KP, :] = jnp.zeros((KP - rows, QW), bf)
    fill_bias(bias, lab_col, lab_row, q_units, k_units)
    c1.wait()
    c2.wait()
    transpose_rows(gb, gbt, rows)
    transpose_rows(normed, normedt, rows)
    db_out[...] = dot(jnp.ones((8, rows), bf), gb[...])[0:1]

    def quad(k, carry):
        s = lax.rem(k, 2)
        for c in inputs(k, s):
            c.wait()

        @pl.when(k + 1 < QUADS)
        def _():
            for c in inputs(k + 1, 1 - s):
                c.start()

        def back(r, inner):
            sl = pl.ds(pl.multiple_of(r * PAIR, 16), PAIR)
            datt[sl, :] = dot(gb[sl, :], w[s, :, 3 * QW : CW]).astype(bf)
            return inner

        red.tick(k - 1, 0)
        lax.fori_loop(0, pairs, back, 0)

        def hook(i):
            pl.when(i == pairs - 1)(functools.partial(red.tick, k - 1, 1))
            pl.when(i == 2 * pairs - 1)(functools.partial(red.tick, k - 1, 2))

        attention_backward(pairs, mixed.at[s], datt, bias, lse, dmixed, dq, dk, dv, k, hook)
        db_qkv[pl.ds(k, 1), :] = dot(jnp.ones((8, KP), bf), dmixed[...])[0:1]

        @pl.when(k >= red.SLOTS)
        def _():
            red.release(k - red.SLOTS)

        def grads(m, inner):
            sl = pl.ds(pl.multiple_of(m * 512, 512), 512)
            put_chunk(red, k, m, dot(normedt[sl, :], dmixed[...]), dot(gbt[sl, :], att[s]))

            @pl.when(m == 0)
            def _():
                red.tick(k - 1, 3)

            return inner

        lax.fori_loop(0, D // 512, grads, 0)

        def back_in(r, inner):
            sl = pl.ds(pl.multiple_of(r * PAIR, 16), PAIR)
            new = dot(dmixed[sl, :], w[s, :, 0 : 3 * QW], NT)
            acc[sl, :] = jnp.where(k == 0, new, acc[sl, :] + new)
            return inner

        lax.fori_loop(0, pairs, back_in, 0)
        return carry

    lax.fori_loop(0, QUADS, quad, 0)
    RB = PAIR // 7
    blocks = rows // RB

    def part(r):
        return pl.ds(pl.multiple_of(r * RB, 16), RB)

    def rcopies(r, s):
        return (pltpu.make_async_copy(x_h.at[part(r)], xb.at[s], xsem.at[s]),
                pltpu.make_async_copy(gm_h.at[part(r)], gmb.at[s], gsem.at[s]))

    for c in rcopies(0, 0):
        c.start()
    dg1[...] = jnp.zeros_like(dg1)
    db1[...] = jnp.zeros_like(db1)

    def last(r, carry):
        s = lax.rem(r, 2)
        for c in rcopies(r, s):
            c.wait()

        @pl.when(r + 1 < blocks)
        def _():
            for c in rcopies(r + 1, 1 - s):
                c.start()

        @pl.when(r >= 2)
        def _():
            pltpu.make_async_copy(ob.at[s], gt_h.at[part(r - 2)], tsem.at[s]).wait()

        xhat, inv = norm_parts(xb[s])
        dn = acc[part(r), :]
        e = dn * g1[...]
        ob[s] = gmb[s] + (e - jnp.mean(e, axis=-1, keepdims=True) - xhat * jnp.mean(e * xhat, axis=-1, keepdims=True)) * inv
        pltpu.make_async_copy(ob.at[s], gt_h.at[part(r)], tsem.at[s]).start()
        dg1[...] += jnp.sum(dn * xhat, axis=0, keepdims=True)
        db1[...] += jnp.sum(dn, axis=0, keepdims=True)
        end_tick(red, QUADS - 1, r)
        return carry

    lax.fori_loop(0, blocks, last, 0)
    for r in (blocks - 2, blocks - 1):
        pltpu.make_async_copy(ob.at[r % 2], gt_h.at[part(r)], tsem.at[r % 2]).wait()
    finish(red, comm, blocks)


def f3(rows, comm, gb, normed, w, mixed, att, lse, x, gm, g1, lab_col, lab_row, q_units, k_units):
    A, V = any_spec(), vmem_spec()
    KP = -(-rows // 256) * 256
    RB = PAIR // 7
    return pl.pallas_call(
        functools.partial(f3_kernel, rows, comm),
        out_shape=(sds((rows, D), f32), grad_shape(comm, QUADS), sds((QUADS, 3 * QW), f32), sds((1, D), f32), sds((1, D), f32),
                   sds((1, D), f32)),
        in_specs=[A, A, A, A, A, V, A, A, V, V, V, V, V],
        out_specs=(A, A, V, V, V, V),
        scratch_shapes=[
            pltpu.VMEM((rows, D), bf), pltpu.VMEM((rows, D), bf), pltpu.VMEM((D, KP), bf), pltpu.VMEM((D, KP), bf),
            pltpu.VMEM((2, D, CW), bf), pltpu.VMEM((2, rows, 3 * QW), bf), pltpu.VMEM((2, KP, QW), bf), pltpu.VMEM((rows, QW), bf),
            pltpu.VMEM((KP, 3 * QW), bf), pltpu.VMEM((rows // PAIR * 4, QMAX, KEYS), f32), pltpu.VMEM((rows, D), f32),
            pltpu.VMEM((PAIR, 128), f32), pltpu.VMEM((PAIR, 128), f32), pltpu.VMEM((PAIR, 128), f32),
            pltpu.VMEM((2, RB, D), f32), pltpu.VMEM((2, RB, D), f32), pltpu.VMEM((2, RB, D), f32),
            pltpu.SemaphoreType.DMA((2,)), pltpu.SemaphoreType.DMA((2,)), pltpu.SemaphoreType.DMA((2, 2)),
            pltpu.SemaphoreType.DMA((2,)), pltpu.SemaphoreType.DMA((2,)), pltpu.SemaphoreType.DMA((2,)),
        ] + (Reduce if comm else Keep).scratch(QUADS),
        compiler_params=kernel_params(comm, 2),
        name="attention_backward",
    )(gb, normed, w, mixed, att, lse, x, gm, g1, lab_col, lab_row, q_units, k_units)


def unit_labels(band_code):
    units = band_code.reshape(-1, UNITS_MB)
    labels = jnp.cumsum((units <= 1).astype(jnp.int32), axis=1) + 16 * jnp.arange(units.shape[0], dtype=jnp.int32)[:, None]
    return labels.reshape(-1).astype(f32)


def window_units(rows):
    units = rows // UNIT
    queries, keys = [], []
    for p in range(rows // PAIR):
        for w, (start, halves) in enumerate(WINDOWS):
            for q0, qn, k0 in halves:
                q = p * PAIR + start + q0 + np.arange(QMAX)
                inside = (q >= p * PAIR + w * BUF) & (q < p * PAIR + (w + 1) * BUF)
                queries.append((q[:, None] // UNIT == np.arange(units)) & inside[:, None])
                k = p * PAIR + start + k0 + np.arange(KEYS)
                keys.append(np.arange(units)[:, None] == k // UNIT)
    return jnp.asarray(np.stack(queries), bf), jnp.asarray(np.stack(keys), bf)


def place_table(gsd_code):
    ratio = jnp.exp2((gsd_code.astype(f32) - 3.0) * 0.5)
    quarter = D // 4
    freq = jnp.exp2(jnp.arange(quarter, dtype=f32) * (-math.log2(10000.0) / quarter))
    a = jnp.arange(GRID, dtype=f32)
    angle = (a[None, :] * ratio[:, None]).reshape(-1)[:, None] * freq[None, :]
    tab = jnp.concatenate([jnp.sin(angle), jnp.cos(angle)], axis=1)
    n = tab.shape[0]
    pad = -(-n // 256) * 256
    tab = jnp.pad(tab, ((0, pad - n), (0, 0)))
    hi = lax.reduce_precision(tab, 8, 7)
    rest = tab - hi
    mid = lax.reduce_precision(rest, 8, 7)
    return jnp.stack([hi, mid, rest - mid]).astype(bf)


def one_hots(rows, width):
    r = np.arange(rows)
    col = np.arange(width)
    ohy = (r[:, None] // GRID == col[None, :])
    ohx = ((r // UNIT * GRID + r % GRID)[:, None] == col[None, :])
    return jnp.asarray(ohy, bf), jnp.asarray(ohx, bf)


def pack_weights(qkv, out, up, down):
    n = qkv.shape[0]
    att = jnp.concatenate([qkv.reshape(n, 3, QUADS, QW).transpose(2, 0, 1, 3).reshape(QUADS, n, 3 * QW),
                           out.T.reshape(n, QUADS, QW).transpose(1, 0, 2)], axis=2)
    ff = up.shape[1] // FC
    feed = jnp.concatenate([up.reshape(n, ff, FC).transpose(1, 0, 2), down.T.reshape(n, ff, FC).transpose(1, 0, 2)], axis=2)
    return jnp.concatenate([att, feed], axis=0)


def local(dp, fsdp, tokens, band_code, gsd_code, norm1_gain, norm1_bias, qkv_weight, bias_q, bias_v, out_weight, bias_out,
          norm2_gain, norm2_bias, up_weight, bias_up, down_weight, bias_down, grad_out):
    rows = tokens.shape[0]
    comm = dp == 4 and fsdp == 8
    shard = pack_weights(qkv_weight, out_weight, up_weight, down_weight)
    n = shard.shape[1]
    chunks = shard.shape[0]
    vectors = (norm1_gain, norm1_bias, bias_q, bias_v, bias_out, norm2_gain, norm2_bias, bias_down)
    labels = unit_labels(band_code)
    tab = place_table(gsd_code)
    ohy, ohx = one_hots(rows, tab.shape[1])
    q_units, k_units = window_units(rows)
    lab = (labels.reshape(-1, 1), labels.reshape(1, -1), q_units, k_units)
    if comm:
        small = jnp.concatenate([jnp.stack(vectors), bias_up.reshape(4, 128), jnp.zeros((4, 128), bf)])
        x, normed, mixed, att, lse, mid, n2, vec, b_up, w = f1(rows, True, chunks, tokens, ohy, ohx, tab, *lab, small, shard)
    else:
        gathered = lax.all_gather(jnp.stack(vectors), "fsdp", axis=1, tiled=True).astype(f32)
        up_bias = lax.all_gather(bias_up, "fsdp", axis=0, tiled=True).astype(f32).reshape(-1, FC)
        w = lax.all_gather(shard, "fsdp", axis=1, tiled=True)
        x, normed, mixed, att, lse, mid, n2, vec, b_up = f1(rows, False, chunks, tokens, ohy, ohx, tab, *lab, gathered, up_bias, w)
    out, gm, gb, gw_ff, db_up, db_down, dg2, db2 = f2(rows, comm, n2, grad_out, mid, w, b_up, vec[7:8], vec[5:6])
    grad_tokens, gw_att, db_qkv, db_out, dg1, db1 = f3(rows, comm, gb, normed, w, mixed, att, lse, x, gm, vec[0:1], *lab)
    small_grads = jnp.concatenate([dg1, db1, db_qkv[:, 0:QW].reshape(1, D), db_qkv[:, 2 * QW :].reshape(1, D), db_out, dg2, db2,
                                   db_down], axis=0)
    small_grads = jnp.concatenate([small_grads.reshape(8, fsdp, n).transpose(1, 0, 2).reshape(fsdp, 8 * n),
                                   db_up.reshape(fsdp, 4 * n)], axis=1)
    gw = jnp.concatenate([gw_att, gw_ff], axis=0)
    if not comm:
        gw = lax.psum(lax.psum_scatter(gw.reshape(chunks, D, CW), "fsdp", scatter_dimension=1, tiled=True), "dp")
    gw = gw.astype(f32)
    sg = lax.psum(lax.psum_scatter(small_grads, "fsdp", scatter_dimension=0, tiled=True), "dp").reshape(12, n)
    g_att, g_ff = gw[:QUADS], gw[QUADS:]
    g_qkv = g_att[:, :, : 3 * QW].reshape(QUADS, n, 3, QW).transpose(1, 2, 0, 3).reshape(n, 3 * D)
    g_out = g_att[:, :, 3 * QW :].transpose(0, 2, 1).reshape(D, n)
    g_up = g_ff[:, :, :FC].transpose(1, 0, 2).reshape(n, -1)
    g_down = g_ff[:, :, FC:].transpose(0, 2, 1).reshape(-1, n)
    return (out, grad_tokens, sg[0], sg[1], g_qkv, sg[2], sg[3], g_out, sg[4], sg[5], sg[6], g_up, sg[8:12].reshape(4 * n), g_down, sg[7])


def solution(mesh):
    rows, vec, first, second = P(("dp", "fsdp"), None), P("fsdp"), P("fsdp", None), P(None, "fsdp")
    codes = P(("dp", "fsdp"))
    return jax.shard_map(
        functools.partial(local, mesh.shape["dp"], mesh.shape["fsdp"]),
        mesh=mesh,
        in_specs=(rows, codes, codes, vec, vec, first, vec, vec, second, vec, vec, vec, first, vec, second, vec, rows),
        out_specs=(rows, rows, vec, vec, first, vec, vec, second, vec, vec, vec, first, vec, second, vec),
        check_vma=False,
    )
```

```python
import functools
import math

import jax
import jax.numpy as jnp
import numpy as np
from jax import lax
from jax.experimental import pallas as pl
from jax.experimental.pallas import tpu as pltpu
from jax.sharding import PartitionSpec as P

bf = jnp.bfloat16
f32 = jnp.float32
NN = (((1,), (0,)), ((), ()))
NT = (((1,), (1,)), ((), ()))
TN = (((0,), (0,)), ((), ()))
D = 1024
HEADS = 16
HEAD_DIM = 64
GRID = 7
UNIT = GRID * GRID
UNITS_MB = 8
BUF = UNIT * UNITS_MB
PAIR = 2 * BUF
QUADS = 4
QW = 256
FC = 512
CW = 1024
EPS = 1e-6
SCALE = 0.125
NEG = -1e30
VMEM_LIMIT = 62 << 20
KEYS = 384
WINDOWS = ((0, ((0, 192, 0), (192, 208, 16))), (384, ((0, 192, 0), (192, 208, 16))))
SPAN = 400


def dot(a, b, dims=NN):
    return lax.dot_general(a, b, dims, preferred_element_type=f32)


def any_spec():
    return pl.BlockSpec(memory_space=pl.ANY)


def vmem_spec():
    return pl.BlockSpec(memory_space=pltpu.VMEM)


def sds(shape, kind):
    return jax.ShapeDtypeStruct(shape, kind)


def norm_parts(v):
    center = v - jnp.mean(v, axis=-1, keepdims=True)
    inv = lax.rsqrt(jnp.mean(center * center, axis=-1, keepdims=True) + EPS)
    return center * inv, inv


def low_lanes(rows):
    return lax.broadcasted_iota(jnp.int32, (rows, 128), 1) < 64


def split_terms(v):
    lane = lax.broadcasted_iota(jnp.int32, v.shape, 1) & 63
    hi = v.astype(bf).astype(f32)
    rest = v - hi
    mid = rest.astype(bf).astype(f32)
    return jnp.where(lane == 0, hi, jnp.where(lane == 1, mid, jnp.where(lane == 2, rest - mid, 0.0))), lane < 3


def attention_forward(pairs, mixed, q_feat, k_feat, attended, stats, hook):
    def one(i, carry):
        p, hp = i // 2, lax.rem(i, 2)
        base = pl.multiple_of(p * PAIR, 16)
        lane0 = pl.multiple_of(hp * 128, 128)
        tail = None
        for w, (start, halves) in enumerate(WINDOWS):
            span = pl.ds(pl.multiple_of(base + start, 16), SPAN)
            k2 = mixed[span, pl.ds(pl.multiple_of(lane0 + QW, 128), 128)]
            v2 = mixed[span, pl.ds(pl.multiple_of(lane0 + 2 * QW, 128), 128)]
            kf = k_feat[span, :]
            low = low_lanes(SPAN)
            keys = (jnp.where(low, k2, kf), jnp.where(low, kf, k2))
            ones = jnp.ones_like(v2)
            values = (jnp.where(low, v2, ones), jnp.where(low, ones, v2))
            for n, (q0, qn, k0) in enumerate(halves):
                row = pl.multiple_of(base + start + q0, 16)
                q2 = mixed[pl.ds(row, qn), pl.ds(lane0, 128)] * jnp.asarray(SCALE, bf)
                qf = q_feat[pl.ds(row, qn), :]
                low = low_lanes(qn)
                tops, outs = [], []
                for h in range(2):
                    s = dot(jnp.where(low, q2, qf) if h == 0 else jnp.where(low, qf, q2), keys[h][k0 : k0 + KEYS], NT)
                    m = jnp.max(s, axis=-1, keepdims=True)
                    outs.append(dot(jnp.exp(s - m).astype(bf), values[h][k0 : k0 + KEYS]))
                    tops.append(m)
                total = jnp.where(low, outs[1], outs[0])
                out = jnp.where(low, outs[0], outs[1]) / pltpu.roll(total, 64, 1)
                terms, at = split_terms(-(jnp.where(low, tops[1], tops[0]) + jnp.log(total)))
                stat = jnp.where(at, terms, qf.astype(f32))
                if w == 0 and n == 1:
                    tail = (out[qn - 16 :], stat[qn - 16 :])
                if w == 1 and n == 0:
                    first = lax.broadcasted_iota(jnp.int32, (16, 128), 0) < 8
                    out = jnp.concatenate([jnp.where(first, tail[0], out[0:16]), out[16:]], axis=0)
                    stat = jnp.concatenate([jnp.where(first, tail[1], stat[0:16]), stat[16:]], axis=0)
                attended[pl.ds(row, qn), pl.ds(lane0, 128)] = out.astype(bf)
                stats[pl.ds(row, qn), pl.ds(lane0, 128)] = stat.astype(bf)
        hook(i)
        return carry

    lax.fori_loop(0, pairs * 2, one, 0)


def attention_backward(pairs, mixed, att, stats, datt, k_feat, swap, dq, dk, dv, hook):
    def one(i, carry):
        p, hp = i // 2, lax.rem(i, 2)
        base = pl.multiple_of(p * PAIR, 16)
        lane0 = pl.multiple_of(hp * 128, 128)
        dq[...] = jnp.zeros_like(dq)
        dk[...] = jnp.zeros_like(dk)
        dv[...] = jnp.zeros_like(dv)
        for w, (start, halves) in enumerate(WINDOWS):
            span = pl.ds(pl.multiple_of(base + start, 16), SPAN)
            k2 = mixed[span, pl.ds(pl.multiple_of(lane0 + QW, 128), 128)]
            v2 = mixed[span, pl.ds(pl.multiple_of(lane0 + 2 * QW, 128), 128)]
            kf = k_feat[span, :]
            low = low_lanes(SPAN)
            zero = jnp.zeros_like(k2)
            terms = (lax.broadcasted_iota(jnp.int32, (SPAN, 128), 1) & 63) < 3
            vf = jnp.where(terms, jnp.ones_like(v2), zero)
            keys = (jnp.where(low, k2, kf), jnp.where(low, kf, k2))
            plain = (jnp.where(low, k2, zero), jnp.where(low, zero, k2))
            values = (jnp.where(low, v2, vf), jnp.where(low, vf, v2))
            for n, (q0, qn, k0) in enumerate(halves):
                at = start + q0
                row = pl.multiple_of(base + at, 16)
                rows = pl.ds(row, qn)
                lanes = pl.ds(lane0, 128)
                q2 = mixed[rows, lanes] * jnp.asarray(SCALE, bf)
                do2 = datt[rows, lanes]
                if w != n:
                    r = lax.broadcasted_iota(jnp.int32, (qn, 128), 0)
                    mine = r < qn - 8 if n == 1 else r >= 8
                    do2 = jnp.where(mine, do2, jnp.zeros_like(do2))
                qf = stats[rows, lanes]
                low = low_lanes(qn)
                zero = jnp.zeros_like(q2)
                prod = do2.astype(f32) * att[rows, lanes].astype(f32)
                hi = prod.astype(bf)
                inner = dot(hi, swap[...]) + dot((prod - hi.astype(f32)).astype(bf), swap[...])
                df = split_terms(-inner)[0].astype(bf)
                pieces = []
                for h in range(2):
                    pick = (lambda a, b: jnp.where(low, a, b)) if h == 0 else (lambda a, b: jnp.where(low, b, a))
                    kk = slice(k0, k0 + KEYS)
                    probs = jnp.exp(dot(pick(q2, qf), keys[h][kk], NT))
                    ds = (probs * dot(pick(do2, df), values[h][kk], NT)).astype(bf)
                    pieces.append((probs.astype(bf), ds, pick(do2, zero), pick(q2, zero), plain[h][kk]))
                (pa, sa, oa, qa, ka), (pb, sb, ob, qb, kb) = pieces
                kat = start + k0
                dv[kat : kat + KEYS, :] += dot(pa, oa, TN) + dot(pb, ob, TN)
                dk[kat : kat + KEYS, :] += dot(sa, qa, TN) + dot(sb, qb, TN)
                dq[at : at + qn, :] += dot(sa, ka) + dot(sb, kb)
        rows = pl.ds(base, PAIR)
        mixed[rows, pl.ds(lane0, 128)] = (dq[...] * SCALE).astype(bf)
        mixed[rows, pl.ds(pl.multiple_of(lane0 + QW, 128), 128)] = dk[...].astype(bf)
        mixed[rows, pl.ds(pl.multiple_of(lane0 + 2 * QW, 128), 128)] = dv[...].astype(bf)
        hook(i)
        return carry

    lax.fori_loop(0, pairs * 2, one, 0)


MESH = pl.DeviceIdType.MESH


class Place:
    def __init__(self):
        self.d = lax.axis_index("dp")
        self.f = lax.axis_index("fsdp")
        self.z = lax.div(self.f, 2)
        self.c = lax.rem(self.f, 2)
        self.dx = self.d + 1 - 2 * lax.rem(self.d, 2)
        self.dy = lax.rem(self.d + 2, 4)
        self.dd = 3 - self.d
        self.sib = self.f + 1 - 2 * self.c
        self.zs = [lax.rem(self.z + n, 4) for n in (1, 2, 3)]
        self.x_dev = (self.dx, self.f)
        self.y_dev = (self.dy, self.f)
        self.sib_dev = (self.d, self.sib)
        self.z_devs = [(self.d, 2 * zz + self.c) for zz in self.zs]

    def barrier(self):
        sem = pltpu.get_barrier_semaphore()
        for dev in [self.x_dev, self.y_dev, self.sib_dev] + self.z_devs:
            pl.semaphore_signal(sem, inc=1, device_id=dev, device_id_type=MESH)
        pl.semaphore_wait(sem, 6)


def remote(src, dst, send, recv, dev):
    return pltpu.make_async_remote_copy(src, dst, send, recv, device_id=dev, device_id_type=MESH)


class Gather:
    def __init__(self, at, shard, whole, send, recv, first=0):
        self.at, self.shard, self.whole, self.send, self.recv, self.first = at, shard, whole, send, recv, first
        self.chunks = whole.shape[0]

    def rows(self, zz, q, first, count):
        return pl.ds(pl.multiple_of((2 * zz + self.at.c) * 128 + 32 * q + first, 16), count)

    def push(self, k, rows, stage, dev, src=None):
        dst = self.whole.at[k, rows]
        remote(dst if src is None else src, dst, self.send.at[k], self.recv.at[k, stage], dev).start()

    def landed(self, k, stage, count):
        part = self.whole.at[k, pl.ds(0, count)]
        remote(part, part, self.send.at[k], self.recv.at[k, stage], self.at.x_dev).wait_recv()

    def begin(self, k):
        at = self.at
        quarter = self.shard.at[self.first + k, pl.ds(pl.multiple_of(32 * at.d, 16), 32)]
        for dev in at.z_devs:
            self.push(k, self.rows(at.z, at.d, 0, 32), 0, dev, quarter)
        self.push(k, self.rows(at.z, 0, 0, 128), 5, at.sib_dev, self.shard.at[self.first + k])

    def spread(self, k):
        at = self.at
        self.landed(k, 0, 96)
        for zz in at.zs:
            self.push(k, self.rows(zz, at.d, 0, 32), 1, at.x_dev)
            self.push(k, self.rows(zz, at.d, 0, 32), 2, at.y_dev)

    def diagonal(self, k):
        at = self.at
        self.landed(k, 1, 96)
        self.landed(k, 2, 96)
        for zz in at.zs:
            self.push(k, self.rows(zz, at.dx, 0, 16), 3, at.y_dev)
            self.push(k, self.rows(zz, at.dy, 16, 16), 4, at.x_dev)

    def pair(self, k):
        at = self.at
        self.landed(k, 3, 48)
        self.landed(k, 4, 48)
        for zz in at.zs:
            self.push(k, self.rows(zz, 0, 0, 128), 5, at.sib_dev)

    def ready(self, k):
        self.landed(k, 5, 512)

    def tick(self, t):
        if t + 3 < self.chunks:
            self.begin(t + 3)
        if 0 <= t < self.chunks:
            self.spread(t)
        if 0 <= t - 1 < self.chunks:
            self.diagonal(t - 1)
        if 0 <= t - 2 < self.chunks:
            self.pair(t - 2)

    def finish(self, k):
        part = self.whole.at[k, pl.ds(0, 896)]
        remote(part, part, self.send.at[k], self.recv.at[k, 0], self.at.x_dev).wait_send()


def spread_vectors(shards, vec, b_up):
    n = vec.shape[1] // 128
    for f in range(n):
        vec[:, 128 * f : 128 * (f + 1)] = shards[f, 0:8, :].astype(f32)
        for i in range(4):
            b_up[f : f + 1, 128 * i : 128 * (i + 1)] = shards[f, 8 + i : 9 + i, :].astype(f32)


def load_chunk(at, shard_h, whole_h, k, offset, dst, sem):
    for n in range(8):
        f = lax.rem(at.f + n, 8)
        rows = pl.ds(pl.multiple_of(f * 128, 128), 128)
        src = shard_h.at[offset + k] if n == 0 else whole_h.at[k, rows]
        pltpu.make_async_copy(src, dst.at[rows], sem).start()


class Reduce:
    SLOTS = 3
    STEPS = ((12, "done"), (10, "share"), (9, "total"), (7, "planes"), (4, "relay"), (1, "cross"), (0, "pair"))

    def __init__(self, at, count, gp, r1, rx, ry, rz, fin, out, send, recv, osem, sizes):
        self.at, self.count, self.gp, self.r1, self.rx, self.ry, self.rz = at, count, gp, r1, rx, ry, rz
        self.fin, self.out, self.send, self.recv, self.osem, self.sizes = fin, out, send, recv, osem, sizes

    @classmethod
    def scratch(cls, count):
        s = cls.SLOTS
        return [pltpu.VMEM((s, 4, 256, CW), bf), pltpu.VMEM((2, 4, 128, CW), bf), pltpu.VMEM((s, 3, 4, 16, CW), bf),
                pltpu.VMEM((s, 3, 4, 16, CW), bf), pltpu.VMEM((s, 3, 32, CW), bf), pltpu.VMEM((count, 32, CW), bf),
                pltpu.SemaphoreType.DMA((count, 2)), pltpu.SemaphoreType.DMA((count, 6)), pltpu.SemaphoreType.DMA((count,))]

    def slot(self, t):
        return lax.rem(t, self.SLOTS)

    def rows(self, q, first, count):
        return pl.ds(pl.multiple_of(self.at.c * 128 + q * 32 + first, 16), count)

    def push(self, t, src, dst, stage, dev, group=0):
        remote(src, dst, self.send.at[t, group], self.recv.at[t, stage], dev).start()

    def landed(self, t, stage, rows):
        part = self.sizes.at[0, pl.ds(0, rows)]
        remote(part, part, self.send.at[t, 0], self.recv.at[t, stage], self.at.x_dev).wait_recv()

    def left(self, t, group, rows):
        part = self.sizes.at[0, pl.ds(0, rows)]
        remote(part, part, self.send.at[t, group], self.recv.at[t, 0], self.at.x_dev).wait_send()

    def add(self, t, q, first, *parts):
        s, sl = self.slot(t), self.rows(q, first, 16)
        total = self.gp[s, :, sl, :].astype(f32)
        for p in parts:
            total = total + p.astype(f32)
        self.gp[s, :, sl, :] = total.astype(bf)

    def pair(self, t):
        s = self.slot(t)
        other = pl.ds(pl.multiple_of((1 - self.at.c) * 128, 128), 128)
        self.push(t, self.gp.at[s, :, other], self.r1.at[lax.rem(t, 2)], 0, self.at.sib_dev)

    def cross(self, t):
        at, s = self.at, self.slot(t)
        self.landed(t, 0, 512)
        own = pl.ds(pl.multiple_of(at.c * 128, 128), 128)

        def plane(zz, carry):
            self.gp[s, zz, own, :] = (self.gp[s, zz, own, :].astype(f32) + self.r1[lax.rem(t, 2), zz].astype(f32)).astype(bf)
            return carry

        lax.fori_loop(0, 4, plane, 0)
        gp = self.gp
        self.push(t, gp.at[s, :, self.rows(at.dd, 0, 16)], self.rx.at[s, 0], 1, at.x_dev)
        self.push(t, gp.at[s, :, self.rows(at.dd, 16, 16)], self.ry.at[s, 0], 1, at.y_dev)
        self.push(t, gp.at[s, :, self.rows(at.dx, 0, 16)], self.rx.at[s, 1], 2, at.x_dev)
        self.push(t, gp.at[s, :, self.rows(at.dy, 16, 16)], self.ry.at[s, 1], 2, at.y_dev)

    def relay(self, t):
        at, s = self.at, self.slot(t)
        self.landed(t, 1, 128)
        self.add(t, at.dy, 0, self.rx[s, 0])
        self.add(t, at.dx, 16, self.ry[s, 0])
        self.push(t, self.gp.at[s, :, self.rows(at.dy, 0, 16)], self.ry.at[s, 2], 2, at.y_dev)
        self.push(t, self.gp.at[s, :, self.rows(at.dx, 16, 16)], self.rx.at[s, 2], 2, at.x_dev)

    def planes(self, t):
        at, s = self.at, self.slot(t)
        self.landed(t, 2, 256)
        self.add(t, at.d, 0, self.rx[s, 1], self.ry[s, 2])
        self.add(t, at.d, 16, self.ry[s, 1], self.rx[s, 2])
        for n, (zz, dev) in enumerate(zip(at.zs, at.z_devs)):
            self.push(t, self.gp.at[s, zz, self.rows(at.d, 0, 32)], self.rz.at[s, n], 3, dev)

    def quarter(self, t, q, first=0, count=32):
        return self.out.at[t, pl.ds(pl.multiple_of(q * 32 + first, 16), count)]

    def total(self, t):
        at, s = self.at, self.slot(t)
        self.landed(t, 3, 96)
        total = self.gp[s, at.z, self.rows(at.d, 0, 32), :].astype(f32)
        for n in range(3):
            total = total + self.rz[s, n].astype(f32)
        self.fin[t] = total.astype(bf)
        pltpu.make_async_copy(self.fin.at[t], self.quarter(t, at.d), self.osem.at[t]).start()
        self.push(t, self.fin.at[t], self.quarter(t, at.d), 4, at.x_dev, 1)
        self.push(t, self.fin.at[t], self.quarter(t, at.d), 4, at.y_dev, 1)

    def share(self, t):
        at = self.at
        self.landed(t, 4, 64)
        self.push(t, self.quarter(t, at.dx, 0, 16), self.quarter(t, at.dx, 0, 16), 5, at.y_dev, 1)
        self.push(t, self.quarter(t, at.dy, 16, 16), self.quarter(t, at.dy, 16, 16), 5, at.x_dev, 1)

    def done(self, t):
        self.landed(t, 5, 32)
        self.left(t, 1, 96)
        pltpu.make_async_copy(self.fin.at[t], self.quarter(t, self.at.d), self.osem.at[t]).wait()

    def release(self, t):
        self.left(t, 0, 992)

    def tick(self, j, i):
        for offset, name in self.STEPS:
            if offset % 4 == i:
                t = j - offset // 4
                if isinstance(t, int):
                    if 0 <= t < self.count:
                        getattr(self, name)(t)
                else:
                    pl.when((t >= 0) & (t < self.count))(functools.partial(getattr(self, name), t))

    def drain(self, j, i, last):
        for k in range(4 * j + i, 4 * (last + 3) + 1):
            self.tick(k // 4, k % 4)


class Keep:
    SLOTS = 3

    def __init__(self, count, gp, out, sem):
        self.count, self.gp, self.out, self.sem = count, gp, out, sem

    @classmethod
    def scratch(cls, count):
        return [pltpu.VMEM((cls.SLOTS, 4, 256, CW), bf), pltpu.SemaphoreType.DMA((count,))]

    def slot(self, t):
        return lax.rem(t, self.SLOTS)

    def copy(self, t):
        return pltpu.make_async_copy(self.gp.at[self.slot(t)], self.out.at[t], self.sem.at[t])

    def tick(self, j, i):
        if i == 0:
            pl.when((j >= 0) & (j < self.count))(lambda: self.copy(j).start())

    def release(self, t):
        self.copy(t).wait()


class Small:
    def __init__(self, at, sums, ra, rb, one, rc, two, rd, out, send, recv):
        self.at, self.sums, self.ra, self.rb, self.one, self.rc, self.two, self.rd = at, sums, ra, rb, one, rc, two, rd
        self.out, self.send, self.recv = out, send, recv

    @staticmethod
    def scratch():
        slab = (16, 128)
        return [pltpu.VMEM(shape + slab, f32) for shape in ((4, 2), (4,), (3,), (), (), (), ())] + [
            pltpu.SemaphoreType.DMA((4,)), pltpu.SemaphoreType.DMA((4,))]

    def copy(self, n, src, dst, dev):
        return remote(src, dst, self.send.at[n], self.recv.at[n], dev)

    def pair(self):
        return self.copy(0, self.sums.at[:, 1 - self.at.c], self.ra, self.at.sib_dev)

    def step(self, n):
        at, c = self.at, self.at.c
        if n == 0:
            self.pair().start()
        if n == 1:
            self.pair().wait()
            self.sums[:, c] = self.sums[:, c] + self.ra[...]
            for i, (zz, dev) in enumerate(zip(at.zs, at.z_devs)):
                self.copy(1, self.sums.at[zz, c], self.rb.at[i], dev).start()
        if n == 2:
            self.copy(1, self.rb, self.rb, at.x_dev).wait()
            self.one[...] = self.sums[at.z, c] + self.rb[0] + self.rb[1] + self.rb[2]
            self.copy(2, self.one, self.rc, at.x_dev).start()
        if n == 3:
            self.copy(2, self.one, self.rc, at.x_dev).wait()
            self.two[...] = self.one[...] + self.rc[...]
            self.copy(3, self.two, self.rd, at.y_dev).start()
        if n == 4:
            self.copy(3, self.two, self.rd, at.y_dev).wait()
            self.out[...] = self.two[...] + self.rd[...]


def transpose_rows(src, dst, rows):
    full = rows // 128

    def one(i, carry):
        o = pl.multiple_of(i * 128, 128)
        dst[0:D, pl.ds(o, 128)] = src[pl.ds(o, 128), :].T
        return carry

    lax.fori_loop(0, full, one, 0)
    if rows % 128:
        dst[0:D, full * 128 : rows] = src[full * 128 : rows, :].T
    dst[0:D, rows:] = jnp.zeros((D, dst.shape[1] - rows), bf)
    if dst.shape[0] > D:
        dst[D:, :] = jnp.ones((dst.shape[0] - D, dst.shape[1]), bf)


def iota(shape, dim):
    return lax.broadcasted_iota(jnp.int32, shape, dim)


def units_of(first, rows):
    d = iota((rows, 128), 0) + first - UNIT * iota((rows, 128), 1)
    return jnp.where((d >= 0) & (d < UNIT), 1.0, 0.0).astype(bf)


def places_of(first, rows, width):
    r = iota((rows, width), 0) + first
    lane = iota((rows, width), 1)
    down = r - GRID * lane
    unit = lax.shift_right_logical(lane * 9363, 16)
    t = r - UNIT * unit
    across = t - GRID * lax.shift_right_logical(t * 37, 8)
    yes = jnp.ones((rows, width), f32)
    no = jnp.zeros((rows, width), f32)
    ohy = jnp.where((down >= 0) & (down < GRID), yes, no).astype(bf)
    ohx = jnp.where((t >= 0) & (t < UNIT) & (across == lane - GRID * unit), yes, no).astype(bf)
    return ohy, ohx


def layer_kernel(rows, comm, *refs):
    refs = list(refs)

    def take(n):
        got = refs[:n]
        del refs[:n]
        return got

    tok_h, g_h, tab, q_table, k_table = take(5)
    if comm:
        small, ws_h = take(2)
    else:
        vec_in, b_up_in, w_h = take(3)
    out_h, gt_h, gw_h = take(3)
    if comm:
        (sums_out,) = take(1)
    else:
        vg, db_qkv, db_up = take(3)
    x_h, normedt_h, mixed_h, att_h, stats_h = take(5)
    if comm:
        (w_h,) = take(1)
    a1, a2, b1, b2, w, q_feat, k_feat, vec, b_up, lsem, wsem, osem, isem, xsem, tsem = take(15)
    chunks = w_h.shape[0]
    feed = chunks - QUADS
    if comm:
        vg, db_qkv, db_up, smalls, ssem, gsend, grecv = take(7)
        small_refs = take(9)
        at = Place()
        gather = Gather(at, ws_h, w_h, gsend, grecv)
        tick = gather.tick
        red = Reduce(at, chunks, *refs[:6], gw_h, *refs[6:], w_h)
    else:
        tick = lambda t: None
        red = Keep(chunks, refs[0], gw_h, refs[1])
    KP = normedt_h.shape[1]
    pairs = rows // PAIR
    RB = PAIR // 7
    blocks = rows // RB

    def block(r):
        return pl.ds(pl.multiple_of(r * RB, 16), RB)

    def pair_rows(r):
        return pl.ds(pl.multiple_of(r * PAIR, 16), PAIR)

    def load(k, s):
        if comm:
            load_chunk(at, ws_h, w_h, k, 0, w.at[s], wsem.at[s])
        else:
            pltpu.make_async_copy(w_h.at[k], w.at[s], wsem.at[s]).start()

    def loaded(s):
        pltpu.make_async_copy(w_h.at[0], w.at[s], wsem.at[s]).wait()

    tok_in = pltpu.make_async_copy(tok_h, b2, lsem.at[0])
    tok_in.start()
    g_in = pltpu.make_async_copy(g_h, b2, lsem.at[1])
    if comm:
        at.barrier()
        own = smalls.at[at.f]
        smalls[at.f] = small[...]
        for dev in at.z_devs:
            remote(own, own, ssem.at[0], ssem.at[1], dev).start()
        for k in range(3):
            gather.begin(k)
    else:
        load(0, 0)
        vec[...] = vec_in[...]
        b_up[...] = b_up_in[...]

    def forward(normed, normedt, mixed, att, stats):
        def features(r, carry):
            unit = units_of(r * RB, RB)
            q_feat[block(r), :] = dot(unit, q_table[...]).astype(bf)
            k_feat[block(r), :] = dot(unit, k_table[...]).astype(bf)
            return carry

        lax.fori_loop(0, blocks, features, 0)
        tok_in.wait()

        def place(r, carry):
            ohy, ohx = places_of(r * RB, RB, tab.shape[1])
            py = dot(ohy, tab[0]) + dot(ohy, tab[1]) + dot(ohy, tab[2])
            px = dot(ohx, tab[0]) + dot(ohx, tab[1]) + dot(ohx, tab[2])
            a1[block(r), :] = b2[block(r), :].astype(f32) + jnp.concatenate([py, px], axis=1)
            return carry

        def norm_one(r, carry):
            xhat, _ = norm_parts(a1[block(r), :])
            normed[block(r), :] = (xhat * vec[0:1, :] + vec[1:2, :]).astype(bf)
            return carry

        if comm:
            lax.fori_loop(0, blocks // 2, place, 0)
            three = smalls.at[pl.ds(0, 3)]
            remote(three, three, ssem.at[0], ssem.at[1], at.x_dev).wait()
            for zz in [at.z] + at.zs:
                slab = smalls.at[2 * zz + at.c]
                remote(slab, slab, ssem.at[2], ssem.at[3], at.sib_dev).start()
            tick(0)
            lax.fori_loop(blocks // 2, blocks, place, 0)
            four = smalls.at[pl.ds(0, 4)]
            remote(four, four, ssem.at[2], ssem.at[3], at.sib_dev).wait()
            spread_vectors(smalls, vec, b_up)
        else:
            lax.fori_loop(0, blocks, place, 0)
        g_in.start()
        x_out = pltpu.make_async_copy(a1, x_h, osem.at[0])
        x_out.start()
        tick(1)
        lax.fori_loop(0, blocks, norm_one, 0)
        tick(2)
        transpose_rows(normed, normedt, rows)
        n_out = pltpu.make_async_copy(normedt, normedt_h, osem.at[1])
        n_out.start()
        if comm:
            gather.ready(0)
            load(0, 0)

        def saves(k):
            return (pltpu.make_async_copy(mixed, mixed_h.at[k], osem.at[2]),
                    pltpu.make_async_copy(att, att_h.at[k], osem.at[3]),
                    pltpu.make_async_copy(stats, stats_h.at[k], osem.at[4]))

        for k in range(QUADS):
            s = k % 2
            loaded(s)
            if not comm:
                load(k + 1, 1 - s)
            if k > 0:
                for c in saves(k - 1):
                    c.wait()
            cols = slice(QW * k, QW * (k + 1))
            b_qkv = jnp.concatenate([vec[2:3, cols], jnp.zeros((1, QW), f32), vec[3:4, cols]], axis=1)

            def project(r, carry):
                sl = pair_rows(r)
                mixed[sl, :] = (dot(normed[sl, :], w[s, :, 0 : 3 * QW]) + b_qkv).astype(bf)
                return carry

            lax.fori_loop(0, pairs, project, 0)
            saves(k)[0].start()

            def hook(i):
                if comm:
                    pl.when(i == pairs - 1)(functools.partial(tick, 3 + 2 * k))

            attention_forward(pairs, mixed, q_feat, k_feat, att, stats, hook)
            saves(k)[1].start()
            saves(k)[2].start()
            if comm:
                gather.ready(k + 1)
                load(k + 1, 1 - s)
            if k == 0:
                x_out.wait()

            def project_out(r, carry):
                sl = pair_rows(r)
                extra = vec[4:5, :] if k == 0 else 0.0
                a1[sl, :] += dot(att[sl, :], w[s, :, 3 * QW : CW], NT) + extra
                return carry

            lax.fori_loop(0, pairs, project_out, 0)
            tick(4 + 2 * k)

        def second(r, carry):
            xhat, _ = norm_parts(a1[block(r), :])
            b1[block(r), :] = (xhat * vec[5:6, :] + vec[6:7, :]).astype(bf)
            return carry

        lax.fori_loop(0, blocks, second, 0)
        n_out.wait()
        for c in saves(QUADS - 1):
            c.wait()

    pl.run_scoped(forward, pltpu.VMEM((rows, D), bf), pltpu.VMEM(normedt_h.shape, bf), pltpu.VMEM((rows, 3 * QW), bf),
                  pltpu.VMEM((rows, QW), bf), pltpu.VMEM((rows, QW), bf))

    def put(t, m, left, right):
        slot, n = red.slot(t), left.shape[1]
        for i in range(2):
            red.gp[slot, 2 * m + i, :, 0:n] = left[256 * i : 256 * (i + 1)].astype(bf)
            red.gp[slot, 2 * m + i, :, n:CW] = right[256 * i : 256 * (i + 1)].astype(bf)

    def out_copy():
        return pltpu.make_async_copy(b1, out_h, osem.at[0])

    def feed_forward(n2t, gt, act, dhid, acc):
        act[rows:KP, :] = jnp.zeros((KP - rows, FC), bf)
        dhid[rows:KP, :] = jnp.zeros((KP - rows, FC), bf)
        acc[...] = jnp.zeros_like(acc)
        a2[...] = jnp.zeros_like(a2)
        transpose_rows(b1, n2t, rows)
        g_in.wait()
        transpose_rows(b2, gt, rows)

        def chunk(j, carry):
            s = lax.rem(j, 2)
            loaded(s)
            after = QUADS + 1 + j
            if comm:
                for n in range(2):
                    pl.when(j == n)(functools.partial(tick, 11 + 2 * n))

                @pl.when(after < chunks)
                def _():
                    gather.ready(after)

            load(jnp.where(after < chunks, after, 0), 1 - s)
            red.tick(j - 1, 0)
            for r in range(pairs):
                sl = pair_rows(r)
                h = dot(b1[sl, :], w[s, :, 0:FC]) + b_up[pl.ds(j, 1), :]
                da = dot(b2[sl, :], w[s, :, FC:CW])
                phi = 0.5 * (1.0 + lax.erf(h * 0.7071067811865476))
                slope = phi + h * (jnp.exp(-0.5 * h * h) * 0.3989422804014327)
                a = (h * phi).astype(bf)
                dh = (da * slope).astype(bf)
                act[sl, :] = a
                dhid[sl, :] = dh
                acc[sl, :] += dot(a, w[s, :, FC:CW], NT)
                a2[sl, :] += dot(dh, w[s, :, 0:FC], NT)
                red.tick(j - 1, r + 1)
                if comm and r == 0:
                    pl.when(j == 0)(functools.partial(tick, 12))

            @pl.when(j >= red.SLOTS)
            def _():
                red.release(j - red.SLOTS)

            put(j, 0, dot(n2t[0:512, :], dhid[...]), dot(gt[0:512, :], act[...]))
            red.tick(j - 1, 3)
            left = dot(n2t[512:, :], dhid[...])
            db_up[pl.ds(j, 1), :] = left[512:513]
            put(j, 1, left, dot(gt[512:, :], act[...]))
            return carry

        lax.fori_loop(0, feed, chunk, 0)
        red.tick(feed - 1, 0)
        vg[...] = jnp.zeros_like(vg)

        def last(r, carry):
            sl = block(r)
            middle = a1[sl, :]
            b1[sl, :] = (middle + acc[sl, :] + vec[7:8, :]).astype(bf)
            a1[sl, :] = jnp.zeros_like(middle)
            xhat, inv = norm_parts(middle)
            dn = a2[sl, :]
            cot = b2[sl, :].astype(f32)
            e = dn * vec[5:6, :]
            gm = cot + (e - jnp.mean(e, axis=-1, keepdims=True) - xhat * jnp.mean(e * xhat, axis=-1, keepdims=True)) * inv
            a2[sl, :] = gm
            gb = gm.astype(bf)
            b2[sl, :] = gb
            vg[2:3, :] += jnp.sum(gb.astype(f32), axis=0, keepdims=True)
            vg[3:4, :] += jnp.sum(dn * xhat, axis=0, keepdims=True)
            vg[4:5, :] += jnp.sum(dn, axis=0, keepdims=True)
            vg[5:6, :] += jnp.sum(cot, axis=0, keepdims=True)
            pl.when(r == blocks // 2)(functools.partial(red.tick, feed - 1, 1))
            return carry

        lax.fori_loop(0, blocks, last, 0)
        out_copy().start()

    pl.run_scoped(feed_forward, pltpu.VMEM(normedt_h.shape, bf), pltpu.VMEM((D, KP), bf), pltpu.VMEM((KP, FC), bf),
                  pltpu.VMEM((KP, FC), bf), pltpu.VMEM((rows, D), f32))

    def backward(normedt, gbt, mixed, att, stats, datt, swap, dq, dk, dv, xb, ob):
        n_in = pltpu.make_async_copy(normedt_h, normedt, lsem.at[0])

        def inputs(k, s):
            return (pltpu.make_async_copy(mixed_h.at[k], mixed.at[s, pl.ds(0, rows)], isem.at[s, 0]),
                    pltpu.make_async_copy(att_h.at[k], att.at[s, pl.ds(0, rows)], isem.at[s, 1]),
                    pltpu.make_async_copy(stats_h.at[k], stats.at[s], isem.at[s, 2]))

        for c in inputs(0, 0):
            c.start()
        n_in.start()
        for s in range(2):
            mixed[s, rows:KP, :] = jnp.zeros((KP - rows, 3 * QW), bf)
            att[s, rows:KP, :] = jnp.zeros((KP - rows, QW), bf)
        swap[...] = jnp.where(low_lanes(128) != (iota((128, 128), 0) < 64), 1.0, 0.0).astype(bf)
        transpose_rows(b2, gbt, rows)

        def quad(k, carry):
            s = lax.rem(k, 2)
            t = feed + k
            loaded(s)
            for c in inputs(k, s):
                c.wait()

            @pl.when(k + 1 < QUADS)
            def _():
                load(k + 1, 1 - s)
                for c in inputs(k + 1, 1 - s):
                    c.start()

            def back(r, inner):
                sl = pair_rows(r)
                datt[sl, :] = dot(b2[sl, :], w[s, :, 3 * QW : CW]).astype(bf)
                return inner

            pl.when(k > 0)(lambda: red.tick(t - 1, 0))
            lax.fori_loop(0, pairs, back, 0)

            def hook(i):
                pl.when((i == pairs - 1) & (k > 0))(functools.partial(red.tick, t - 1, 1))
                pl.when(i == 2 * pairs - 1)(functools.partial(red.tick, t - 1, 2))

            attention_backward(pairs, mixed.at[s], att.at[s], stats.at[s], datt, k_feat, swap, dq, dk, dv, hook)
            red.release(t - red.SLOTS)
            pl.when(k == 0)(n_in.wait)
            put(t, 0, dot(normedt[0:512, :], mixed[s]), dot(gbt[0:512, :], att[s]))
            red.tick(t - 1, 3)
            left = dot(normedt[512:, :], mixed[s])
            db_qkv[pl.ds(k, 1), :] = left[512:513]
            put(t, 1, left, dot(gbt[512:, :], att[s]))

            @pl.when(k == QUADS - 1)
            def _():
                red.tick(t, 0)

            def back_in(r, inner):
                sl = pair_rows(r)
                a1[sl, :] += dot(mixed[s, sl, :], w[s, :, 0 : 3 * QW], NT)
                return inner

            lax.fori_loop(0, pairs, back_in, 0)
            return carry

        lax.fori_loop(0, QUADS, quad, 0)
        ring = xb.shape[0]

        def xcopy(r):
            s = lax.rem(r, ring)
            return pltpu.make_async_copy(x_h.at[block(r)], xb.at[s], xsem.at[s])

        def tcopy(r):
            s = lax.rem(r, 2)
            return pltpu.make_async_copy(ob.at[s], gt_h.at[block(r)], tsem.at[s])

        for r in range(ring):
            xcopy(r).start()

        def last(r, carry):
            xcopy(r).wait()
            pl.when(r >= 2)(lambda: tcopy(r - 2).wait())
            xhat, inv = norm_parts(xb[lax.rem(r, ring)])
            dn = a1[block(r), :]
            e = dn * vec[0:1, :]
            ob[lax.rem(r, 2)] = a2[block(r), :] + (
                e - jnp.mean(e, axis=-1, keepdims=True) - xhat * jnp.mean(e * xhat, axis=-1, keepdims=True)) * inv
            tcopy(r).start()
            vg[0:1, :] += jnp.sum(dn * xhat, axis=0, keepdims=True)
            vg[1:2, :] += jnp.sum(dn, axis=0, keepdims=True)
            pl.when(r + ring < blocks)(lambda: xcopy(r + ring).start())
            if comm:
                for n in range(1, 5):
                    pl.when(r == 3 * n - 1)(functools.partial(red.tick, chunks - 1 + n // 4, n % 4))
            return carry

        lax.fori_loop(0, blocks, last, 0)
        out_copy().wait()
        if comm:
            share = Small(at, *small_refs[:7], sums_out, *small_refs[7:])
            sums = share.sums
            sums[...] = jnp.zeros_like(sums)
            for f in range(8):
                lanes = slice(128 * f, 128 * (f + 1))
                q, half = slice(f // 2, f // 2 + 1), 128 * (f % 2)
                rows_of = [vg[0:1, lanes], vg[1:2, lanes], db_qkv[q, half : half + 128],
                           db_qkv[q, 2 * QW + half : 2 * QW + half + 128]] + [vg[n : n + 1, lanes] for n in (2, 3, 4, 5)]
                rows_of += [db_up[f : f + 1, 128 * i : 128 * (i + 1)] for i in range(4)]
                for i, row in enumerate(rows_of):
                    sums[f // 2, f % 2, i : i + 1, :] = row
            for n, k in enumerate(range(5, 13)):
                red.tick(chunks - 1 + k // 4, k % 4)
                share.step(n)
            for k in range(chunks):
                gather.finish(k)
        for r in (blocks - 2, blocks - 1):
            tcopy(r).wait()
        for t in range(chunks - red.SLOTS, chunks):
            red.release(t)

    pl.run_scoped(backward, pltpu.VMEM(normedt_h.shape, bf), pltpu.VMEM((D, KP), bf), pltpu.VMEM((2, KP, 3 * QW), bf),
                  pltpu.VMEM((2, KP, QW), bf), pltpu.VMEM((2, rows, QW), bf), pltpu.VMEM((rows, QW), bf), pltpu.VMEM((128, 128), bf), pltpu.VMEM((PAIR, 128), f32),
                  pltpu.VMEM((PAIR, 128), f32), pltpu.VMEM((PAIR, 128), f32), pltpu.VMEM((3, RB, D), f32),
                  pltpu.VMEM((2, RB, D), f32))


def layer(rows, comm, chunks, *args):
    A, V = any_spec(), vmem_spec()
    KP = -(-rows // 256) * 256
    sums = ((8, D), (QUADS, 3 * QW), (chunks - QUADS, FC))
    kept = [sds((rows, D), f32), sds((D + 16, KP), bf), sds((QUADS, rows, 3 * QW), bf), sds((QUADS, rows, QW), bf),
            sds((QUADS, rows, QW), bf)]
    first = [sds((rows, D), bf), sds((rows, D), f32), sds((chunks, 128, CW) if comm else (chunks, 4, 256, CW), bf)]
    scratch = [
        pltpu.VMEM((rows, D), f32), pltpu.VMEM((rows, D), f32), pltpu.VMEM((rows, D), bf), pltpu.VMEM((rows, D), bf),
        pltpu.VMEM((2, D, CW), bf), pltpu.VMEM((rows, 128), bf), pltpu.VMEM((rows, 128), bf), pltpu.VMEM((8, D), f32),
        pltpu.VMEM((chunks - QUADS, FC), f32),
        pltpu.SemaphoreType.DMA((2,)), pltpu.SemaphoreType.DMA((2,)), pltpu.SemaphoreType.DMA((5,)),
        pltpu.SemaphoreType.DMA((2, 3)), pltpu.SemaphoreType.DMA((3,)), pltpu.SemaphoreType.DMA((2,)),
    ]
    if comm:
        in_specs = [A, A, V, V, V, V, A]
        out_shape = first + [sds((16, 128), f32)] + kept + [sds((chunks, D, CW), bf)]
        out_specs = [A, A, A, V] + [A] * 6
        scratch += [pltpu.VMEM(shape, f32) for shape in sums] + [
            pltpu.VMEM((8, 16, 128), bf), pltpu.SemaphoreType.DMA((4,)), pltpu.SemaphoreType.DMA((chunks,)),
            pltpu.SemaphoreType.DMA((chunks, 6))] + Small.scratch() + Reduce.scratch(chunks)
        params = pltpu.CompilerParams(vmem_limit_bytes=VMEM_LIMIT, collective_id=0, has_side_effects=True)
    else:
        in_specs = [A, A, V, V, V, V, V, A]
        out_shape = first + [sds(shape, f32) for shape in sums] + kept
        out_specs = [A, A, A, V, V, V] + [A] * 5
        scratch += Keep.scratch(chunks)
        params = pltpu.CompilerParams(vmem_limit_bytes=VMEM_LIMIT)
    return pl.pallas_call(
        functools.partial(layer_kernel, rows, comm), out_shape=out_shape, in_specs=in_specs, out_specs=out_specs,
        scratch_shapes=scratch, compiler_params=params, name="encoder_layer",
    )(*args)


def unit_features(band_code):
    units = band_code.reshape(-1, UNITS_MB)
    labels = jnp.cumsum((units <= 1).astype(jnp.int32), axis=1) - 1 + UNITS_MB * (jnp.arange(units.shape[0], dtype=jnp.int32)[:, None] % 2)
    place = np.arange(128) % 64 - 3
    item = labels.reshape(-1, 1) == place[None, :]
    used = (place >= 0) & (place < 2 * UNITS_MB)
    keys = jnp.where(used & ~item, NEG, np.where(place < 0, 1.0, 0.0))
    pad = ((0, 128 - item.shape[0]), (0, 0))
    return jnp.pad(item.astype(bf), pad), jnp.pad(keys.astype(bf), pad)


def place_table(gsd_code):
    ratio = jnp.exp2((gsd_code.astype(f32) - 3.0) * 0.5)
    quarter = D // 4
    freq = jnp.exp2(jnp.arange(quarter, dtype=f32) * (-math.log2(10000.0) / quarter))
    a = jnp.arange(GRID, dtype=f32)
    angle = (a[None, :] * ratio[:, None]).reshape(-1)[:, None] * freq[None, :]
    tab = jnp.concatenate([jnp.sin(angle), jnp.cos(angle)], axis=1)
    n = tab.shape[0]
    pad = -(-n // 256) * 256
    tab = jnp.pad(tab, ((0, pad - n), (0, 0)))
    hi = lax.reduce_precision(tab, 8, 7)
    rest = tab - hi
    mid = lax.reduce_precision(rest, 8, 7)
    return jnp.stack([hi, mid, rest - mid]).astype(bf)


def pack_weights(qkv, out, up, down):
    n = qkv.shape[0]
    att = jnp.concatenate([qkv.reshape(n, 3, QUADS, QW).transpose(2, 0, 1, 3).reshape(QUADS, n, 3 * QW),
                           out.T.reshape(n, QUADS, QW).transpose(1, 0, 2)], axis=2)
    ff = up.shape[1] // FC
    feed = jnp.concatenate([up.reshape(n, ff, FC).transpose(1, 0, 2), down.T.reshape(n, ff, FC).transpose(1, 0, 2)], axis=2)
    return jnp.concatenate([att, feed], axis=0)


def local(dp, fsdp, tokens, band_code, gsd_code, norm1_gain, norm1_bias, qkv_weight, bias_q, bias_v, out_weight, bias_out,
          norm2_gain, norm2_bias, up_weight, bias_up, down_weight, bias_down, grad_out):
    rows = tokens.shape[0]
    comm = dp == 4 and fsdp == 8
    shard = pack_weights(qkv_weight, out_weight, up_weight, down_weight)
    chunks, n, _ = shard.shape
    vectors = (norm1_gain, norm1_bias, bias_q, bias_v, bias_out, norm2_gain, norm2_bias, bias_down)
    args = (tokens, grad_out, place_table(gsd_code)) + unit_features(band_code)
    if comm:
        small = jnp.concatenate([jnp.stack(vectors), bias_up.reshape(4, 128), jnp.zeros((4, 128), bf)])
        out, grad_tokens, gw, sg, *_ = layer(rows, True, chunks, *args, small, shard)
    else:
        gathered = lax.all_gather(jnp.stack(vectors), "fsdp", axis=1, tiled=True).astype(f32)
        up_bias = lax.all_gather(bias_up, "fsdp", axis=0, tiled=True).astype(f32).reshape(-1, FC)
        whole = lax.all_gather(shard, "fsdp", axis=1, tiled=True)
        out, grad_tokens, gw, vg, db_qkv, db_up, *_ = layer(rows, False, chunks, *args, gathered, up_bias, whole)
        sg = jnp.concatenate([vg[0:2], db_qkv[:, 0:QW].reshape(1, D), db_qkv[:, 2 * QW :].reshape(1, D), vg[2:6]], axis=0)
        sg = jnp.concatenate([sg.reshape(8, fsdp, n).transpose(1, 0, 2).reshape(fsdp, 8 * n), db_up.reshape(fsdp, 4 * n)], axis=1)
        sg = lax.psum(lax.psum_scatter(sg, "fsdp", scatter_dimension=0, tiled=True), "dp").reshape(12, n)
        gw = lax.psum(lax.psum_scatter(gw.reshape(chunks, D, CW), "fsdp", scatter_dimension=1, tiled=True), "dp")
    gw = gw.astype(f32)
    g_ff, g_att = gw[: chunks - QUADS], gw[chunks - QUADS :]
    g_qkv = g_att[:, :, : 3 * QW].reshape(QUADS, n, 3, QW).transpose(1, 2, 0, 3).reshape(n, 3 * D)
    g_out = g_att[:, :, 3 * QW :].transpose(0, 2, 1).reshape(D, n)
    g_up = g_ff[:, :, :FC].transpose(1, 0, 2).reshape(n, -1)
    g_down = g_ff[:, :, FC:].transpose(0, 2, 1).reshape(-1, n)
    return (out, grad_tokens, sg[0], sg[1], g_qkv, sg[2], sg[3], g_out, sg[4], sg[5], sg[6], g_up, sg[8:12].reshape(4 * n), g_down, sg[7])


def solution(mesh):
    rows, vec, first, second = P(("dp", "fsdp"), None), P("fsdp"), P("fsdp", None), P(None, "fsdp")
    codes = P(("dp", "fsdp"))
    return jax.shard_map(
        functools.partial(local, mesh.shape["dp"], mesh.shape["fsdp"]),
        mesh=mesh,
        in_specs=(rows, codes, codes, vec, vec, first, vec, vec, second, vec, vec, vec, first, vec, second, vec, rows),
        out_specs=(rows, rows, vec, vec, first, vec, vec, second, vec, vec, vec, first, vec, second, vec),
        check_vma=False,
    )
```

```python
import functools
import math

import jax
import jax.numpy as jnp
import numpy as np
from jax import lax
from jax.experimental import pallas as pl
from jax.experimental.pallas import tpu as pltpu
from jax.sharding import PartitionSpec as P

bf = jnp.bfloat16
f32 = jnp.float32
NN = (((1,), (0,)), ((), ()))
NT = (((1,), (1,)), ((), ()))
TN = (((0,), (0,)), ((), ()))
D = 1024
HEADS = 16
HEAD_DIM = 64
GRID = 7
UNIT = GRID * GRID
UNITS_MB = 8
BUF = UNIT * UNITS_MB
PAIR = 2 * BUF
QUADS = 4
QW = 256
FC = 512
CW = 1024
EPS = 1e-6
SCALE = 0.125
NEG = -1e30
VMEM_LIMIT = 62 << 20
KEYS = 384
WINDOWS = ((0, ((0, 192, 0), (192, 208, 16))), (384, ((0, 192, 0), (192, 208, 16))))
SPAN = 400


def dot(a, b, dims=NN):
    return lax.dot_general(a, b, dims, preferred_element_type=f32)


def any_spec():
    return pl.BlockSpec(memory_space=pl.ANY)


def vmem_spec():
    return pl.BlockSpec(memory_space=pltpu.VMEM)


def sds(shape, kind):
    return jax.ShapeDtypeStruct(shape, kind)


def norm_parts(v):
    center = v - jnp.mean(v, axis=-1, keepdims=True)
    inv = lax.rsqrt(jnp.mean(center * center, axis=-1, keepdims=True) + EPS)
    return center * inv, inv


def low_lanes(rows):
    return lax.broadcasted_iota(jnp.int32, (rows, 128), 1) < 64


def split_terms(v):
    lane = lax.broadcasted_iota(jnp.int32, v.shape, 1) & 63
    hi = v.astype(bf).astype(f32)
    rest = v - hi
    mid = rest.astype(bf).astype(f32)
    return jnp.where(lane == 0, hi, jnp.where(lane == 1, mid, jnp.where(lane == 2, rest - mid, 0.0))), lane < 3


def attention_forward(pairs, mixed, q_feat, k_feat, attended, stats, hook):
    def one(i, carry):
        p, hp = i // 2, lax.rem(i, 2)
        base = pl.multiple_of(p * PAIR, 16)
        lane0 = pl.multiple_of(hp * 128, 128)
        blocks = [(w, n, start, *half) for w, (start, halves) in enumerate(WINDOWS) for n, half in enumerate(halves)]
        spans = {}

        def window(w, start):
            if w not in spans:
                span = pl.ds(pl.multiple_of(base + start, 16), SPAN)
                k2 = mixed[span, pl.ds(pl.multiple_of(lane0 + QW, 128), 128)]
                v2 = mixed[span, pl.ds(pl.multiple_of(lane0 + 2 * QW, 128), 128)]
                kf = k_feat[span, :]
                low = low_lanes(SPAN)
                ones = jnp.ones_like(v2)
                spans[w] = ((jnp.where(low, k2, kf), jnp.where(low, kf, k2)), (jnp.where(low, v2, ones), jnp.where(low, ones, v2)))
            return spans[w]

        def scores(block):
            w, n, start, q0, qn, k0 = block
            keys, _ = window(w, start)
            rows = pl.ds(pl.multiple_of(base + start + q0, 16), qn)
            q2 = mixed[rows, pl.ds(lane0, 128)] * jnp.asarray(SCALE, bf)
            qf = q_feat[rows, :]
            low = low_lanes(qn)
            return [dot(q, keys[h][k0 : k0 + KEYS], NT) for h, q in enumerate((jnp.where(low, q2, qf), jnp.where(low, qf, q2)))]

        tail = None
        ahead = scores(blocks[0])
        for b, (w, n, start, q0, qn, k0) in enumerate(blocks):
            now = ahead
            if b + 1 < len(blocks):
                ahead = scores(blocks[b + 1])
            _, values = window(w, start)
            rows = pl.ds(pl.multiple_of(base + start + q0, 16), qn)
            low = low_lanes(qn)
            tops = [jnp.max(s, axis=-1, keepdims=True) for s in now]
            outs = [dot(jnp.exp(s - m).astype(bf), values[h][k0 : k0 + KEYS]) for h, (s, m) in enumerate(zip(now, tops))]
            total = jnp.where(low, outs[1], outs[0])
            out = jnp.where(low, outs[0], outs[1]) / pltpu.roll(total, 64, 1)
            terms, at = split_terms(-(jnp.where(low, tops[1], tops[0]) + jnp.log(total)))
            stat = jnp.where(at, terms, q_feat[rows, :].astype(f32))
            if w == 0 and n == 1:
                tail = (out[qn - 16 :], stat[qn - 16 :])
            if w == 1 and n == 0:
                first = lax.broadcasted_iota(jnp.int32, (16, 128), 0) < 8
                out = jnp.concatenate([jnp.where(first, tail[0], out[0:16]), out[16:]], axis=0)
                stat = jnp.concatenate([jnp.where(first, tail[1], stat[0:16]), stat[16:]], axis=0)
            attended[rows, pl.ds(lane0, 128)] = out.astype(bf)
            stats[rows, pl.ds(lane0, 128)] = stat.astype(bf)
        hook(i)
        return carry

    lax.fori_loop(0, pairs * 2, one, 0)


def attention_backward(pairs, mixed, att, stats, datt, k_feat, swap, dq, dk, dv, hook):
    def one(i, carry):
        p, hp = i // 2, lax.rem(i, 2)
        base = pl.multiple_of(p * PAIR, 16)
        lane0 = pl.multiple_of(hp * 128, 128)
        lanes = pl.ds(lane0, 128)
        dq[...] = jnp.zeros_like(dq)
        dk[...] = jnp.zeros_like(dk)
        dv[...] = jnp.zeros_like(dv)
        blocks = [(w, n, start, *half) for w, (start, halves) in enumerate(WINDOWS) for n, half in enumerate(halves)]
        spans = {}

        def window(w, start):
            if w not in spans:
                span = pl.ds(pl.multiple_of(base + start, 16), SPAN)
                k2 = mixed[span, pl.ds(pl.multiple_of(lane0 + QW, 128), 128)]
                v2 = mixed[span, pl.ds(pl.multiple_of(lane0 + 2 * QW, 128), 128)]
                kf = k_feat[span, :]
                low = low_lanes(SPAN)
                zero = jnp.zeros_like(k2)
                terms = (lax.broadcasted_iota(jnp.int32, (SPAN, 128), 1) & 63) < 3
                vf = jnp.where(terms, jnp.ones_like(v2), zero)
                spans[w] = ((jnp.where(low, k2, kf), jnp.where(low, kf, k2)), (jnp.where(low, k2, zero), jnp.where(low, zero, k2)),
                            (jnp.where(low, v2, vf), jnp.where(low, vf, v2)))
            return spans[w]

        def products(block):
            w, n, start, q0, qn, k0 = block
            keys, _, values = window(w, start)
            rows = pl.ds(pl.multiple_of(base + start + q0, 16), qn)
            q2 = mixed[rows, lanes] * jnp.asarray(SCALE, bf)
            do2 = datt[rows, lanes]
            if w != n:
                r = lax.broadcasted_iota(jnp.int32, (qn, 128), 0)
                mine = r < qn - 8 if n == 1 else r >= 8
                do2 = jnp.where(mine, do2, jnp.zeros_like(do2))
            qf = stats[rows, lanes]
            low = low_lanes(qn)
            zero = jnp.zeros_like(q2)
            prod = do2.astype(f32) * att[rows, lanes].astype(f32)
            hi = prod.astype(bf)
            inner = dot(hi, swap[...]) + dot((prod - hi.astype(f32)).astype(bf), swap[...])
            df = split_terms(-inner)[0].astype(bf)
            kk = slice(k0, k0 + KEYS)
            heads = []
            for h in range(2):
                pick = (lambda a, b: jnp.where(low, a, b)) if h == 0 else (lambda a, b: jnp.where(low, b, a))
                heads.append((dot(pick(q2, qf), keys[h][kk], NT), dot(pick(do2, df), values[h][kk], NT), pick(do2, zero), pick(q2, zero)))
            return heads

        ahead = products(blocks[0])
        for b, (w, n, start, q0, qn, k0) in enumerate(blocks):
            now = ahead
            if b + 1 < len(blocks):
                ahead = products(blocks[b + 1])
            plain = window(w, start)[1]
            at, kat = start + q0, start + k0
            pieces = []
            for h, (s, slope, o, q) in enumerate(now):
                probs = jnp.exp(s)
                pieces.append((probs.astype(bf), (probs * slope).astype(bf), o, q, plain[h][k0 : k0 + KEYS]))
            (pa, sa, oa, qa, ka), (pb, sb, ob, qb, kb) = pieces
            dv[kat : kat + KEYS, :] += dot(pa, oa, TN) + dot(pb, ob, TN)
            dk[kat : kat + KEYS, :] += dot(sa, qa, TN) + dot(sb, qb, TN)
            dq[at : at + qn, :] += dot(sa, ka) + dot(sb, kb)
        rows = pl.ds(base, PAIR)
        mixed[rows, lanes] = (dq[...] * SCALE).astype(bf)
        mixed[rows, pl.ds(pl.multiple_of(lane0 + QW, 128), 128)] = dk[...].astype(bf)
        mixed[rows, pl.ds(pl.multiple_of(lane0 + 2 * QW, 128), 128)] = dv[...].astype(bf)
        hook(i)
        return carry

    lax.fori_loop(0, pairs * 2, one, 0)


MESH = pl.DeviceIdType.MESH


class Place:
    def __init__(self):
        self.d = lax.axis_index("dp")
        self.f = lax.axis_index("fsdp")
        self.z = lax.div(self.f, 2)
        self.c = lax.rem(self.f, 2)
        self.dx = self.d + 1 - 2 * lax.rem(self.d, 2)
        self.dy = lax.rem(self.d + 2, 4)
        self.dd = 3 - self.d
        self.sib = self.f + 1 - 2 * self.c
        self.zs = [lax.rem(self.z + n, 4) for n in (1, 2, 3)]
        self.x_dev = (self.dx, self.f)
        self.y_dev = (self.dy, self.f)
        self.sib_dev = (self.d, self.sib)
        self.z_devs = [(self.d, 2 * zz + self.c) for zz in self.zs]

    def barrier(self):
        sem = pltpu.get_barrier_semaphore()
        for dev in [self.x_dev, self.y_dev, self.sib_dev] + self.z_devs:
            pl.semaphore_signal(sem, inc=1, device_id=dev, device_id_type=MESH)
        pl.semaphore_wait(sem, 6)


def remote(src, dst, send, recv, dev):
    return pltpu.make_async_remote_copy(src, dst, send, recv, device_id=dev, device_id_type=MESH)


class Gather:
    def __init__(self, at, shard, whole, send, recv):
        self.at, self.shard, self.whole, self.send, self.recv = at, shard, whole, send, recv
        self.chunks = whole.shape[0]

    def rows(self, q, first, count):
        return pl.ds(pl.multiple_of(self.at.c * 128 + 32 * q + first, 16), count)

    def push(self, k, planes, rows, stage, dev, src=None):
        dst = self.whole.at[k, planes, rows]
        remote(dst if src is None else src, dst, self.send.at[k], self.recv.at[k, stage], dev).start()

    def landed(self, k, stage, planes, rows):
        part = self.whole.at[k, pl.ds(0, planes), pl.ds(0, rows)]
        remote(part, part, self.send.at[k], self.recv.at[k, stage], self.at.x_dev).wait_recv()

    def begin(self, k):
        at = self.at
        quarter = self.shard.at[k, pl.ds(pl.multiple_of(32 * at.d, 16), 32)]
        for n, dev in enumerate(at.z_devs):
            self.push(k, 3 - n, self.rows(at.d, 0, 32), 0, dev, quarter)
        self.push(k, 0, self.rows(0, 0, 128), 5, at.sib_dev, self.shard.at[k])

    def spread(self, k):
        at = self.at
        self.landed(k, 0, 3, 32)
        self.push(k, pl.ds(1, 3), self.rows(at.d, 0, 32), 1, at.x_dev)
        self.push(k, pl.ds(1, 3), self.rows(at.d, 0, 32), 2, at.y_dev)

    def diagonal(self, k):
        at = self.at
        self.landed(k, 1, 3, 32)
        self.landed(k, 2, 3, 32)
        self.push(k, pl.ds(1, 3), self.rows(at.dx, 0, 16), 3, at.y_dev)
        self.push(k, pl.ds(1, 3), self.rows(at.dy, 16, 16), 4, at.x_dev)

    def pair(self, k):
        self.landed(k, 3, 3, 16)
        self.landed(k, 4, 3, 16)
        self.push(k, pl.ds(1, 3), self.rows(0, 0, 128), 5, self.at.sib_dev)

    def ready(self, k):
        self.landed(k, 5, 4, 128)

    def load(self, k, dst, sem):
        at = self.at
        own = pl.multiple_of(at.z * 256 + at.c * 128, 128)
        other = pl.multiple_of((1 - at.c) * 128, 128)
        pltpu.make_async_copy(self.shard.at[k], dst.at[pl.ds(own, 128)], sem).start()
        pltpu.make_async_copy(self.whole.at[k, 0, pl.ds(other, 128)], dst.at[pl.ds(at.z * 256 + other, 128)], sem).start()
        for n, zz in enumerate(at.zs):
            pltpu.make_async_copy(self.whole.at[k, n + 1], dst.at[pl.ds(pl.multiple_of(zz * 256, 256), 256)], sem).start()

    def run(self, *steps):
        for step, k in steps:
            if step == "s":
                if k + 3 < self.chunks:
                    self.begin(k + 3)
                self.spread(k)
            elif step == "d":
                self.diagonal(k)
            else:
                self.pair(k)

    def finish(self, k):
        part = self.whole.at[k, :, pl.ds(0, 224)]
        remote(part, part, self.send.at[k], self.recv.at[k, 0], self.at.x_dev).wait_send()


def spread_vectors(shards, vec, b_up):
    n = vec.shape[1] // 128
    for f in range(n):
        vec[:, 128 * f : 128 * (f + 1)] = shards[f, 0:8, :].astype(f32)
        for i in range(4):
            b_up[f : f + 1, 128 * i : 128 * (i + 1)] = shards[f, 8 + i : 9 + i, :].astype(f32)


class Reduce:
    SLOTS = 3
    STEPS = ((16, "done"), (13, "share"), (10, "total"), (8, "planes"), (5, "relay"), (1, "cross"), (0, "pair"))

    def __init__(self, at, count, gp, r1, rx, ry, rz, fin, out, send, recv, osem, sizes):
        self.at, self.count, self.gp, self.r1, self.rx, self.ry, self.rz = at, count, gp, r1, rx, ry, rz
        self.fin, self.out, self.send, self.recv, self.osem, self.sizes = fin, out, send, recv, osem, sizes

    @classmethod
    def scratch(cls, count):
        s = cls.SLOTS
        return [pltpu.VMEM((s, 4, 256, CW), bf), pltpu.VMEM((2, 4, 128, CW), bf), pltpu.VMEM((s, 3, 4, 16, CW), bf),
                pltpu.VMEM((s, 3, 4, 16, CW), bf), pltpu.VMEM((s, 3, 32, CW), bf), pltpu.VMEM((count, 32, CW), bf),
                pltpu.SemaphoreType.DMA((count, 3)), pltpu.SemaphoreType.DMA((count, 6)), pltpu.SemaphoreType.DMA((count,))]

    def slot(self, t):
        return lax.rem(t, self.SLOTS)

    def rows(self, q, first, count):
        return pl.ds(pl.multiple_of(self.at.c * 128 + q * 32 + first, 16), count)

    def push(self, t, src, dst, stage, dev, group=0):
        remote(src, dst, self.send.at[t, group], self.recv.at[t, stage], dev).start()

    def landed(self, t, stage, rows):
        part = self.part(rows)
        remote(part, part, self.send.at[t, 0], self.recv.at[t, stage], self.at.x_dev).wait_recv()

    def part(self, rows):
        planes = 1 if rows <= 256 else 4
        return self.sizes.at[0, pl.ds(0, planes), pl.ds(0, rows // planes)]

    def left(self, t, group, rows):
        part = self.part(rows)
        remote(part, part, self.send.at[t, group], self.recv.at[t, 0], self.at.x_dev).wait_send()

    def add(self, t, q, first, *parts):
        s, sl = self.slot(t), self.rows(q, first, 16)
        total = self.gp[s, :, sl, :].astype(f32)
        for p in parts:
            total = total + p.astype(f32)
        self.gp[s, :, sl, :] = total.astype(bf)

    def pair(self, t):
        s = self.slot(t)
        other = pl.ds(pl.multiple_of((1 - self.at.c) * 128, 128), 128)
        self.push(t, self.gp.at[s, :, other], self.r1.at[lax.rem(t, 2)], 0, self.at.sib_dev)

    def cross(self, t):
        at, s = self.at, self.slot(t)
        self.landed(t, 0, 512)
        own = pl.ds(pl.multiple_of(at.c * 128, 128), 128)

        def plane(zz, carry):
            self.gp[s, zz, own, :] = (self.gp[s, zz, own, :].astype(f32) + self.r1[lax.rem(t, 2), zz].astype(f32)).astype(bf)
            return carry

        lax.fori_loop(0, 4, plane, 0)
        gp = self.gp
        self.push(t, gp.at[s, :, self.rows(at.dd, 0, 16)], self.rx.at[s, 0], 1, at.x_dev)
        self.push(t, gp.at[s, :, self.rows(at.dd, 16, 16)], self.ry.at[s, 0], 1, at.y_dev)
        self.push(t, gp.at[s, :, self.rows(at.dx, 0, 16)], self.rx.at[s, 1], 2, at.x_dev)
        self.push(t, gp.at[s, :, self.rows(at.dy, 16, 16)], self.ry.at[s, 1], 2, at.y_dev)

    def relay(self, t):
        at, s = self.at, self.slot(t)
        self.landed(t, 1, 128)
        self.add(t, at.dy, 0, self.rx[s, 0])
        self.add(t, at.dx, 16, self.ry[s, 0])
        self.push(t, self.gp.at[s, :, self.rows(at.dy, 0, 16)], self.ry.at[s, 2], 2, at.y_dev)
        self.push(t, self.gp.at[s, :, self.rows(at.dx, 16, 16)], self.rx.at[s, 2], 2, at.x_dev)

    def planes(self, t):
        at, s = self.at, self.slot(t)
        self.landed(t, 2, 256)
        self.add(t, at.d, 0, self.rx[s, 1], self.ry[s, 2])
        self.add(t, at.d, 16, self.ry[s, 1], self.rx[s, 2])
        for n, (zz, dev) in enumerate(zip(at.zs, at.z_devs)):
            self.push(t, self.gp.at[s, zz, self.rows(at.d, 0, 32)], self.rz.at[s, n], 3, dev, 2)

    def quarter(self, t, q, first=0, count=32):
        return self.out.at[t, pl.ds(pl.multiple_of(q * 32 + first, 16), count)]

    def total(self, t):
        at, s = self.at, self.slot(t)
        self.landed(t, 3, 96)
        total = self.gp[s, at.z, self.rows(at.d, 0, 32), :].astype(f32)
        for n in range(3):
            total = total + self.rz[s, n].astype(f32)
        self.fin[t] = total.astype(bf)
        pltpu.make_async_copy(self.fin.at[t], self.quarter(t, at.d), self.osem.at[t]).start()
        self.push(t, self.fin.at[t], self.quarter(t, at.d), 4, at.x_dev, 1)
        self.push(t, self.fin.at[t], self.quarter(t, at.d), 4, at.y_dev, 1)

    def share(self, t):
        at = self.at
        self.landed(t, 4, 64)
        self.push(t, self.quarter(t, at.dx, 0, 16), self.quarter(t, at.dx, 0, 16), 5, at.y_dev, 1)
        self.push(t, self.quarter(t, at.dy, 16, 16), self.quarter(t, at.dy, 16, 16), 5, at.x_dev, 1)

    def done(self, t):
        self.landed(t, 5, 32)
        self.left(t, 1, 96)
        pltpu.make_async_copy(self.fin.at[t], self.quarter(t, self.at.d), self.osem.at[t]).wait()

    def release(self, t):
        self.left(t, 0, 896)
        self.left(t, 2, 96)

    def tick(self, j, i):
        for offset, name in self.STEPS:
            if offset % 4 == i:
                t = j - offset // 4
                if isinstance(t, int):
                    if 0 <= t < self.count:
                        getattr(self, name)(t)
                else:
                    pl.when((t >= 0) & (t < self.count))(functools.partial(getattr(self, name), t))

    def drain(self, j, i, last):
        for k in range(4 * j + i, 4 * (last + 3) + 1):
            self.tick(k // 4, k % 4)


class Keep:
    SLOTS = 3

    def __init__(self, count, gp, out, sem):
        self.count, self.gp, self.out, self.sem = count, gp, out, sem

    @classmethod
    def scratch(cls, count):
        return [pltpu.VMEM((cls.SLOTS, 4, 256, CW), bf), pltpu.SemaphoreType.DMA((count,))]

    def slot(self, t):
        return lax.rem(t, self.SLOTS)

    def copy(self, t):
        return pltpu.make_async_copy(self.gp.at[self.slot(t)], self.out.at[t], self.sem.at[t])

    def tick(self, j, i):
        if i == 0:
            pl.when((j >= 0) & (j < self.count))(lambda: self.copy(j).start())

    def release(self, t):
        self.copy(t).wait()


class Small:
    def __init__(self, at, sums, ra, rb, one, rc, two, rd, out, send, recv):
        self.at, self.sums, self.ra, self.rb, self.one, self.rc, self.two, self.rd = at, sums, ra, rb, one, rc, two, rd
        self.out, self.send, self.recv = out, send, recv

    @staticmethod
    def scratch():
        slab = (16, 128)
        return [pltpu.VMEM(shape + slab, f32) for shape in ((4, 2), (4,), (3,), (), (), (), ())] + [
            pltpu.SemaphoreType.DMA((4,)), pltpu.SemaphoreType.DMA((4,))]

    def copy(self, n, src, dst, dev):
        return remote(src, dst, self.send.at[n], self.recv.at[n], dev)

    def pair(self):
        return self.copy(0, self.sums.at[:, 1 - self.at.c], self.ra, self.at.sib_dev)

    def step(self, n):
        at, c = self.at, self.at.c
        if n > 4:
            return
        if n == 0:
            self.pair().start()
        if n == 1:
            self.pair().wait()
            self.sums[:, c] = self.sums[:, c] + self.ra[...]
            for i, (zz, dev) in enumerate(zip(at.zs, at.z_devs)):
                self.copy(1, self.sums.at[zz, c], self.rb.at[i], dev).start()
        if n == 2:
            self.copy(1, self.rb, self.rb, at.x_dev).wait()
            self.one[...] = self.sums[at.z, c] + self.rb[0] + self.rb[1] + self.rb[2]
            self.copy(2, self.one, self.rc, at.x_dev).start()
        if n == 3:
            self.copy(2, self.one, self.rc, at.x_dev).wait()
            self.two[...] = self.one[...] + self.rc[...]
            self.copy(3, self.two, self.rd, at.y_dev).start()
        if n == 4:
            self.copy(3, self.two, self.rd, at.y_dev).wait()
            self.out[...] = self.two[...] + self.rd[...]


def transpose_rows(src, dst, rows):
    full = rows // 128

    def one(i, carry):
        o = pl.multiple_of(i * 128, 128)
        dst[0:D, pl.ds(o, 128)] = src[pl.ds(o, 128), :].T
        return carry

    lax.fori_loop(0, full, one, 0)
    if rows % 128:
        dst[0:D, full * 128 : rows] = src[full * 128 : rows, :].T
    dst[0:D, rows:] = jnp.zeros((D, dst.shape[1] - rows), bf)
    if dst.shape[0] > D:
        dst[D:, :] = jnp.ones((dst.shape[0] - D, dst.shape[1]), bf)


def iota(shape, dim):
    return lax.broadcasted_iota(jnp.int32, shape, dim)


def units_of(first, rows):
    d = iota((rows, 128), 0) + first - UNIT * iota((rows, 128), 1)
    return jnp.where((d >= 0) & (d < UNIT), 1.0, 0.0).astype(bf)


def places_of(first, rows, width):
    r = iota((rows, width), 0) + first
    lane = iota((rows, width), 1)
    down = r - GRID * lane
    unit = lax.shift_right_logical(lane * 9363, 16)
    t = r - UNIT * unit
    across = t - GRID * lax.shift_right_logical(t * 37, 8)
    yes = jnp.ones((rows, width), f32)
    no = jnp.zeros((rows, width), f32)
    ohy = jnp.where((down >= 0) & (down < GRID), yes, no).astype(bf)
    ohx = jnp.where((t >= 0) & (t < UNIT) & (across == lane - GRID * unit), yes, no).astype(bf)
    return ohy, ohx


FIRST_STEPS = ((("s", 8),), (("s", 10), ("p", 7), ("d", 8)), (("p", 8), ("d", 10)), (("p", 10),))
SECOND_STEPS = ((("s", 9), ("p", 6), ("d", 7)), (("s", 11), ("d", 9)), (("p", 9), ("d", 11)), (("p", 11),))


def layer_kernel(rows, comm, *refs):
    refs = list(refs)

    def take(n):
        got = refs[:n]
        del refs[:n]
        return got

    tok_h, g_h, tab, q_table, k_table = take(5)
    if comm:
        small, ws_h = take(2)
    else:
        vec_in, b_up_in, w_h = take(3)
    out_h, gt_h, gw_h = take(3)
    if comm:
        (sums_out,) = take(1)
    else:
        vg, db_qkv, db_up = take(3)
    x_h, normedt_h, mixed_h, att_h, stats_h = take(5)
    if comm:
        (w_h,) = take(1)
    a1, a2, b1, b2, w, q_feat, k_feat, vec, b_up, lsem, wsem, osem, isem, xsem, tsem = take(15)
    chunks = w_h.shape[0]
    feed = chunks - QUADS
    if comm:
        vg, db_qkv, db_up, smalls, ssem, gsend, grecv = take(7)
        small_refs = take(9)
        at = Place()
        gather = Gather(at, ws_h, w_h, gsend, grecv)
        tick = gather.run
        red = Reduce(at, chunks, *refs[:6], gw_h, *refs[6:], w_h)
    else:
        tick = lambda *steps: None
        red = Keep(chunks, refs[0], gw_h, refs[1])
    KP = normedt_h.shape[1]
    pairs = rows // PAIR
    RB = PAIR // 7
    blocks = rows // RB

    def block(r):
        return pl.ds(pl.multiple_of(r * RB, 16), RB)

    def pair_rows(r):
        return pl.ds(pl.multiple_of(r * PAIR, 16), PAIR)

    def load(k, s):
        if comm:
            gather.load(k, w.at[s], wsem.at[s])
        else:
            pltpu.make_async_copy(w_h.at[k], w.at[s], wsem.at[s]).start()

    def loaded(s):
        pltpu.make_async_copy(w.at[s], w.at[s], wsem.at[s]).wait()

    tok_in = pltpu.make_async_copy(tok_h, b2, lsem.at[0])
    tok_in.start()
    g_in = pltpu.make_async_copy(g_h, b2, lsem.at[1])
    if comm:
        at.barrier()
        own = smalls.at[at.f]
        smalls[at.f] = small[...]
        for dev in at.z_devs:
            remote(own, own, ssem.at[0], ssem.at[1], dev).start()
        for k in range(3):
            gather.begin(k)
    else:
        load(0, 0)
        vec[...] = vec_in[...]
        b_up[...] = b_up_in[...]

    def forward(normed, normedt, mixed, att, stats):
        def features(r, carry):
            unit = units_of(r * RB, RB)
            q_feat[block(r), :] = dot(unit, q_table[...]).astype(bf)
            k_feat[block(r), :] = dot(unit, k_table[...]).astype(bf)
            return carry

        lax.fori_loop(0, blocks, features, 0)
        tok_in.wait()

        def place(r, carry):
            n = PAIR
            sl = pl.ds(pl.multiple_of(r * n, 16), n)
            for half, hot in enumerate(places_of(r * n, n, tab.shape[1])):
                cols = slice(D // 2 * half, D // 2 * (half + 1))
                a1[sl, cols] = b2[sl, cols].astype(f32) + (dot(hot, tab[0]) + dot(hot, tab[1]) + dot(hot, tab[2]))
            return carry

        def norm_one(r, carry):
            xhat, _ = norm_parts(a1[block(r), :])
            normed[block(r), :] = (xhat * vec[0:1, :] + vec[1:2, :]).astype(bf)
            return carry

        if comm:
            lax.fori_loop(0, pairs // 2, place, 0)
            three = smalls.at[pl.ds(0, 3)]
            remote(three, three, ssem.at[0], ssem.at[1], at.x_dev).wait()
            for zz in [at.z] + at.zs:
                slab = smalls.at[2 * zz + at.c]
                remote(slab, slab, ssem.at[2], ssem.at[3], at.sib_dev).start()
            tick(("s", 0))
            lax.fori_loop(pairs // 2, pairs, place, 0)
            four = smalls.at[pl.ds(0, 4)]
            remote(four, four, ssem.at[2], ssem.at[3], at.sib_dev).wait()
            spread_vectors(smalls, vec, b_up)
        else:
            lax.fori_loop(0, pairs, place, 0)
        g_in.start()
        x_out = pltpu.make_async_copy(a1, x_h, osem.at[0])
        x_out.start()
        tick(("s", 1))
        lax.fori_loop(0, blocks, norm_one, 0)
        tick(("s", 2), ("d", 0))
        transpose_rows(normed, normedt, rows)
        n_out = pltpu.make_async_copy(normedt, normedt_h, osem.at[1])
        n_out.start()
        tick(("p", 0), ("d", 1))
        if comm:
            gather.ready(0)
            load(0, 0)

        def saves(k):
            return (pltpu.make_async_copy(mixed, mixed_h.at[k], osem.at[2]),
                    pltpu.make_async_copy(att, att_h.at[k], osem.at[3]),
                    pltpu.make_async_copy(stats, stats_h.at[k], osem.at[4]))

        for k in range(QUADS):
            s = k % 2
            loaded(s)
            if not comm:
                load(k + 1, 1 - s)
            if k > 0:
                for c in saves(k - 1):
                    c.wait()
            cols = slice(QW * k, QW * (k + 1))
            b_qkv = jnp.concatenate([vec[2:3, cols], jnp.zeros((1, QW), f32), vec[3:4, cols]], axis=1)

            tick(("p", k + 1), ("s", k + 3))

            def project(r, carry):
                sl = pair_rows(r)
                mixed[sl, :] = (dot(normed[sl, :], w[s, :, 0 : 3 * QW]) + b_qkv).astype(bf)
                return carry

            lax.fori_loop(0, pairs, project, 0)
            saves(k)[0].start()

            def advance():
                gather.ready(k + 1)
                load(k + 1, 1 - s)
                tick(("d", k + 2))

            def hook(i):
                if comm:
                    pl.when(i == pairs - 1)(advance)

            attention_forward(pairs, mixed, q_feat, k_feat, att, stats, hook)
            saves(k)[1].start()
            saves(k)[2].start()
            if k == 0:
                x_out.wait()

            def project_out(r, carry):
                sl = pair_rows(r)
                extra = vec[4:5, :] if k == 0 else 0.0
                a1[sl, :] += dot(att[sl, :], w[s, :, 3 * QW : CW], NT) + extra
                return carry

            lax.fori_loop(0, pairs, project_out, 0)

        def second(r, carry):
            xhat, _ = norm_parts(a1[block(r), :])
            b1[block(r), :] = (xhat * vec[5:6, :] + vec[6:7, :]).astype(bf)
            return carry

        lax.fori_loop(0, blocks, second, 0)
        tick(("s", 7), ("p", 5), ("d", 6))
        n_out.wait()
        for c in saves(QUADS - 1):
            c.wait()

    pl.run_scoped(forward, pltpu.VMEM((rows, D), bf), pltpu.VMEM(normedt_h.shape, bf), pltpu.VMEM((rows, 3 * QW), bf),
                  pltpu.VMEM((rows, QW), bf), pltpu.VMEM((rows, QW), bf))

    def put(t, m, left, right):
        slot, n = red.slot(t), left.shape[1]
        for i in range(2):
            red.gp[slot, 2 * m + i, :, 0:n] = left[256 * i : 256 * (i + 1)].astype(bf)
            red.gp[slot, 2 * m + i, :, n:CW] = right[256 * i : 256 * (i + 1)].astype(bf)

    def out_copy():
        return pltpu.make_async_copy(b1, out_h, osem.at[0])

    def feed_forward(n2t, gt, act, dhid, acc):
        act[rows:KP, :] = jnp.zeros((KP - rows, FC), bf)
        dhid[rows:KP, :] = jnp.zeros((KP - rows, FC), bf)
        acc[...] = jnp.zeros_like(acc)
        a2[...] = jnp.zeros_like(a2)
        transpose_rows(b1, n2t, rows)
        g_in.wait()
        transpose_rows(b2, gt, rows)

        def chunk(j, carry):
            s = lax.rem(j, 2)
            loaded(s)
            after = QUADS + 1 + j
            if comm:
                for n, steps in enumerate(FIRST_STEPS):
                    pl.when(j == n)(functools.partial(tick, *steps))
            red.tick(j - 1, 0)
            for r in range(pairs):
                sl = pair_rows(r)
                h = dot(b1[sl, :], w[s, :, 0:FC]) + b_up[pl.ds(j, 1), :]
                da = dot(b2[sl, :], w[s, :, FC:CW])
                phi = 0.5 * (1.0 + lax.erf(h * 0.7071067811865476))
                slope = phi + h * (jnp.exp(-0.5 * h * h) * 0.3989422804014327)
                a = (h * phi).astype(bf)
                dh = (da * slope).astype(bf)
                act[sl, :] = a
                dhid[sl, :] = dh
                acc[sl, :] += dot(a, w[s, :, FC:CW], NT)
                a2[sl, :] += dot(dh, w[s, :, 0:FC], NT)
                red.tick(j - 1, r + 1)
                if r == 0:
                    if comm:
                        pl.when(after < chunks)(lambda: gather.ready(after))
                    load(jnp.where(after < chunks, after, 0), 1 - s)
                    if comm:
                        for n, steps in enumerate(SECOND_STEPS):
                            pl.when(j == n)(functools.partial(tick, *steps))

            @pl.when(j >= red.SLOTS)
            def _():
                red.release(j - red.SLOTS)

            put(j, 0, dot(n2t[0:512, :], dhid[...]), dot(gt[0:512, :], act[...]))
            red.tick(j - 1, 3)
            left = dot(n2t[512:, :], dhid[...])
            db_up[pl.ds(j, 1), :] = left[512:513]
            put(j, 1, left, dot(gt[512:, :], act[...]))
            return carry

        lax.fori_loop(0, feed, chunk, 0)
        red.tick(feed - 1, 0)
        vg[...] = jnp.zeros_like(vg)

        def last(r, carry):
            sl = block(r)
            middle = a1[sl, :]
            b1[sl, :] = (middle + acc[sl, :] + vec[7:8, :]).astype(bf)
            a1[sl, :] = jnp.zeros_like(middle)
            xhat, inv = norm_parts(middle)
            dn = a2[sl, :]
            cot = b2[sl, :].astype(f32)
            e = dn * vec[5:6, :]
            gm = cot + (e - jnp.mean(e, axis=-1, keepdims=True) - xhat * jnp.mean(e * xhat, axis=-1, keepdims=True)) * inv
            a2[sl, :] = gm
            gb = gm.astype(bf)
            b2[sl, :] = gb
            vg[2:3, :] += jnp.sum(gb.astype(f32), axis=0, keepdims=True)
            vg[3:4, :] += jnp.sum(dn * xhat, axis=0, keepdims=True)
            vg[4:5, :] += jnp.sum(dn, axis=0, keepdims=True)
            vg[5:6, :] += jnp.sum(cot, axis=0, keepdims=True)
            pl.when(r == blocks // 2)(functools.partial(red.tick, feed - 1, 1))
            return carry

        lax.fori_loop(0, blocks, last, 0)
        out_copy().start()

    pl.run_scoped(feed_forward, pltpu.VMEM(normedt_h.shape, bf), pltpu.VMEM((D, KP), bf), pltpu.VMEM((KP, FC), bf),
                  pltpu.VMEM((KP, FC), bf), pltpu.VMEM((rows, D), f32))

    def backward(normedt, gbt, mixed, att, stats, datt, swap, dq, dk, dv, xb, ob):
        n_in = pltpu.make_async_copy(normedt_h, normedt, lsem.at[0])

        def inputs(k, s):
            return (pltpu.make_async_copy(mixed_h.at[k], mixed.at[s, pl.ds(0, rows)], isem.at[s, 0]),
                    pltpu.make_async_copy(att_h.at[k], att.at[s, pl.ds(0, rows)], isem.at[s, 1]),
                    pltpu.make_async_copy(stats_h.at[k], stats.at[s], isem.at[s, 2]))

        for c in inputs(0, 0):
            c.start()
        n_in.start()
        for s in range(2):
            mixed[s, rows:KP, :] = jnp.zeros((KP - rows, 3 * QW), bf)
            att[s, rows:KP, :] = jnp.zeros((KP - rows, QW), bf)
        swap[...] = jnp.where(low_lanes(128) != (iota((128, 128), 0) < 64), 1.0, 0.0).astype(bf)
        transpose_rows(b2, gbt, rows)

        def keep(k, s):
            return pltpu.make_async_copy(mixed.at[s, pl.ds(0, rows)], mixed_h.at[k], isem.at[s, 3])

        def quad(k, carry):
            s = lax.rem(k, 2)
            t = feed + k
            loaded(s)
            for c in inputs(k, s):
                c.wait()

            @pl.when(k > 0)
            def _():
                keep(k - 1, 1 - s).wait()

            @pl.when(k + 1 < QUADS)
            def _():
                load(k + 1, 1 - s)
                for c in inputs(k + 1, 1 - s):
                    c.start()

            def back(r, inner):
                sl = pair_rows(r)
                datt[sl, :] = dot(b2[sl, :], w[s, :, 3 * QW : CW]).astype(bf)
                return inner

            pl.when(k > 0)(lambda: red.tick(t - 1, 0))
            lax.fori_loop(0, pairs, back, 0)

            def hook(i):
                pl.when((i == pairs - 1) & (k > 0))(functools.partial(red.tick, t - 1, 1))
                pl.when(i == 2 * pairs - 1)(functools.partial(red.tick, t - 1, 2))

            attention_backward(pairs, mixed.at[s], att.at[s], stats.at[s], datt, k_feat, swap, dq, dk, dv, hook)
            red.release(t - red.SLOTS)
            pl.when(k == 0)(n_in.wait)
            put(t, 0, dot(normedt[0:512, :], mixed[s]), dot(gbt[0:512, :], att[s]))
            red.tick(t - 1, 3)
            left = dot(normedt[512:, :], mixed[s])
            db_qkv[pl.ds(k, 1), :] = left[512:513]
            put(t, 1, left, dot(gbt[512:, :], att[s]))

            pl.when(k + 1 < QUADS)(lambda: keep(k, s).start())
            return carry

        lax.fori_loop(0, QUADS, quad, 0)
        red.tick(chunks - 1, 0)

        def again(k, s):
            load(k, s)
            inputs(k, s)[0].start()

        again(0, 0)

        def back_in(n, carry):
            s = lax.rem(n + 1, 2)

            @pl.when(n > 0)
            def _():
                loaded(s)
                inputs(n - 1, s)[0].wait()

            for r in range(pairs):
                sl = pl.ds(r * PAIR, PAIR)
                a1[sl, :] += dot(mixed[s, sl, :], w[s, :, 0 : 3 * QW], NT)

            pl.when(n + 2 < QUADS)(lambda: again(n + 1, s))

            if comm:
                for m, (j, i) in enumerate(((0, 1), (0, 2), (0, 3), (1, 0))):
                    pl.when(n == m)(functools.partial(red.tick, chunks - 1 + j, i))
            return carry

        lax.fori_loop(0, QUADS, back_in, 0)
        ring = xb.shape[0]

        def xcopy(r):
            s = lax.rem(r, ring)
            return pltpu.make_async_copy(x_h.at[block(r)], xb.at[s], xsem.at[s])

        def tcopy(r):
            s = lax.rem(r, 2)
            return pltpu.make_async_copy(ob.at[s], gt_h.at[block(r)], tsem.at[s])

        for r in range(ring):
            xcopy(r).start()

        def last(r, carry):
            xcopy(r).wait()
            pl.when(r >= 2)(lambda: tcopy(r - 2).wait())
            xhat, inv = norm_parts(xb[lax.rem(r, ring)])
            dn = a1[block(r), :]
            e = dn * vec[0:1, :]
            total = a2[block(r), :] + (e - jnp.mean(e, axis=-1, keepdims=True) - xhat * jnp.mean(e * xhat, axis=-1, keepdims=True)) * inv
            ob[lax.rem(r, 2)] = total.astype(bf)
            tcopy(r).start()
            vg[0:1, :] += jnp.sum(dn * xhat, axis=0, keepdims=True)
            vg[1:2, :] += jnp.sum(dn, axis=0, keepdims=True)
            pl.when(r + ring < blocks)(lambda: xcopy(r + ring).start())
            if comm:
                for at_r, steps in ((0, ((1, 1),)), (2, ((1, 2),)), (4, ((1, 3),)), (7, ((2, 0),)), (13, ((2, 1), (2, 2)))):
                    for j, i in steps:
                        pl.when(r == at_r)(functools.partial(red.tick, chunks - 1 + j, i))
            return carry

        lax.fori_loop(0, blocks, last, 0)
        out_copy().wait()
        if comm:
            share = Small(at, *small_refs[:7], sums_out, *small_refs[7:])
            sums = share.sums
            sums[...] = jnp.zeros_like(sums)
            for f in range(8):
                lanes = slice(128 * f, 128 * (f + 1))
                q, half = slice(f // 2, f // 2 + 1), 128 * (f % 2)
                rows_of = [vg[0:1, lanes], vg[1:2, lanes], db_qkv[q, half : half + 128],
                           db_qkv[q, 2 * QW + half : 2 * QW + half + 128]] + [vg[n : n + 1, lanes] for n in (2, 3, 4, 5)]
                rows_of += [db_up[f : f + 1, 128 * i : 128 * (i + 1)] for i in range(4)]
                for i, row in enumerate(rows_of):
                    sums[f // 2, f % 2, i : i + 1, :] = row
            for n, k in enumerate(range(11, 17)):
                red.tick(chunks - 1 + k // 4, k % 4)
                share.step(n)
            for k in range(chunks):
                gather.finish(k)
        for r in (blocks - 2, blocks - 1):
            tcopy(r).wait()
        for t in range(chunks - red.SLOTS, chunks):
            red.release(t)

    pl.run_scoped(backward, pltpu.VMEM(normedt_h.shape, bf), pltpu.VMEM((D, KP), bf), pltpu.VMEM((2, KP, 3 * QW), bf),
                  pltpu.VMEM((2, KP, QW), bf), pltpu.VMEM((2, rows, QW), bf), pltpu.VMEM((rows, QW), bf), pltpu.VMEM((128, 128), bf), pltpu.VMEM((PAIR, 128), f32),
                  pltpu.VMEM((PAIR, 128), f32), pltpu.VMEM((PAIR, 128), f32), pltpu.VMEM((3, RB, D), f32),
                  pltpu.VMEM((2, RB, D), bf))


def layer(rows, comm, chunks, *args):
    A, V = any_spec(), vmem_spec()
    KP = -(-rows // 256) * 256
    sums = ((8, D), (QUADS, 3 * QW), (chunks - QUADS, FC))
    kept = [sds((rows, D), f32), sds((D + 16, KP), bf), sds((QUADS, rows, 3 * QW), bf), sds((QUADS, rows, QW), bf),
            sds((QUADS, rows, QW), bf)]
    first = [sds((rows, D), bf), sds((rows, D), bf), sds((chunks, 128, CW) if comm else (chunks, 4, 256, CW), bf)]
    scratch = [
        pltpu.VMEM((rows, D), f32), pltpu.VMEM((rows, D), f32), pltpu.VMEM((rows, D), bf), pltpu.VMEM((rows, D), bf),
        pltpu.VMEM((2, D, CW), bf), pltpu.VMEM((rows, 128), bf), pltpu.VMEM((rows, 128), bf), pltpu.VMEM((8, D), f32),
        pltpu.VMEM((chunks - QUADS, FC), f32),
        pltpu.SemaphoreType.DMA((2,)), pltpu.SemaphoreType.DMA((2,)), pltpu.SemaphoreType.DMA((5,)),
        pltpu.SemaphoreType.DMA((2, 4)), pltpu.SemaphoreType.DMA((3,)), pltpu.SemaphoreType.DMA((2,)),
    ]
    if comm:
        in_specs = [A, A, V, V, V, V, A]
        out_shape = first + [sds((16, 128), f32)] + kept + [sds((chunks, 4, 256, CW), bf)]
        out_specs = [A, A, A, V] + [A] * 6
        scratch += [pltpu.VMEM(shape, f32) for shape in sums] + [
            pltpu.VMEM((8, 16, 128), bf), pltpu.SemaphoreType.DMA((4,)), pltpu.SemaphoreType.DMA((chunks,)),
            pltpu.SemaphoreType.DMA((chunks, 6))] + Small.scratch() + Reduce.scratch(chunks)
        params = pltpu.CompilerParams(vmem_limit_bytes=VMEM_LIMIT, collective_id=0, has_side_effects=True)
    else:
        in_specs = [A, A, V, V, V, V, V, A]
        out_shape = first + [sds(shape, f32) for shape in sums] + kept
        out_specs = [A, A, A, V, V, V] + [A] * 5
        scratch += Keep.scratch(chunks)
        params = pltpu.CompilerParams(vmem_limit_bytes=VMEM_LIMIT)
    return pl.pallas_call(
        functools.partial(layer_kernel, rows, comm), out_shape=out_shape, in_specs=in_specs, out_specs=out_specs,
        scratch_shapes=scratch, compiler_params=params, name="encoder_layer",
    )(*args)


def prepare_kernel(units, band, gsd, freq, qkv, out, up, down, shard, tab, q_table, k_table):
    for k in range(QUADS):
        for i in range(3):
            shard[k, :, QW * i : QW * (i + 1)] = qkv[:, D * i + QW * k : D * i + QW * (k + 1)]
        shard[k, :, 3 * QW : CW] = out[QW * k : QW * (k + 1), :].T
    for j in range(up.shape[1] // FC):
        shard[QUADS + j, :, 0:FC] = up[:, FC * j : FC * (j + 1)]
        shard[QUADS + j, :, FC:CW] = down[FC * j : FC * (j + 1), :].T
    entry = iota((tab.shape[1], 128), 0)
    unit = lax.shift_right_logical(entry * 9363, 16)
    level = jnp.zeros(entry.shape, jnp.int32)
    row = iota((128, 128), 0)
    item = jnp.full((128, 128), -100, jnp.int32)
    label = jnp.int32(0)
    for u in range(units):
        if u % UNITS_MB == 0:
            label = jnp.int32(-1 + UNITS_MB * (u // UNITS_MB % 2))
        label = label + jnp.where(band[u] <= 1, 1, 0)
        item = jnp.where(row == u, label, item)
        level = jnp.where(unit == u, gsd[u], level)
    place = (entry - GRID * unit).astype(f32) * jnp.exp2((level.astype(f32) - 3.0) * 0.5)
    angle = jnp.concatenate([place, place], axis=1) * freq[...]
    wave = jnp.concatenate([jnp.sin(angle), jnp.cos(angle)], axis=1)
    wave = jnp.where(iota(wave.shape, 0) < GRID * units, wave, 0.0)
    high = wave.astype(bf)
    rest = wave - high.astype(f32)
    middle = rest.astype(bf)
    tab[0] = high
    tab[1] = middle
    tab[2] = (rest - middle.astype(f32)).astype(bf)
    slot = (iota((128, 128), 1) & 63) - 3
    used = (slot >= 0) & (slot < 2 * UNITS_MB)
    real = row < units
    q_table[...] = jnp.where(real & (item == slot), 1.0, 0.0).astype(bf)
    k_table[...] = jnp.where(real, jnp.where(used & (item != slot), NEG, jnp.where(slot < 0, 1.0, 0.0)), 0.0).astype(bf)


def prepare(rows, band_code, gsd_code, qkv, out, up, down):
    units = rows // UNIT
    n = qkv.shape[0]
    places = -(-GRID * units // 256) * 256
    quarter = D // 4
    freq = np.exp2(np.arange(quarter, dtype=np.float32) * np.float32(-math.log2(10000.0) / quarter)).astype(np.float32)
    V, S = vmem_spec(), pl.BlockSpec(memory_space=pltpu.SMEM)
    return pl.pallas_call(
        functools.partial(prepare_kernel, units),
        out_shape=(sds((QUADS + up.shape[1] // FC, n, CW), bf), sds((3, places, 2 * quarter), bf), sds((128, 128), bf),
                   sds((128, 128), bf)),
        in_specs=[S, S, V, V, V, V, V], out_specs=(V, V, V, V),
        compiler_params=pltpu.CompilerParams(vmem_limit_bytes=VMEM_LIMIT), name="prepare",
    )(band_code, gsd_code, jnp.asarray(freq)[None, :], qkv, out, up, down)


def results_kernel(rows, out_i, gt_i, gw_i, sums, out_h, gt_h, dg1, db1, g_qkv, dbq, dbv, g_out, dbo, dg2, db2, g_up, db_up, g_down,
                   db_down, out_v, gt_v, gt_f, gw, qkv_v, o_v, up_v, down_v, sem_in, sem_out):
    loads = [pltpu.make_async_copy(src, dst, sem_in.at[i])
             for i, (src, dst) in enumerate(((gw_i, gw), (out_i, out_v), (gt_i, gt_v)))]
    stores = [pltpu.make_async_copy(src, dst, sem_out.at[i])
              for i, (src, dst) in enumerate(((out_v, out_h), (gt_f, gt_h), (qkv_v, g_qkv), (o_v, g_out), (up_v, g_up), (down_v, g_down)))]
    for c in loads:
        c.start()
    for i, ref in enumerate((dg1, db1, dbq, dbv, dbo, dg2, db2, db_down)):
        ref[...] = sums[i]
    for i in range(4):
        db_up[128 * i : 128 * (i + 1)] = sums[8 + i]
    loads[0].wait()
    feed = gw.shape[0] - QUADS
    for k in range(QUADS):
        for i in range(3):
            qkv_v[:, D * i + QW * k : D * i + QW * (k + 1)] = gw[feed + k, :, QW * i : QW * (i + 1)].astype(f32)
        o_v[QW * k : QW * (k + 1), :] = gw[feed + k, :, 3 * QW : CW].T.astype(f32)
    stores[2].start()
    stores[3].start()
    loads[1].wait()
    stores[0].start()
    for j in range(feed):
        up_v[:, FC * j : FC * (j + 1)] = gw[j, :, 0:FC].astype(f32)
        down_v[FC * j : FC * (j + 1), :] = gw[j, :, FC:CW].T.astype(f32)
    stores[4].start()
    stores[5].start()
    loads[2].wait()
    RB = PAIR // 7

    def widen(r, carry):
        sl = pl.ds(pl.multiple_of(r * RB, 16), RB)
        gt_f[sl, :] = gt_v[sl, :].astype(f32)
        return carry

    lax.fori_loop(0, rows // RB, widen, 0)
    stores[1].start()
    for c in stores:
        c.wait()


def results(out, gt, gw, sums):
    rows, chunks = out.shape[0], gw.shape[0]
    hidden = (chunks - QUADS) * FC
    A, V = any_spec(), vmem_spec()
    vec = sds((128,), f32)
    wide = [sds((128, 3 * D), f32), sds((D, 128), f32), sds((128, hidden), f32), sds((hidden, 128), f32)]
    return pl.pallas_call(
        functools.partial(results_kernel, rows),
        out_shape=(sds((rows, D), bf), sds((rows, D), f32), vec, vec, wide[0], vec, vec, wide[1], vec, vec, vec, wide[2],
                   sds((512,), f32), wide[3], vec),
        in_specs=[A, A, A, V], out_specs=(A, A, V, V, A, V, V, A, V, V, V, A, V, A, V),
        scratch_shapes=[pltpu.VMEM((rows, D), bf), pltpu.VMEM((rows, D), bf), pltpu.VMEM((rows, D), f32), pltpu.VMEM(gw.shape, bf)]
        + [pltpu.VMEM(v.shape, f32) for v in wide] + [pltpu.SemaphoreType.DMA((3,)), pltpu.SemaphoreType.DMA((6,))],
        compiler_params=pltpu.CompilerParams(vmem_limit_bytes=VMEM_LIMIT), name="results",
    )(out, gt, gw, sums)


def local(dp, fsdp, tokens, band_code, gsd_code, norm1_gain, norm1_bias, qkv_weight, bias_q, bias_v, out_weight, bias_out,
          norm2_gain, norm2_bias, up_weight, bias_up, down_weight, bias_down, grad_out):
    rows = tokens.shape[0]
    comm = dp == 4 and fsdp == 8
    shard, *tables = prepare(rows, band_code, gsd_code, qkv_weight, out_weight, up_weight, down_weight)
    chunks, n, _ = shard.shape
    vectors = (norm1_gain, norm1_bias, bias_q, bias_v, bias_out, norm2_gain, norm2_bias, bias_down)
    args = (tokens, grad_out, *tables)
    if comm:
        small = jnp.concatenate([jnp.stack(vectors), bias_up.reshape(4, 128), jnp.zeros((4, 128), bf)])
        out, grad_tokens, gw, sg, *_ = layer(rows, True, chunks, *args, small, shard)
        return results(out, grad_tokens, gw, sg)
    else:
        gathered = lax.all_gather(jnp.stack(vectors), "fsdp", axis=1, tiled=True).astype(f32)
        up_bias = lax.all_gather(bias_up, "fsdp", axis=0, tiled=True).astype(f32).reshape(-1, FC)
        whole = lax.all_gather(shard, "fsdp", axis=1, tiled=True)
        out, grad_tokens, gw, vg, db_qkv, db_up, *_ = layer(rows, False, chunks, *args, gathered, up_bias, whole)
        sg = jnp.concatenate([vg[0:2], db_qkv[:, 0:QW].reshape(1, D), db_qkv[:, 2 * QW :].reshape(1, D), vg[2:6]], axis=0)
        sg = jnp.concatenate([sg.reshape(8, fsdp, n).transpose(1, 0, 2).reshape(fsdp, 8 * n), db_up.reshape(fsdp, 4 * n)], axis=1)
        sg = lax.psum(lax.psum_scatter(sg, "fsdp", scatter_dimension=0, tiled=True), "dp").reshape(12, n)
        gw = lax.psum(lax.psum_scatter(gw.reshape(chunks, D, CW), "fsdp", scatter_dimension=1, tiled=True), "dp")
    gw = gw.astype(f32)
    g_ff, g_att = gw[: chunks - QUADS], gw[chunks - QUADS :]
    g_qkv = g_att[:, :, : 3 * QW].reshape(QUADS, n, 3, QW).transpose(1, 2, 0, 3).reshape(n, 3 * D)
    g_out = g_att[:, :, 3 * QW :].transpose(0, 2, 1).reshape(D, n)
    g_up = g_ff[:, :, :FC].transpose(1, 0, 2).reshape(n, -1)
    g_down = g_ff[:, :, FC:].transpose(0, 2, 1).reshape(-1, n)
    grad_tokens = grad_tokens.astype(f32)
    return (out, grad_tokens, sg[0], sg[1], g_qkv, sg[2], sg[3], g_out, sg[4], sg[5], sg[6], g_up, sg[8:12].reshape(4 * n), g_down, sg[7])


def solution(mesh):
    rows, vec, first, second = P(("dp", "fsdp"), None), P("fsdp"), P("fsdp", None), P(None, "fsdp")
    codes = P(("dp", "fsdp"))
    return jax.shard_map(
        functools.partial(local, mesh.shape["dp"], mesh.shape["fsdp"]),
        mesh=mesh,
        in_specs=(rows, codes, codes, vec, vec, first, vec, vec, second, vec, vec, vec, first, vec, second, vec, rows),
        out_specs=(rows, rows, vec, vec, first, vec, vec, second, vec, vec, vec, first, vec, second, vec),
        check_vma=False,
    )
```

```python
import functools
import math

import jax
import jax.numpy as jnp
import numpy as np
from jax import lax
from jax.experimental import pallas as pl
from jax.experimental.pallas import tpu as pltpu
from jax.sharding import PartitionSpec as P

bf = jnp.bfloat16
f32 = jnp.float32
NN = (((1,), (0,)), ((), ()))
NT = (((1,), (1,)), ((), ()))
TN = (((0,), (0,)), ((), ()))
D = 1024
HEADS = 16
HEAD_DIM = 64
GRID = 7
UNIT = GRID * GRID
UNITS_MB = 8
BUF = UNIT * UNITS_MB
PAIR = 2 * BUF
QUADS = 4
QW = 256
FC = 512
CW = 1024
EPS = 1e-6
SCALE = 0.125
NEG = -1e30
VMEM_LIMIT = 62 << 20
KEYS = 384
WINDOWS = ((0, ((0, 192, 0), (192, 208, 16))), (384, ((0, 192, 0), (192, 208, 16))))
SPAN = 400


def dot(a, b, dims=NN):
    return lax.dot_general(a, b, dims, preferred_element_type=f32)


def any_spec():
    return pl.BlockSpec(memory_space=pl.ANY)


def vmem_spec():
    return pl.BlockSpec(memory_space=pltpu.VMEM)


def sds(shape, kind):
    return jax.ShapeDtypeStruct(shape, kind)


def norm_parts(v):
    center = v - jnp.mean(v, axis=-1, keepdims=True)
    inv = lax.rsqrt(jnp.mean(center * center, axis=-1, keepdims=True) + EPS)
    return center * inv, inv


def low_lanes(rows):
    return lax.broadcasted_iota(jnp.int32, (rows, 128), 1) < 64


def split_terms(v):
    lane = lax.broadcasted_iota(jnp.int32, v.shape, 1) & 63
    hi = v.astype(bf).astype(f32)
    rest = v - hi
    mid = rest.astype(bf).astype(f32)
    return jnp.where(lane == 0, hi, jnp.where(lane == 1, mid, jnp.where(lane == 2, rest - mid, 0.0))), lane < 3


def attention_forward(pairs, mixed, q_feat, k_feat, attended, stats, hook):
    def one(i, carry):
        p, hp = i // 2, lax.rem(i, 2)
        base = pl.multiple_of(p * PAIR, 16)
        lane0 = pl.multiple_of(hp * 128, 128)
        blocks = [(w, n, start, *half) for w, (start, halves) in enumerate(WINDOWS) for n, half in enumerate(halves)]
        spans = {}

        def window(w, start):
            if w not in spans:
                span = pl.ds(pl.multiple_of(base + start, 16), SPAN)
                k2 = mixed[span, pl.ds(pl.multiple_of(lane0 + QW, 128), 128)]
                v2 = mixed[span, pl.ds(pl.multiple_of(lane0 + 2 * QW, 128), 128)]
                kf = k_feat[span, :]
                low = low_lanes(SPAN)
                ones = jnp.ones_like(v2)
                spans[w] = ((jnp.where(low, k2, kf), jnp.where(low, kf, k2)), (jnp.where(low, v2, ones), jnp.where(low, ones, v2)))
            return spans[w]

        def scores(block):
            w, n, start, q0, qn, k0 = block
            keys, _ = window(w, start)
            rows = pl.ds(pl.multiple_of(base + start + q0, 16), qn)
            q2 = mixed[rows, pl.ds(lane0, 128)] * jnp.asarray(SCALE, bf)
            qf = q_feat[rows, :]
            low = low_lanes(qn)
            return [dot(q, keys[h][k0 : k0 + KEYS], NT) for h, q in enumerate((jnp.where(low, q2, qf), jnp.where(low, qf, q2)))]

        tail = None
        ahead = scores(blocks[0])
        for b, (w, n, start, q0, qn, k0) in enumerate(blocks):
            now = ahead
            if b + 1 < len(blocks):
                ahead = scores(blocks[b + 1])
            _, values = window(w, start)
            rows = pl.ds(pl.multiple_of(base + start + q0, 16), qn)
            low = low_lanes(qn)
            tops = [jnp.max(s, axis=-1, keepdims=True) for s in now]
            outs = [dot(jnp.exp(s - m).astype(bf), values[h][k0 : k0 + KEYS]) for h, (s, m) in enumerate(zip(now, tops))]
            total = jnp.where(low, outs[1], outs[0])
            out = jnp.where(low, outs[0], outs[1]) / pltpu.roll(total, 64, 1)
            terms, at = split_terms(-(jnp.where(low, tops[1], tops[0]) + jnp.log(total)))
            stat = jnp.where(at, terms, q_feat[rows, :].astype(f32))
            if w == 0 and n == 1:
                tail = (out[qn - 16 :], stat[qn - 16 :])
            if w == 1 and n == 0:
                first = lax.broadcasted_iota(jnp.int32, (16, 128), 0) < 8
                out = jnp.concatenate([jnp.where(first, tail[0], out[0:16]), out[16:]], axis=0)
                stat = jnp.concatenate([jnp.where(first, tail[1], stat[0:16]), stat[16:]], axis=0)
            attended[rows, pl.ds(lane0, 128)] = out.astype(bf)
            stats[rows, pl.ds(lane0, 128)] = stat.astype(bf)
        hook(i)
        return carry

    lax.fori_loop(0, pairs * 2, one, 0)


def attention_backward(pairs, mixed, att, stats, datt, k_feat, swap, dq, dk, dv, hook):
    def one(i, carry):
        p, hp = i // 2, lax.rem(i, 2)
        base = pl.multiple_of(p * PAIR, 16)
        lane0 = pl.multiple_of(hp * 128, 128)
        lanes = pl.ds(lane0, 128)
        dq[...] = jnp.zeros_like(dq)
        dk[...] = jnp.zeros_like(dk)
        dv[...] = jnp.zeros_like(dv)
        blocks = [(w, n, start, *half) for w, (start, halves) in enumerate(WINDOWS) for n, half in enumerate(halves)]
        spans = {}

        def window(w, start):
            if w not in spans:
                span = pl.ds(pl.multiple_of(base + start, 16), SPAN)
                k2 = mixed[span, pl.ds(pl.multiple_of(lane0 + QW, 128), 128)]
                v2 = mixed[span, pl.ds(pl.multiple_of(lane0 + 2 * QW, 128), 128)]
                kf = k_feat[span, :]
                low = low_lanes(SPAN)
                zero = jnp.zeros_like(k2)
                terms = (lax.broadcasted_iota(jnp.int32, (SPAN, 128), 1) & 63) < 3
                vf = jnp.where(terms, jnp.ones_like(v2), zero)
                spans[w] = ((jnp.where(low, k2, kf), jnp.where(low, kf, k2)), (jnp.where(low, k2, zero), jnp.where(low, zero, k2)),
                            (jnp.where(low, v2, vf), jnp.where(low, vf, v2)))
            return spans[w]

        def products(block):
            w, n, start, q0, qn, k0 = block
            keys, _, values = window(w, start)
            rows = pl.ds(pl.multiple_of(base + start + q0, 16), qn)
            q2 = mixed[rows, lanes] * jnp.asarray(SCALE, bf)
            do2 = datt[rows, lanes]
            if w != n:
                r = lax.broadcasted_iota(jnp.int32, (qn, 128), 0)
                mine = r < qn - 8 if n == 1 else r >= 8
                do2 = jnp.where(mine, do2, jnp.zeros_like(do2))
            qf = stats[rows, lanes]
            low = low_lanes(qn)
            zero = jnp.zeros_like(q2)
            prod = do2.astype(f32) * att[rows, lanes].astype(f32)
            hi = prod.astype(bf)
            inner = dot(hi, swap[...]) + dot((prod - hi.astype(f32)).astype(bf), swap[...])
            df = split_terms(-inner)[0].astype(bf)
            kk = slice(k0, k0 + KEYS)
            heads = []
            for h in range(2):
                pick = (lambda a, b: jnp.where(low, a, b)) if h == 0 else (lambda a, b: jnp.where(low, b, a))
                heads.append((dot(pick(q2, qf), keys[h][kk], NT), dot(pick(do2, df), values[h][kk], NT), pick(do2, zero), pick(q2, zero)))
            return heads

        ahead = products(blocks[0])
        for b, (w, n, start, q0, qn, k0) in enumerate(blocks):
            now = ahead
            if b + 1 < len(blocks):
                ahead = products(blocks[b + 1])
            plain = window(w, start)[1]
            at, kat = start + q0, start + k0
            pieces = []
            for h, (s, slope, o, q) in enumerate(now):
                probs = jnp.exp(s)
                pieces.append((probs.astype(bf), (probs * slope).astype(bf), o, q, plain[h][k0 : k0 + KEYS]))
            (pa, sa, oa, qa, ka), (pb, sb, ob, qb, kb) = pieces
            dv[kat : kat + KEYS, :] += dot(pa, oa, TN) + dot(pb, ob, TN)
            dk[kat : kat + KEYS, :] += dot(sa, qa, TN) + dot(sb, qb, TN)
            dq[at : at + qn, :] += dot(sa, ka) + dot(sb, kb)
        rows = pl.ds(base, PAIR)
        mixed[rows, lanes] = (dq[...] * SCALE).astype(bf)
        mixed[rows, pl.ds(pl.multiple_of(lane0 + QW, 128), 128)] = dk[...].astype(bf)
        mixed[rows, pl.ds(pl.multiple_of(lane0 + 2 * QW, 128), 128)] = dv[...].astype(bf)
        hook(i)
        return carry

    lax.fori_loop(0, pairs * 2, one, 0)


MESH = pl.DeviceIdType.MESH


class Place:
    def __init__(self):
        self.d = lax.axis_index("dp")
        self.f = lax.axis_index("fsdp")
        self.z = lax.div(self.f, 2)
        self.c = lax.rem(self.f, 2)
        self.dx = self.d + 1 - 2 * lax.rem(self.d, 2)
        self.dy = lax.rem(self.d + 2, 4)
        self.dd = 3 - self.d
        self.sib = self.f + 1 - 2 * self.c
        self.zs = [lax.rem(self.z + n, 4) for n in (1, 2, 3)]
        self.x_dev = (self.dx, self.f)
        self.y_dev = (self.dy, self.f)
        self.sib_dev = (self.d, self.sib)
        self.z_devs = [(self.d, 2 * zz + self.c) for zz in self.zs]

    def barrier(self):
        sem = pltpu.get_barrier_semaphore()
        for dev in [self.x_dev, self.y_dev, self.sib_dev] + self.z_devs:
            pl.semaphore_signal(sem, inc=1, device_id=dev, device_id_type=MESH)
        pl.semaphore_wait(sem, 6)


def remote(src, dst, send, recv, dev):
    return pltpu.make_async_remote_copy(src, dst, send, recv, device_id=dev, device_id_type=MESH)


class Gather:
    def __init__(self, at, shard, whole, send, recv):
        self.at, self.shard, self.whole, self.send, self.recv = at, shard, whole, send, recv
        self.chunks = whole.shape[0]

    def cols(self, k):
        return pl.ds(0, 3 * QW if isinstance(k, int) and k < QUADS else CW)

    def rows(self, q, first, count):
        return pl.ds(pl.multiple_of(self.at.c * 128 + 32 * q + first, 16), count)

    def push(self, k, planes, rows, stage, dev, src=None):
        dst = self.whole.at[k, planes, rows, self.cols(k)]
        remote(dst if src is None else src, dst, self.send.at[k], self.recv.at[k, stage], dev).start()

    def landed(self, k, stage, planes, rows):
        part = self.whole.at[k, pl.ds(0, planes), pl.ds(0, rows), self.cols(k)]
        remote(part, part, self.send.at[k], self.recv.at[k, stage], self.at.x_dev).wait_recv()

    def begin(self, k):
        at = self.at
        quarter = self.shard.at[k, pl.ds(pl.multiple_of(32 * at.d, 16), 32), self.cols(k)]
        for n, dev in enumerate(at.z_devs):
            self.push(k, 3 - n, self.rows(at.d, 0, 32), 0, dev, quarter)
        self.push(k, 0, self.rows(0, 0, 128), 5, at.sib_dev, self.shard.at[k, :, self.cols(k)])

    def spread(self, k):
        at = self.at
        self.landed(k, 0, 3, 32)
        self.push(k, pl.ds(1, 3), self.rows(at.d, 0, 32), 1, at.x_dev)
        self.push(k, pl.ds(1, 3), self.rows(at.d, 0, 32), 2, at.y_dev)

    def diagonal(self, k):
        at = self.at
        self.landed(k, 1, 3, 32)
        self.landed(k, 2, 3, 32)
        self.push(k, pl.ds(1, 3), self.rows(at.dx, 0, 16), 3, at.y_dev)
        self.push(k, pl.ds(1, 3), self.rows(at.dy, 16, 16), 4, at.x_dev)

    def pair(self, k):
        self.landed(k, 3, 3, 16)
        self.landed(k, 4, 3, 16)
        self.push(k, pl.ds(1, 3), self.rows(0, 0, 128), 5, self.at.sib_dev)

    def ready(self, k):
        self.landed(k, 5, 4, 128)

    def load(self, k, cols, dst, sem):
        at = self.at
        own = pl.multiple_of(at.z * 256 + at.c * 128, 128)
        other = pl.multiple_of((1 - at.c) * 128, 128)
        pltpu.make_async_copy(self.shard.at[k, :, cols], dst.at[pl.ds(own, 128)], sem).start()
        pltpu.make_async_copy(self.whole.at[k, 0, pl.ds(other, 128), cols], dst.at[pl.ds(at.z * 256 + other, 128)], sem).start()
        for n, zz in enumerate(at.zs):
            pltpu.make_async_copy(self.whole.at[k, n + 1, :, cols], dst.at[pl.ds(pl.multiple_of(zz * 256, 256), 256)], sem).start()

    def run(self, *steps):
        for step, k in steps:
            if step == "s":
                if k + 3 < self.chunks:
                    self.begin(k + 3)
                self.spread(k)
            elif step == "d":
                self.diagonal(k)
            else:
                self.pair(k)

    def finish(self, k):
        part = self.whole.at[k, :, pl.ds(0, 224), self.cols(k)]
        remote(part, part, self.send.at[k], self.recv.at[k, 0], self.at.x_dev).wait_send()


def spread_vectors(shards, vec, b_up):
    n = vec.shape[1] // 128
    for f in range(n):
        vec[:, 128 * f : 128 * (f + 1)] = shards[f, 0:8, :].astype(f32)
        for i in range(4):
            b_up[f : f + 1, 128 * i : 128 * (i + 1)] = shards[f, 8 + i : 9 + i, :].astype(f32)


class Reduce:
    SLOTS = 3
    STEPS = ((16, "done"), (13, "share"), (10, "total"), (8, "planes"), (5, "relay"), (1, "cross"), (0, "pair"))

    def __init__(self, at, count, gp, r1, rx, ry, rz, fin, out, send, recv, osem, sizes):
        self.at, self.count, self.gp, self.r1, self.rx, self.ry, self.rz = at, count, gp, r1, rx, ry, rz
        self.fin, self.out, self.send, self.recv, self.osem, self.sizes = fin, out, send, recv, osem, sizes

    @classmethod
    def scratch(cls, count):
        s = cls.SLOTS
        return [pltpu.VMEM((s, 4, 256, CW), bf), pltpu.VMEM((2, 4, 128, CW), bf), pltpu.VMEM((s, 3, 4, 16, CW), bf),
                pltpu.VMEM((s, 3, 4, 16, CW), bf), pltpu.VMEM((s, 3, 32, CW), bf), pltpu.VMEM((count, 32, CW), bf),
                pltpu.SemaphoreType.DMA((count, 3)), pltpu.SemaphoreType.DMA((count, 6)), pltpu.SemaphoreType.DMA((count,))]

    def slot(self, t):
        return lax.rem(t, self.SLOTS)

    def rows(self, q, first, count):
        return pl.ds(pl.multiple_of(self.at.c * 128 + q * 32 + first, 16), count)

    def push(self, t, src, dst, stage, dev, group=0):
        remote(src, dst, self.send.at[t, group], self.recv.at[t, stage], dev).start()

    def landed(self, t, stage, rows):
        part = self.part(rows)
        remote(part, part, self.send.at[t, 0], self.recv.at[t, stage], self.at.x_dev).wait_recv()

    def part(self, rows):
        planes = 1 if rows <= 256 else 4
        return self.sizes.at[0, pl.ds(0, planes), pl.ds(0, rows // planes)]

    def left(self, t, group, rows):
        part = self.part(rows)
        remote(part, part, self.send.at[t, group], self.recv.at[t, 0], self.at.x_dev).wait_send()

    def add(self, t, q, first, *parts):
        s, sl = self.slot(t), self.rows(q, first, 16)
        total = self.gp[s, :, sl, :].astype(f32)
        for p in parts:
            total = total + p.astype(f32)
        self.gp[s, :, sl, :] = total.astype(bf)

    def pair(self, t):
        s = self.slot(t)
        other = pl.ds(pl.multiple_of((1 - self.at.c) * 128, 128), 128)
        self.push(t, self.gp.at[s, :, other], self.r1.at[lax.rem(t, 2)], 0, self.at.sib_dev)

    def cross(self, t):
        at, s = self.at, self.slot(t)
        self.landed(t, 0, 512)
        own = pl.ds(pl.multiple_of(at.c * 128, 128), 128)

        def plane(zz, carry):
            self.gp[s, zz, own, :] = (self.gp[s, zz, own, :].astype(f32) + self.r1[lax.rem(t, 2), zz].astype(f32)).astype(bf)
            return carry

        lax.fori_loop(0, 4, plane, 0)
        gp = self.gp
        self.push(t, gp.at[s, :, self.rows(at.dd, 0, 16)], self.rx.at[s, 0], 1, at.x_dev)
        self.push(t, gp.at[s, :, self.rows(at.dd, 16, 16)], self.ry.at[s, 0], 1, at.y_dev)
        self.push(t, gp.at[s, :, self.rows(at.dx, 0, 16)], self.rx.at[s, 1], 2, at.x_dev)
        self.push(t, gp.at[s, :, self.rows(at.dy, 16, 16)], self.ry.at[s, 1], 2, at.y_dev)

    def relay(self, t):
        at, s = self.at, self.slot(t)
        self.landed(t, 1, 128)
        self.add(t, at.dy, 0, self.rx[s, 0])
        self.add(t, at.dx, 16, self.ry[s, 0])
        self.push(t, self.gp.at[s, :, self.rows(at.dy, 0, 16)], self.ry.at[s, 2], 2, at.y_dev)
        self.push(t, self.gp.at[s, :, self.rows(at.dx, 16, 16)], self.rx.at[s, 2], 2, at.x_dev)

    def planes(self, t):
        at, s = self.at, self.slot(t)
        self.landed(t, 2, 256)
        self.add(t, at.d, 0, self.rx[s, 1], self.ry[s, 2])
        self.add(t, at.d, 16, self.ry[s, 1], self.rx[s, 2])
        for n, (zz, dev) in enumerate(zip(at.zs, at.z_devs)):
            self.push(t, self.gp.at[s, zz, self.rows(at.d, 0, 32)], self.rz.at[s, n], 3, dev, 2)

    def quarter(self, t, q, first=0, count=32):
        return self.out.at[t, pl.ds(pl.multiple_of(q * 32 + first, 16), count)]

    def total(self, t):
        at, s = self.at, self.slot(t)
        self.landed(t, 3, 96)
        total = self.gp[s, at.z, self.rows(at.d, 0, 32), :].astype(f32)
        for n in range(3):
            total = total + self.rz[s, n].astype(f32)
        self.fin[t] = total.astype(bf)
        pltpu.make_async_copy(self.fin.at[t], self.quarter(t, at.d), self.osem.at[t]).start()
        self.push(t, self.fin.at[t], self.quarter(t, at.d), 4, at.x_dev, 1)
        self.push(t, self.fin.at[t], self.quarter(t, at.d), 4, at.y_dev, 1)

    def share(self, t):
        at = self.at
        self.landed(t, 4, 64)
        self.push(t, self.quarter(t, at.dx, 0, 16), self.quarter(t, at.dx, 0, 16), 5, at.y_dev, 1)
        self.push(t, self.quarter(t, at.dy, 16, 16), self.quarter(t, at.dy, 16, 16), 5, at.x_dev, 1)

    def done(self, t):
        self.landed(t, 5, 32)
        self.left(t, 1, 96)
        pltpu.make_async_copy(self.fin.at[t], self.quarter(t, self.at.d), self.osem.at[t]).wait()

    def release(self, t):
        self.left(t, 0, 896)
        self.left(t, 2, 96)

    def tick(self, j, i):
        for offset, name in self.STEPS:
            if offset % 4 == i:
                t = j - offset // 4
                if isinstance(t, int):
                    if 0 <= t < self.count:
                        getattr(self, name)(t)
                else:
                    pl.when((t >= 0) & (t < self.count))(functools.partial(getattr(self, name), t))

    def drain(self, j, i, last):
        for k in range(4 * j + i, 4 * (last + 3) + 1):
            self.tick(k // 4, k % 4)


class Keep:
    SLOTS = 3

    def __init__(self, count, gp, out, sem):
        self.count, self.gp, self.out, self.sem = count, gp, out, sem

    @classmethod
    def scratch(cls, count):
        return [pltpu.VMEM((cls.SLOTS, 4, 256, CW), bf), pltpu.SemaphoreType.DMA((count,))]

    def slot(self, t):
        return lax.rem(t, self.SLOTS)

    def copy(self, t):
        return pltpu.make_async_copy(self.gp.at[self.slot(t)], self.out.at[t], self.sem.at[t])

    def tick(self, j, i):
        if i == 0:
            pl.when((j >= 0) & (j < self.count))(lambda: self.copy(j).start())

    def release(self, t):
        self.copy(t).wait()


class Small:
    def __init__(self, at, sums, ra, rb, one, rc, two, rd, out, send, recv):
        self.at, self.sums, self.ra, self.rb, self.one, self.rc, self.two, self.rd = at, sums, ra, rb, one, rc, two, rd
        self.out, self.send, self.recv = out, send, recv

    @staticmethod
    def scratch():
        slab = (16, 128)
        return [pltpu.VMEM(shape + slab, f32) for shape in ((4, 2), (4,), (3,), (), (), (), ())] + [
            pltpu.SemaphoreType.DMA((4,)), pltpu.SemaphoreType.DMA((4,))]

    def copy(self, n, src, dst, dev):
        return remote(src, dst, self.send.at[n], self.recv.at[n], dev)

    def pair(self):
        return self.copy(0, self.sums.at[:, 1 - self.at.c], self.ra, self.at.sib_dev)

    def step(self, n):
        at, c = self.at, self.at.c
        if n > 4:
            return
        if n == 0:
            self.pair().start()
        if n == 1:
            self.pair().wait()
            self.sums[:, c] = self.sums[:, c] + self.ra[...]
            for i, (zz, dev) in enumerate(zip(at.zs, at.z_devs)):
                self.copy(1, self.sums.at[zz, c], self.rb.at[i], dev).start()
        if n == 2:
            self.copy(1, self.rb, self.rb, at.x_dev).wait()
            self.one[...] = self.sums[at.z, c] + self.rb[0] + self.rb[1] + self.rb[2]
            self.copy(2, self.one, self.rc, at.x_dev).start()
        if n == 3:
            self.copy(2, self.one, self.rc, at.x_dev).wait()
            self.two[...] = self.one[...] + self.rc[...]
            self.copy(3, self.two, self.rd, at.y_dev).start()
        if n == 4:
            self.copy(3, self.two, self.rd, at.y_dev).wait()
            self.out[...] = self.two[...] + self.rd[...]


def transpose_rows(src, dst, rows):
    full = rows // 128

    def one(i, carry):
        o = pl.multiple_of(i * 128, 128)
        dst[0:D, pl.ds(o, 128)] = src[pl.ds(o, 128), :].T
        return carry

    lax.fori_loop(0, full, one, 0)
    if rows % 128:
        dst[0:D, full * 128 : rows] = src[full * 128 : rows, :].T
    dst[0:D, rows:] = jnp.zeros((D, dst.shape[1] - rows), bf)
    if dst.shape[0] > D:
        dst[D:, :] = jnp.ones((dst.shape[0] - D, dst.shape[1]), bf)


def iota(shape, dim):
    return lax.broadcasted_iota(jnp.int32, shape, dim)


def units_of(first, rows):
    d = iota((rows, 128), 0) + first - UNIT * iota((rows, 128), 1)
    return jnp.where((d >= 0) & (d < UNIT), 1.0, 0.0).astype(bf)


def places_of(first, rows, width):
    r = iota((rows, width), 0) + first
    lane = iota((rows, width), 1)
    down = r - GRID * lane
    unit = lax.shift_right_logical(lane * 9363, 16)
    t = r - UNIT * unit
    across = t - GRID * lax.shift_right_logical(t * 37, 8)
    yes = jnp.ones((rows, width), f32)
    no = jnp.zeros((rows, width), f32)
    ohy = jnp.where((down >= 0) & (down < GRID), yes, no).astype(bf)
    ohx = jnp.where((t >= 0) & (t < UNIT) & (across == lane - GRID * unit), yes, no).astype(bf)
    return ohy, ohx


FIRST_STEPS = ((("s", 9),), (("s", 11), ("p", 8), ("d", 9)), (("p", 9), ("d", 11)), (("p", 11),))
SECOND_STEPS = ((("s", 10), ("p", 7), ("d", 8)), (("s", 12), ("d", 10)), (("p", 10), ("d", 12)), (("p", 12),))


def layer_kernel(rows, comm, *refs):
    refs = list(refs)

    def take(n):
        got = refs[:n]
        del refs[:n]
        return got

    tok_h, g_h, tab, q_table, k_table = take(5)
    if comm:
        small, ws_h = take(2)
    else:
        vec_in, b_up_in, w_h = take(3)
    out_h, gt_h, gw_h = take(3)
    if comm:
        (sums_out,) = take(1)
    else:
        vg, db_qkv, db_up = take(3)
    x_h, normedt_h, mixed_h, att_h, stats_h = take(5)
    if comm:
        (w_h,) = take(1)
    a1, a2, b1, b2, w, q_feat, k_feat, vec, b_up, lsem, wsem, osem, isem, xsem, tsem = take(15)
    parts = w_h.shape[0]
    chunks = parts - 1
    feed = chunks - QUADS
    if comm:
        vg, db_qkv, db_up, smalls, ssem, gsend, grecv = take(7)
        small_refs = take(9)
        at = Place()
        gather = Gather(at, ws_h, w_h, gsend, grecv)
        tick = gather.run
        red = Reduce(at, chunks, *refs[:6], gw_h, *refs[6:], w_h)
    else:
        tick = lambda *steps: None
        red = Keep(chunks, refs[0], gw_h, refs[1])
    KP = normedt_h.shape[1]
    pairs = rows // PAIR
    RB = PAIR // 7
    blocks = rows // RB

    def block(r):
        return pl.ds(pl.multiple_of(r * RB, 16), RB)

    def pair_rows(r):
        return pl.ds(pl.multiple_of(r * PAIR, 16), PAIR)

    every, qkv, out = pl.ds(0, CW), pl.ds(0, 3 * QW), pl.ds(3 * QW, QW)

    def load(k, s, src=every, dst=every):
        if comm:
            gather.load(k, src, w.at[s, :, dst], wsem.at[s])
        else:
            pltpu.make_async_copy(w_h.at[k, :, src], w.at[s, :, dst], wsem.at[s]).start()

    def load_quad(k, s):
        load(k, s, qkv, qkv)
        load(QUADS, s, pl.ds(pl.multiple_of(k * QW, QW), QW), out)

    def loaded(s, cols=every):
        pltpu.make_async_copy(w.at[s, :, cols], w.at[s, :, cols], wsem.at[s]).wait()

    tok_in = pltpu.make_async_copy(tok_h, b2, lsem.at[0])
    tok_in.start()
    g_in = pltpu.make_async_copy(g_h, b2, lsem.at[1])
    if comm:
        at.barrier()
        own = smalls.at[at.f]
        smalls[at.f] = small[...]
        for dev in at.z_devs:
            remote(own, own, ssem.at[0], ssem.at[1], dev).start()
        gather.begin(0)
    else:
        load(0, 0, qkv, qkv)
        vec[...] = vec_in[...]
        b_up[...] = b_up_in[...]

    def forward(normed, normedt, mixed, att, stats):
        def features(r, carry):
            unit = units_of(r * RB, RB)
            q_feat[block(r), :] = dot(unit, q_table[...]).astype(bf)
            k_feat[block(r), :] = dot(unit, k_table[...]).astype(bf)
            return carry

        lax.fori_loop(0, blocks, features, 0)
        tok_in.wait()
        if comm:
            gather.begin(1)

        def place(r, carry):
            n = PAIR
            sl = pl.ds(pl.multiple_of(r * n, 16), n)
            for half, hot in enumerate(places_of(r * n, n, tab.shape[1])):
                cols = slice(D // 2 * half, D // 2 * (half + 1))
                a1[sl, cols] = b2[sl, cols].astype(f32) + (dot(hot, tab[0]) + dot(hot, tab[1]) + dot(hot, tab[2]))
            return carry

        def norm_one(r, carry):
            xhat, _ = norm_parts(a1[block(r), :])
            normed[block(r), :] = (xhat * vec[0:1, :] + vec[1:2, :]).astype(bf)
            return carry

        if comm:
            lax.fori_loop(0, pairs // 2, place, 0)
            three = smalls.at[pl.ds(0, 3)]
            remote(three, three, ssem.at[0], ssem.at[1], at.x_dev).wait()
            for zz in [at.z] + at.zs:
                slab = smalls.at[2 * zz + at.c]
                remote(slab, slab, ssem.at[2], ssem.at[3], at.sib_dev).start()
            gather.begin(2)
            tick(("s", 0))
            lax.fori_loop(pairs // 2, pairs, place, 0)
            four = smalls.at[pl.ds(0, 4)]
            remote(four, four, ssem.at[2], ssem.at[3], at.sib_dev).wait()
            spread_vectors(smalls, vec, b_up)
        else:
            lax.fori_loop(0, pairs, place, 0)
        x_out = pltpu.make_async_copy(a1, x_h, osem.at[0])
        tick(("s", 1))
        lax.fori_loop(0, blocks // 2, norm_one, 0)
        tick(("d", 0))
        lax.fori_loop(blocks // 2, blocks, norm_one, 0)
        tick(("s", 2), ("p", 0))
        transpose_rows(normed, normedt, rows)
        n_out = pltpu.make_async_copy(normedt, normedt_h, osem.at[1])
        tick(("d", 1))
        if comm:
            gather.ready(0)
            load(0, 0, qkv, qkv)
        x_out.start()
        n_out.start()

        def saves(k):
            return (pltpu.make_async_copy(mixed, mixed_h.at[k], osem.at[2]),
                    pltpu.make_async_copy(att.at[:, pl.ds(QW * k, QW)], att_h.at[k], osem.at[3]),
                    pltpu.make_async_copy(stats, stats_h.at[k], osem.at[4]))

        for k in range(QUADS):
            s = k % 2
            loaded(s, qkv)

            def following():
                if k + 1 < QUADS:
                    load(k + 1, 1 - s, qkv, qkv)
                else:
                    load(QUADS, 1 - s)

            if not comm:
                following()
            if k > 0:
                for c in saves(k - 1):
                    c.wait()
            cols = slice(QW * k, QW * (k + 1))
            b_qkv = jnp.concatenate([vec[2:3, cols], jnp.zeros((1, QW), f32), vec[3:4, cols]], axis=1)

            tick(("p", k + 1), ("s", k + 3))

            def project(r, carry):
                sl = pair_rows(r)
                mixed[sl, :] = (dot(normed[sl, :], w[s, :, 0 : 3 * QW]) + b_qkv).astype(bf)
                return carry

            lax.fori_loop(0, pairs, project, 0)
            tick(("d", k + 2))
            saves(k)[0].start()
            if k == 1:
                g_in.start()

            def advance():
                gather.ready(k + 1)
                following()

            def hook(i):
                if comm:
                    pl.when(i == pairs - 1)(advance)

            attention_forward(pairs, mixed, q_feat, k_feat, att.at[:, pl.ds(QW * k, QW)], stats, hook)
            saves(k)[1].start()
            saves(k)[2].start()
        tick(("p", QUADS + 1), ("s", QUADS + 3))
        loaded(0)
        x_out.wait()

        def project_out(r, carry):
            sl = pair_rows(r)
            a1[sl, :] += dot(att[sl, :], w[0], NT) + vec[4:5, :]
            return carry

        lax.fori_loop(0, pairs, project_out, 0)
        tick(("d", QUADS + 2))
        if comm:
            gather.ready(QUADS + 1)
        load(QUADS + 1, 1)

        def second(r, carry):
            xhat, _ = norm_parts(a1[block(r), :])
            b1[block(r), :] = (xhat * vec[5:6, :] + vec[6:7, :]).astype(bf)
            return carry

        lax.fori_loop(0, blocks, second, 0)
        tick(("s", 8), ("p", 6), ("d", 7))
        n_out.wait()
        for c in saves(QUADS - 1):
            c.wait()

    pl.run_scoped(forward, pltpu.VMEM((rows, D), bf), pltpu.VMEM(normedt_h.shape, bf), pltpu.VMEM((rows, 3 * QW), bf),
                  pltpu.VMEM((rows, D), bf), pltpu.VMEM((rows, QW), bf))

    def put(t, m, left, right):
        slot, n = red.slot(t), left.shape[1]
        for i in range(2):
            red.gp[slot, 2 * m + i, :, 0:n] = left[256 * i : 256 * (i + 1)].astype(bf)
            red.gp[slot, 2 * m + i, :, n:CW] = right[256 * i : 256 * (i + 1)].astype(bf)

    def out_copy():
        return pltpu.make_async_copy(b1, out_h, osem.at[0])

    def feed_forward(n2t, gt, act, dhid, acc):
        act[rows:KP, :] = jnp.zeros((KP - rows, FC), bf)
        dhid[rows:KP, :] = jnp.zeros((KP - rows, FC), bf)
        acc[...] = jnp.zeros_like(acc)
        a2[...] = jnp.zeros_like(a2)
        transpose_rows(b1, n2t, rows)
        g_in.wait()
        transpose_rows(b2, gt, rows)

        def chunk(j, carry):
            s = lax.rem(j + 1, 2)
            loaded(s)
            after = QUADS + 2 + j
            if comm:
                for n, steps in enumerate(FIRST_STEPS):
                    pl.when(j == n)(functools.partial(tick, *steps))
            red.tick(j - 1, 0)
            for r in range(pairs):
                sl = pair_rows(r)
                h = dot(b1[sl, :], w[s, :, 0:FC]) + b_up[pl.ds(j, 1), :]
                da = dot(b2[sl, :], w[s, :, FC:CW])
                phi = 0.5 * (1.0 + lax.erf(h * 0.7071067811865476))
                slope = phi + h * (jnp.exp(-0.5 * h * h) * 0.3989422804014327)
                a = (h * phi).astype(bf)
                dh = (da * slope).astype(bf)
                act[sl, :] = a
                dhid[sl, :] = dh
                acc[sl, :] += dot(a, w[s, :, FC:CW], NT)
                a2[sl, :] += dot(dh, w[s, :, 0:FC], NT)
                red.tick(j - 1, r + 1)
                if r == 0:
                    @pl.when(after < parts)
                    def _():
                        if comm:
                            gather.ready(after)
                        load(after, 1 - s)

                    pl.when(after == parts)(lambda: load_quad(0, 1 - s))
                    if comm:
                        for n, steps in enumerate(SECOND_STEPS):
                            pl.when(j == n)(functools.partial(tick, *steps))

            @pl.when(j >= red.SLOTS)
            def _():
                red.release(j - red.SLOTS)

            put(j, 0, dot(n2t[0:512, :], dhid[...]), dot(gt[0:512, :], act[...]))
            red.tick(j - 1, 3)
            left = dot(n2t[512:, :], dhid[...])
            db_up[pl.ds(j, 1), :] = left[512:513]
            put(j, 1, left, dot(gt[512:, :], act[...]))
            return carry

        lax.fori_loop(0, feed, chunk, 0)
        red.tick(feed - 1, 0)
        vg[...] = jnp.zeros_like(vg)

        def last(r, carry):
            sl = block(r)
            middle = a1[sl, :]
            b1[sl, :] = (middle + acc[sl, :] + vec[7:8, :]).astype(bf)
            a1[sl, :] = jnp.zeros_like(middle)
            xhat, inv = norm_parts(middle)
            dn = a2[sl, :]
            cot = b2[sl, :].astype(f32)
            e = dn * vec[5:6, :]
            gm = cot + (e - jnp.mean(e, axis=-1, keepdims=True) - xhat * jnp.mean(e * xhat, axis=-1, keepdims=True)) * inv
            a2[sl, :] = gm
            gb = gm.astype(bf)
            b2[sl, :] = gb
            vg[2:3, :] += jnp.sum(gb.astype(f32), axis=0, keepdims=True)
            vg[3:4, :] += jnp.sum(dn * xhat, axis=0, keepdims=True)
            vg[4:5, :] += jnp.sum(dn, axis=0, keepdims=True)
            vg[5:6, :] += jnp.sum(cot, axis=0, keepdims=True)
            pl.when(r == blocks // 2)(functools.partial(red.tick, feed - 1, 1))
            return carry

        lax.fori_loop(0, blocks, last, 0)
        out_copy().start()

    pl.run_scoped(feed_forward, pltpu.VMEM(normedt_h.shape, bf), pltpu.VMEM((D, KP), bf), pltpu.VMEM((KP, FC), bf),
                  pltpu.VMEM((KP, FC), bf), pltpu.VMEM((rows, D), f32))

    def backward(normedt, gbt, mixed, att, stats, datt, swap, dq, dk, dv, xb, ob):
        n_in = pltpu.make_async_copy(normedt_h, normedt, lsem.at[0])

        def inputs(k, s):
            return (pltpu.make_async_copy(mixed_h.at[k], mixed.at[s, pl.ds(0, rows)], isem.at[s, 0]),
                    pltpu.make_async_copy(att_h.at[k], att.at[s, pl.ds(0, rows)], isem.at[s, 1]),
                    pltpu.make_async_copy(stats_h.at[k], stats.at[s], isem.at[s, 2]))

        for c in inputs(0, 1):
            c.start()
        n_in.start()
        for s in range(2):
            mixed[s, rows:KP, :] = jnp.zeros((KP - rows, 3 * QW), bf)
            att[s, rows:KP, :] = jnp.zeros((KP - rows, QW), bf)
        swap[...] = jnp.where(low_lanes(128) != (iota((128, 128), 0) < 64), 1.0, 0.0).astype(bf)
        transpose_rows(b2, gbt, rows)

        def keep(k, s):
            return pltpu.make_async_copy(mixed.at[s, pl.ds(0, rows)], mixed_h.at[k], isem.at[s, 3])

        def quad(k, carry):
            s = lax.rem(k + 1, 2)
            t = feed + k
            loaded(s)
            for c in inputs(k, s):
                c.wait()

            @pl.when(k > 0)
            def _():
                keep(k - 1, 1 - s).wait()

            @pl.when(k + 1 < QUADS)
            def _():
                load_quad(k + 1, 1 - s)
                for c in inputs(k + 1, 1 - s):
                    c.start()

            def back(r, inner):
                sl = pair_rows(r)
                datt[sl, :] = dot(b2[sl, :], w[s, :, 3 * QW : CW]).astype(bf)
                return inner

            pl.when(k > 0)(lambda: red.tick(t - 1, 0))
            lax.fori_loop(0, pairs, back, 0)

            def hook(i):
                pl.when((i == pairs - 1) & (k > 0))(functools.partial(red.tick, t - 1, 1))
                pl.when(i == 2 * pairs - 1)(functools.partial(red.tick, t - 1, 2))

            attention_backward(pairs, mixed.at[s], att.at[s], stats.at[s], datt, k_feat, swap, dq, dk, dv, hook)
            red.release(t - red.SLOTS)
            pl.when(k == 0)(n_in.wait)
            put(t, 0, dot(normedt[0:512, :], mixed[s]), dot(gbt[0:512, :], att[s]))
            red.tick(t - 1, 3)
            left = dot(normedt[512:, :], mixed[s])
            db_qkv[pl.ds(k, 1), :] = left[512:513]
            put(t, 1, left, dot(gbt[512:, :], att[s]))

            pl.when(k + 1 < QUADS)(lambda: keep(k, s).start())
            return carry

        lax.fori_loop(0, QUADS, quad, 0)
        red.tick(chunks - 1, 0)

        def again(k, s):
            load(k, s, qkv, qkv)
            inputs(k, s)[0].start()

        again(0, 1)

        def back_in(n, carry):
            s = lax.rem(n, 2)

            @pl.when(n > 0)
            def _():
                loaded(s, qkv)
                inputs(n - 1, s)[0].wait()

            for r in range(pairs):
                sl = pl.ds(r * PAIR, PAIR)
                a1[sl, :] += dot(mixed[s, sl, :], w[s, :, 0 : 3 * QW], NT)

            pl.when(n + 2 < QUADS)(lambda: again(n + 1, s))

            if comm:
                for m, (j, i) in enumerate(((0, 1), (0, 2), (0, 3), (1, 0))):
                    pl.when(n == m)(functools.partial(red.tick, chunks - 1 + j, i))
            return carry

        lax.fori_loop(0, QUADS, back_in, 0)
        ring = xb.shape[0]

        def xcopy(r):
            s = lax.rem(r, ring)
            return pltpu.make_async_copy(x_h.at[block(r)], xb.at[s], xsem.at[s])

        def tcopy(r):
            s = lax.rem(r, 2)
            return pltpu.make_async_copy(ob.at[s], gt_h.at[block(r)], tsem.at[s])

        for r in range(ring):
            xcopy(r).start()

        def last(r, carry):
            xcopy(r).wait()
            pl.when(r >= 2)(lambda: tcopy(r - 2).wait())
            xhat, inv = norm_parts(xb[lax.rem(r, ring)])
            dn = a1[block(r), :]
            e = dn * vec[0:1, :]
            total = a2[block(r), :] + (e - jnp.mean(e, axis=-1, keepdims=True) - xhat * jnp.mean(e * xhat, axis=-1, keepdims=True)) * inv
            ob[lax.rem(r, 2)] = total.astype(bf)
            tcopy(r).start()
            vg[0:1, :] += jnp.sum(dn * xhat, axis=0, keepdims=True)
            vg[1:2, :] += jnp.sum(dn, axis=0, keepdims=True)
            pl.when(r + ring < blocks)(lambda: xcopy(r + ring).start())
            if comm:
                for at_r, steps in ((0, ((1, 1),)), (2, ((1, 2),)), (4, ((1, 3),)), (7, ((2, 0),)), (13, ((2, 1), (2, 2)))):
                    for j, i in steps:
                        pl.when(r == at_r)(functools.partial(red.tick, chunks - 1 + j, i))
            return carry

        lax.fori_loop(0, blocks, last, 0)
        out_copy().wait()
        if comm:
            share = Small(at, *small_refs[:7], sums_out, *small_refs[7:])
            sums = share.sums
            sums[...] = jnp.zeros_like(sums)
            for f in range(8):
                lanes = slice(128 * f, 128 * (f + 1))
                q, half = slice(f // 2, f // 2 + 1), 128 * (f % 2)
                rows_of = [vg[0:1, lanes], vg[1:2, lanes], db_qkv[q, half : half + 128],
                           db_qkv[q, 2 * QW + half : 2 * QW + half + 128]] + [vg[n : n + 1, lanes] for n in (2, 3, 4, 5)]
                rows_of += [db_up[f : f + 1, 128 * i : 128 * (i + 1)] for i in range(4)]
                for i, row in enumerate(rows_of):
                    sums[f // 2, f % 2, i : i + 1, :] = row
            for n, k in enumerate(range(11, 17)):
                red.tick(chunks - 1 + k // 4, k % 4)
                share.step(n)
            for k in range(parts):
                gather.finish(k)
        for r in (blocks - 2, blocks - 1):
            tcopy(r).wait()
        for t in range(chunks - red.SLOTS, chunks):
            red.release(t)

    pl.run_scoped(backward, pltpu.VMEM(normedt_h.shape, bf), pltpu.VMEM((D, KP), bf), pltpu.VMEM((2, KP, 3 * QW), bf),
                  pltpu.VMEM((2, KP, QW), bf), pltpu.VMEM((2, rows, QW), bf), pltpu.VMEM((rows, QW), bf), pltpu.VMEM((128, 128), bf), pltpu.VMEM((PAIR, 128), f32),
                  pltpu.VMEM((PAIR, 128), f32), pltpu.VMEM((PAIR, 128), f32), pltpu.VMEM((3, RB, D), f32),
                  pltpu.VMEM((2, RB, D), bf))


def layer(rows, comm, chunks, *args):
    A, V = any_spec(), vmem_spec()
    KP = -(-rows // 256) * 256
    sums = ((8, D), (QUADS, 3 * QW), (chunks - QUADS, FC))
    kept = [sds((rows, D), f32), sds((D + 16, KP), bf), sds((QUADS, rows, 3 * QW), bf), sds((QUADS, rows, QW), bf),
            sds((QUADS, rows, QW), bf)]
    first = [sds((rows, D), bf), sds((rows, D), bf), sds((chunks, 128, CW) if comm else (chunks, 4, 256, CW), bf)]
    scratch = [
        pltpu.VMEM((rows, D), f32), pltpu.VMEM((rows, D), f32), pltpu.VMEM((rows, D), bf), pltpu.VMEM((rows, D), bf),
        pltpu.VMEM((2, D, CW), bf), pltpu.VMEM((rows, 128), bf), pltpu.VMEM((rows, 128), bf), pltpu.VMEM((8, D), f32),
        pltpu.VMEM((chunks - QUADS, FC), f32),
        pltpu.SemaphoreType.DMA((2,)), pltpu.SemaphoreType.DMA((2,)), pltpu.SemaphoreType.DMA((5,)),
        pltpu.SemaphoreType.DMA((2, 4)), pltpu.SemaphoreType.DMA((3,)), pltpu.SemaphoreType.DMA((2,)),
    ]
    if comm:
        in_specs = [A, A, V, V, V, V, A]
        out_shape = first + [sds((16, 128), f32)] + kept + [sds((chunks + 1, 4, 256, CW), bf)]
        out_specs = [A, A, A, V] + [A] * 6
        scratch += [pltpu.VMEM(shape, f32) for shape in sums] + [
            pltpu.VMEM((8, 16, 128), bf), pltpu.SemaphoreType.DMA((4,)), pltpu.SemaphoreType.DMA((chunks + 1,)),
            pltpu.SemaphoreType.DMA((chunks + 1, 6))] + Small.scratch() + Reduce.scratch(chunks)
        params = pltpu.CompilerParams(vmem_limit_bytes=VMEM_LIMIT, collective_id=0, has_side_effects=True)
    else:
        in_specs = [A, A, V, V, V, V, V, A]
        out_shape = first + [sds(shape, f32) for shape in sums] + kept
        out_specs = [A, A, A, V, V, V] + [A] * 5
        scratch += Keep.scratch(chunks)
        params = pltpu.CompilerParams(vmem_limit_bytes=VMEM_LIMIT)
    return pl.pallas_call(
        functools.partial(layer_kernel, rows, comm), out_shape=out_shape, in_specs=in_specs, out_specs=out_specs,
        scratch_shapes=scratch, compiler_params=params, name="encoder_layer",
    )(*args)


def prepare_kernel(units, band, gsd, freq, qkv, out, up, down, *refs):
    *vectors, shard, tab, q_table, k_table = refs
    if vectors:
        *vectors, bias_up, shard, tab, q_table, k_table, small = refs
        rows = [v[...].reshape(1, 128) for v in vectors] + [bias_up[128 * i : 128 * (i + 1)].reshape(1, 128) for i in range(4)]
        rows.append(jnp.zeros((16 - len(rows), 128), bf))
        small[...] = jnp.concatenate([r.astype(f32) for r in rows], axis=0).astype(bf)
    for k in range(QUADS):
        for i in range(3):
            shard[k, :, QW * i : QW * (i + 1)] = qkv[:, D * i + QW * k : D * i + QW * (k + 1)]
        shard[QUADS, :, QW * k : QW * (k + 1)] = out[QW * k : QW * (k + 1), :].T
    for j in range(up.shape[1] // FC):
        shard[QUADS + 1 + j, :, 0:FC] = up[:, FC * j : FC * (j + 1)]
        shard[QUADS + 1 + j, :, FC:CW] = down[FC * j : FC * (j + 1), :].T
    entry = iota((tab.shape[1], 128), 0)
    unit = lax.shift_right_logical(entry * 9363, 16)
    level = jnp.zeros(entry.shape, jnp.int32)
    row = iota((128, 128), 0)
    item = jnp.full((128, 128), -100, jnp.int32)
    label = jnp.int32(0)
    for u in range(units):
        if u % UNITS_MB == 0:
            label = jnp.int32(-1 + UNITS_MB * (u // UNITS_MB % 2))
        label = label + jnp.where(band[u] <= 1, 1, 0)
        item = jnp.where(row == u, label, item)
        level = jnp.where(unit == u, gsd[u], level)
    place = (entry - GRID * unit).astype(f32) * jnp.exp2((level.astype(f32) - 3.0) * 0.5)
    angle = jnp.concatenate([place, place], axis=1) * freq[...]
    wave = jnp.concatenate([jnp.sin(angle), jnp.cos(angle)], axis=1)
    wave = jnp.where(iota(wave.shape, 0) < GRID * units, wave, 0.0)
    high = wave.astype(bf)
    rest = wave - high.astype(f32)
    middle = rest.astype(bf)
    tab[0] = high
    tab[1] = middle
    tab[2] = (rest - middle.astype(f32)).astype(bf)
    slot = (iota((128, 128), 1) & 63) - 3
    used = (slot >= 0) & (slot < 2 * UNITS_MB)
    real = row < units
    q_table[...] = jnp.where(real & (item == slot), 1.0, 0.0).astype(bf)
    k_table[...] = jnp.where(real, jnp.where(used & (item != slot), NEG, jnp.where(slot < 0, 1.0, 0.0)), 0.0).astype(bf)


def prepare(rows, band_code, gsd_code, qkv, out, up, down, *vectors):
    units = rows // UNIT
    n = qkv.shape[0]
    places = -(-GRID * units // 256) * 256
    quarter = D // 4
    freq = np.exp2(np.arange(quarter, dtype=np.float32) * np.float32(-math.log2(10000.0) / quarter)).astype(np.float32)
    V, S = vmem_spec(), pl.BlockSpec(memory_space=pltpu.SMEM)
    return pl.pallas_call(
        functools.partial(prepare_kernel, units),
        out_shape=(sds((QUADS + 1 + up.shape[1] // FC, n, CW), bf), sds((3, places, 2 * quarter), bf), sds((128, 128), bf),
                   sds((128, 128), bf)) + ((sds((16, 128), bf),) if vectors else ()),
        in_specs=[S, S, V, V, V, V, V] + [V] * len(vectors), out_specs=(V, V, V, V) + ((V,) if vectors else ()),
        compiler_params=pltpu.CompilerParams(vmem_limit_bytes=VMEM_LIMIT), name="prepare",
    )(band_code, gsd_code, jnp.asarray(freq)[None, :], qkv, out, up, down, *vectors)


def results_kernel(rows, out_i, gt_i, gw_i, sums, out_h, gt_h, dg1, db1, g_qkv, dbq, dbv, g_out, dbo, dg2, db2, g_up, db_up, g_down,
                   db_down, out_v, gt_v, gt_f, gw, qkv_v, o_v, up_v, down_v, sem_in, sem_out):
    loads = [pltpu.make_async_copy(src, dst, sem_in.at[i])
             for i, (src, dst) in enumerate(((gw_i, gw), (out_i, out_v), (gt_i, gt_v)))]
    stores = [pltpu.make_async_copy(src, dst, sem_out.at[i])
              for i, (src, dst) in enumerate(((out_v, out_h), (gt_f, gt_h), (qkv_v, g_qkv), (o_v, g_out), (up_v, g_up), (down_v, g_down)))]
    for c in loads:
        c.start()
    for i, ref in enumerate((dg1, db1, dbq, dbv, dbo, dg2, db2, db_down)):
        ref[...] = sums[i]
    for i in range(4):
        db_up[128 * i : 128 * (i + 1)] = sums[8 + i]
    loads[0].wait()
    feed = gw.shape[0] - QUADS
    for k in range(QUADS):
        for i in range(3):
            qkv_v[:, D * i + QW * k : D * i + QW * (k + 1)] = gw[feed + k, :, QW * i : QW * (i + 1)].astype(f32)
        o_v[QW * k : QW * (k + 1), :] = gw[feed + k, :, 3 * QW : CW].T.astype(f32)
    stores[2].start()
    stores[3].start()
    loads[1].wait()
    stores[0].start()
    for j in range(feed):
        up_v[:, FC * j : FC * (j + 1)] = gw[j, :, 0:FC].astype(f32)
        down_v[FC * j : FC * (j + 1), :] = gw[j, :, FC:CW].T.astype(f32)
    stores[4].start()
    stores[5].start()
    loads[2].wait()
    RB = PAIR // 7

    def widen(r, carry):
        sl = pl.ds(pl.multiple_of(r * RB, 16), RB)
        gt_f[sl, :] = gt_v[sl, :].astype(f32)
        return carry

    lax.fori_loop(0, rows // RB, widen, 0)
    stores[1].start()
    for c in stores:
        c.wait()


def results(out, gt, gw, sums):
    rows, chunks = out.shape[0], gw.shape[0]
    hidden = (chunks - QUADS) * FC
    A, V = any_spec(), vmem_spec()
    vec = sds((128,), f32)
    wide = [sds((128, 3 * D), f32), sds((D, 128), f32), sds((128, hidden), f32), sds((hidden, 128), f32)]
    return pl.pallas_call(
        functools.partial(results_kernel, rows),
        out_shape=(sds((rows, D), bf), sds((rows, D), f32), vec, vec, wide[0], vec, vec, wide[1], vec, vec, vec, wide[2],
                   sds((512,), f32), wide[3], vec),
        in_specs=[A, A, A, V], out_specs=(A, A, V, V, A, V, V, A, V, V, V, A, V, A, V),
        scratch_shapes=[pltpu.VMEM((rows, D), bf), pltpu.VMEM((rows, D), bf), pltpu.VMEM((rows, D), f32), pltpu.VMEM(gw.shape, bf)]
        + [pltpu.VMEM(v.shape, f32) for v in wide] + [pltpu.SemaphoreType.DMA((3,)), pltpu.SemaphoreType.DMA((6,))],
        compiler_params=pltpu.CompilerParams(vmem_limit_bytes=VMEM_LIMIT), name="results",
    )(out, gt, gw, sums)


def local(dp, fsdp, tokens, band_code, gsd_code, norm1_gain, norm1_bias, qkv_weight, bias_q, bias_v, out_weight, bias_out,
          norm2_gain, norm2_bias, up_weight, bias_up, down_weight, bias_down, grad_out):
    rows = tokens.shape[0]
    comm = dp == 4 and fsdp == 8
    vectors = (norm1_gain, norm1_bias, bias_q, bias_v, bias_out, norm2_gain, norm2_bias, bias_down)
    shard, tab, q_table, k_table, *small = prepare(rows, band_code, gsd_code, qkv_weight, out_weight, up_weight, down_weight,
                                                   *(vectors + (bias_up,) if comm else ()))
    chunks, n = shard.shape[0] - 1, shard.shape[1]
    args = (tokens, grad_out, tab, q_table, k_table)
    if comm:
        out, grad_tokens, gw, sg, *_ = layer(rows, True, chunks, *args, *small, shard)
        return results(out, grad_tokens, gw, sg)
    else:
        gathered = lax.all_gather(jnp.stack(vectors), "fsdp", axis=1, tiled=True).astype(f32)
        up_bias = lax.all_gather(bias_up, "fsdp", axis=0, tiled=True).astype(f32).reshape(-1, FC)
        whole = lax.all_gather(shard, "fsdp", axis=1, tiled=True)
        out, grad_tokens, gw, vg, db_qkv, db_up, *_ = layer(rows, False, chunks, *args, gathered, up_bias, whole)
        sg = jnp.concatenate([vg[0:2], db_qkv[:, 0:QW].reshape(1, D), db_qkv[:, 2 * QW :].reshape(1, D), vg[2:6]], axis=0)
        sg = jnp.concatenate([sg.reshape(8, fsdp, n).transpose(1, 0, 2).reshape(fsdp, 8 * n), db_up.reshape(fsdp, 4 * n)], axis=1)
        sg = lax.psum(lax.psum_scatter(sg, "fsdp", scatter_dimension=0, tiled=True), "dp").reshape(12, n)
        gw = lax.psum(lax.psum_scatter(gw.reshape(chunks, D, CW), "fsdp", scatter_dimension=1, tiled=True), "dp")
    gw = gw.astype(f32)
    g_ff, g_att = gw[: chunks - QUADS], gw[chunks - QUADS :]
    g_qkv = g_att[:, :, : 3 * QW].reshape(QUADS, n, 3, QW).transpose(1, 2, 0, 3).reshape(n, 3 * D)
    g_out = g_att[:, :, 3 * QW :].transpose(0, 2, 1).reshape(D, n)
    g_up = g_ff[:, :, :FC].transpose(1, 0, 2).reshape(n, -1)
    g_down = g_ff[:, :, FC:].transpose(0, 2, 1).reshape(-1, n)
    grad_tokens = grad_tokens.astype(f32)
    return (out, grad_tokens, sg[0], sg[1], g_qkv, sg[2], sg[3], g_out, sg[4], sg[5], sg[6], g_up, sg[8:12].reshape(4 * n), g_down, sg[7])


def solution(mesh):
    rows, vec, first, second = P(("dp", "fsdp"), None), P("fsdp"), P("fsdp", None), P(None, "fsdp")
    codes = P(("dp", "fsdp"))
    return jax.shard_map(
        functools.partial(local, mesh.shape["dp"], mesh.shape["fsdp"]),
        mesh=mesh,
        in_specs=(rows, codes, codes, vec, vec, first, vec, vec, second, vec, vec, vec, first, vec, second, vec, rows),
        out_specs=(rows, rows, vec, vec, first, vec, vec, second, vec, vec, vec, first, vec, second, vec),
        check_vma=False,
    )
```

```python
import functools
import math

import jax
import jax.numpy as jnp
import numpy as np
from jax import lax
from jax.experimental import pallas as pl
from jax.experimental.pallas import tpu as pltpu
from jax.sharding import PartitionSpec as P

bf = jnp.bfloat16
f32 = jnp.float32
NN = (((1,), (0,)), ((), ()))
NT = (((1,), (1,)), ((), ()))
TN = (((0,), (0,)), ((), ()))
D = 1024
HEADS = 16
HEAD_DIM = 64
GRID = 7
UNIT = GRID * GRID
UNITS_MB = 8
BUF = UNIT * UNITS_MB
PAIR = 2 * BUF
QUADS = 4
QW = 256
FC = 512
CW = 1024
EPS = 1e-6
SCALE = 0.125
NEG = -1e30
VMEM_LIMIT = 62 << 20
KEYS = 384
WINDOWS = ((0, ((0, 192, 0), (192, 208, 16))), (384, ((0, 192, 0), (192, 208, 16))))
SPAN = 400


def dot(a, b, dims=NN):
    return lax.dot_general(a, b, dims, preferred_element_type=f32)


def any_spec():
    return pl.BlockSpec(memory_space=pl.ANY)


def vmem_spec():
    return pl.BlockSpec(memory_space=pltpu.VMEM)


def sds(shape, kind):
    return jax.ShapeDtypeStruct(shape, kind)


def norm_parts(v):
    center = v - jnp.mean(v, axis=-1, keepdims=True)
    inv = lax.rsqrt(jnp.mean(center * center, axis=-1, keepdims=True) + EPS)
    return center * inv, inv


def low_lanes(rows):
    return lax.broadcasted_iota(jnp.int32, (rows, 128), 1) < 64


def split_terms(v):
    lane = lax.broadcasted_iota(jnp.int32, v.shape, 1) & 63
    hi = v.astype(bf).astype(f32)
    rest = v - hi
    mid = rest.astype(bf).astype(f32)
    return jnp.where(lane == 0, hi, jnp.where(lane == 1, mid, jnp.where(lane == 2, rest - mid, 0.0))), lane < 3


def attention_forward(pairs, mixed, q_feat, k_feat, attended, stats, hook):
    def one(i, carry):
        p, hp = i // 2, lax.rem(i, 2)
        base = pl.multiple_of(p * PAIR, 16)
        lane0 = pl.multiple_of(hp * 128, 128)
        blocks = [(w, n, start, *half) for w, (start, halves) in enumerate(WINDOWS) for n, half in enumerate(halves)]
        spans = {}

        def window(w, start):
            if w not in spans:
                span = pl.ds(pl.multiple_of(base + start, 16), SPAN)
                k2 = mixed[span, pl.ds(pl.multiple_of(lane0 + QW, 128), 128)]
                v2 = mixed[span, pl.ds(pl.multiple_of(lane0 + 2 * QW, 128), 128)]
                kf = k_feat[span, :]
                low = low_lanes(SPAN)
                ones = jnp.ones_like(v2)
                spans[w] = ((jnp.where(low, k2, kf), jnp.where(low, kf, k2)), (jnp.where(low, v2, ones), jnp.where(low, ones, v2)))
            return spans[w]

        def scores(block):
            w, n, start, q0, qn, k0 = block
            keys, _ = window(w, start)
            rows = pl.ds(pl.multiple_of(base + start + q0, 16), qn)
            q2 = mixed[rows, pl.ds(lane0, 128)] * jnp.asarray(SCALE, bf)
            qf = q_feat[rows, :]
            low = low_lanes(qn)
            return [dot(q, keys[h][k0 : k0 + KEYS], NT) for h, q in enumerate((jnp.where(low, q2, qf), jnp.where(low, qf, q2)))]

        tail = None
        ahead = scores(blocks[0])
        for b, (w, n, start, q0, qn, k0) in enumerate(blocks):
            now = ahead
            if b + 1 < len(blocks):
                ahead = scores(blocks[b + 1])
            _, values = window(w, start)
            rows = pl.ds(pl.multiple_of(base + start + q0, 16), qn)
            low = low_lanes(qn)
            tops = [jnp.max(s, axis=-1, keepdims=True) for s in now]
            outs = [dot(jnp.exp(s - m).astype(bf), values[h][k0 : k0 + KEYS]) for h, (s, m) in enumerate(zip(now, tops))]
            total = jnp.where(low, outs[1], outs[0])
            out = jnp.where(low, outs[0], outs[1]) / pltpu.roll(total, 64, 1)
            terms, at = split_terms(-(jnp.where(low, tops[1], tops[0]) + jnp.log(total)))
            stat = jnp.where(at, terms, q_feat[rows, :].astype(f32))
            if w == 0 and n == 1:
                tail = (out[qn - 16 :], stat[qn - 16 :])
            if w == 1 and n == 0:
                first = lax.broadcasted_iota(jnp.int32, (16, 128), 0) < 8
                out = jnp.concatenate([jnp.where(first, tail[0], out[0:16]), out[16:]], axis=0)
                stat = jnp.concatenate([jnp.where(first, tail[1], stat[0:16]), stat[16:]], axis=0)
            attended[rows, pl.ds(lane0, 128)] = out.astype(bf)
            stats[rows, pl.ds(lane0, 128)] = stat.astype(bf)
        hook(i)
        return carry

    lax.fori_loop(0, pairs * 2, one, 0)


def attention_backward(pairs, mixed, att, stats, datt, k_feat, swap, dq, dk, dv, hook):
    def one(i, carry):
        p, hp = i // 2, lax.rem(i, 2)
        base = pl.multiple_of(p * PAIR, 16)
        lane0 = pl.multiple_of(hp * 128, 128)
        lanes = pl.ds(lane0, 128)
        dq[...] = jnp.zeros_like(dq)
        dk[...] = jnp.zeros_like(dk)
        dv[...] = jnp.zeros_like(dv)
        blocks = [(w, n, start, *half) for w, (start, halves) in enumerate(WINDOWS) for n, half in enumerate(halves)]
        spans = {}

        def window(w, start):
            if w not in spans:
                span = pl.ds(pl.multiple_of(base + start, 16), SPAN)
                k2 = mixed[span, pl.ds(pl.multiple_of(lane0 + QW, 128), 128)]
                v2 = mixed[span, pl.ds(pl.multiple_of(lane0 + 2 * QW, 128), 128)]
                kf = k_feat[span, :]
                low = low_lanes(SPAN)
                zero = jnp.zeros_like(k2)
                terms = (lax.broadcasted_iota(jnp.int32, (SPAN, 128), 1) & 63) < 3
                vf = jnp.where(terms, jnp.ones_like(v2), zero)
                spans[w] = ((jnp.where(low, k2, kf), jnp.where(low, kf, k2)), (jnp.where(low, k2, zero), jnp.where(low, zero, k2)),
                            (jnp.where(low, v2, vf), jnp.where(low, vf, v2)))
            return spans[w]

        def products(block):
            w, n, start, q0, qn, k0 = block
            keys, _, values = window(w, start)
            rows = pl.ds(pl.multiple_of(base + start + q0, 16), qn)
            q2 = mixed[rows, lanes] * jnp.asarray(SCALE, bf)
            do2 = datt[rows, lanes]
            if w != n:
                r = lax.broadcasted_iota(jnp.int32, (qn, 128), 0)
                mine = r < qn - 8 if n == 1 else r >= 8
                do2 = jnp.where(mine, do2, jnp.zeros_like(do2))
            qf = stats[rows, lanes]
            low = low_lanes(qn)
            zero = jnp.zeros_like(q2)
            prod = do2.astype(f32) * att[rows, lanes].astype(f32)
            hi = prod.astype(bf)
            inner = dot(hi, swap[...]) + dot((prod - hi.astype(f32)).astype(bf), swap[...])
            df = split_terms(-inner)[0].astype(bf)
            kk = slice(k0, k0 + KEYS)
            heads = []
            for h in range(2):
                pick = (lambda a, b: jnp.where(low, a, b)) if h == 0 else (lambda a, b: jnp.where(low, b, a))
                heads.append((dot(pick(q2, qf), keys[h][kk], NT), dot(pick(do2, df), values[h][kk], NT), pick(do2, zero), pick(q2, zero)))
            return heads

        ahead = products(blocks[0])
        for b, (w, n, start, q0, qn, k0) in enumerate(blocks):
            now = ahead
            if b + 1 < len(blocks):
                ahead = products(blocks[b + 1])
            plain = window(w, start)[1]
            at, kat = start + q0, start + k0
            pieces = []
            for h, (s, slope, o, q) in enumerate(now):
                probs = jnp.exp(s)
                pieces.append((probs.astype(bf), (probs * slope).astype(bf), o, q, plain[h][k0 : k0 + KEYS]))
            (pa, sa, oa, qa, ka), (pb, sb, ob, qb, kb) = pieces
            dv[kat : kat + KEYS, :] += dot(jnp.concatenate([pa, pb], axis=0), jnp.concatenate([oa, ob], axis=0), TN)
            dk[kat : kat + KEYS, :] += dot(jnp.concatenate([sa, sb], axis=0), jnp.concatenate([qa, qb], axis=0), TN)
            dq[at : at + qn, :] += dot(jnp.concatenate([sa, sb], axis=1), jnp.concatenate([ka, kb], axis=0))
        rows = pl.ds(base, PAIR)
        mixed[rows, lanes] = (dq[...] * SCALE).astype(bf)
        mixed[rows, pl.ds(pl.multiple_of(lane0 + QW, 128), 128)] = dk[...].astype(bf)
        mixed[rows, pl.ds(pl.multiple_of(lane0 + 2 * QW, 128), 128)] = dv[...].astype(bf)
        hook(i)
        return carry

    lax.fori_loop(0, pairs * 2, one, 0)


MESH = pl.DeviceIdType.MESH


class Place:
    def __init__(self):
        self.d = lax.axis_index("dp")
        self.f = lax.axis_index("fsdp")
        self.z = lax.div(self.f, 2)
        self.c = lax.rem(self.f, 2)
        self.dx = self.d + 1 - 2 * lax.rem(self.d, 2)
        self.dy = lax.rem(self.d + 2, 4)
        self.dd = 3 - self.d
        self.sib = self.f + 1 - 2 * self.c
        self.zs = [lax.rem(self.z + n, 4) for n in (1, 2, 3)]
        self.x_dev = (self.dx, self.f)
        self.y_dev = (self.dy, self.f)
        self.sib_dev = (self.d, self.sib)
        self.z_devs = [(self.d, 2 * zz + self.c) for zz in self.zs]

    def barrier(self):
        sem = pltpu.get_barrier_semaphore()
        for dev in [self.x_dev, self.y_dev, self.sib_dev] + self.z_devs:
            pl.semaphore_signal(sem, inc=1, device_id=dev, device_id_type=MESH)
        pl.semaphore_wait(sem, 6)


def remote(src, dst, send, recv, dev):
    return pltpu.make_async_remote_copy(src, dst, send, recv, device_id=dev, device_id_type=MESH)


class Gather:
    def __init__(self, at, shard, whole, send, recv):
        self.at, self.shard, self.whole, self.send, self.recv = at, shard, whole, send, recv
        self.chunks = whole.shape[0]

    def cols(self, k):
        return pl.ds(0, 3 * QW if isinstance(k, int) and k < QUADS else CW)

    def rows(self, q, first, count):
        return pl.ds(pl.multiple_of(self.at.c * 128 + 32 * q + first, 16), count)

    def push(self, k, planes, rows, stage, dev, src=None):
        dst = self.whole.at[k, planes, rows, self.cols(k)]
        remote(dst if src is None else src, dst, self.send.at[k], self.recv.at[k, stage], dev).start()

    def landed(self, k, stage, planes, rows):
        part = self.whole.at[k, pl.ds(0, planes), pl.ds(0, rows), self.cols(k)]
        remote(part, part, self.send.at[k], self.recv.at[k, stage], self.at.x_dev).wait_recv()

    def begin(self, k):
        at = self.at
        quarter = self.shard.at[k, pl.ds(pl.multiple_of(32 * at.d, 16), 32), self.cols(k)]
        for n, dev in enumerate(at.z_devs):
            self.push(k, 3 - n, self.rows(at.d, 0, 32), 0, dev, quarter)
        self.push(k, 0, self.rows(0, 0, 128), 5, at.sib_dev, self.shard.at[k, :, self.cols(k)])

    def spread(self, k):
        at = self.at
        self.landed(k, 0, 3, 32)
        self.push(k, pl.ds(1, 3), self.rows(at.d, 0, 32), 1, at.x_dev)
        self.push(k, pl.ds(1, 3), self.rows(at.d, 0, 32), 2, at.y_dev)

    def diagonal(self, k):
        at = self.at
        self.landed(k, 1, 3, 32)
        self.landed(k, 2, 3, 32)
        self.push(k, pl.ds(1, 3), self.rows(at.dx, 0, 16), 3, at.y_dev)
        self.push(k, pl.ds(1, 3), self.rows(at.dy, 16, 16), 4, at.x_dev)

    def pair(self, k):
        self.landed(k, 3, 3, 16)
        self.landed(k, 4, 3, 16)
        self.push(k, pl.ds(1, 3), self.rows(0, 0, 128), 5, self.at.sib_dev)

    def ready(self, k):
        self.landed(k, 5, 4, 128)

    def load(self, k, cols, dst, sem):
        at = self.at
        own = pl.multiple_of(at.z * 256 + at.c * 128, 128)
        other = pl.multiple_of((1 - at.c) * 128, 128)
        pltpu.make_async_copy(self.shard.at[k, :, cols], dst.at[pl.ds(own, 128)], sem).start()
        pltpu.make_async_copy(self.whole.at[k, 0, pl.ds(other, 128), cols], dst.at[pl.ds(at.z * 256 + other, 128)], sem).start()
        for n, zz in enumerate(at.zs):
            pltpu.make_async_copy(self.whole.at[k, n + 1, :, cols], dst.at[pl.ds(pl.multiple_of(zz * 256, 256), 256)], sem).start()

    def run(self, *steps):
        for step, k in steps:
            if step == "s":
                if k + 3 < self.chunks:
                    self.begin(k + 3)
                self.spread(k)
            elif step == "d":
                self.diagonal(k)
            else:
                self.pair(k)

    def finish(self, k):
        part = self.whole.at[k, :, pl.ds(0, 224), self.cols(k)]
        remote(part, part, self.send.at[k], self.recv.at[k, 0], self.at.x_dev).wait_send()


def spread_vectors(shards, vec, b_up):
    n = vec.shape[1] // 128
    for f in range(n):
        vec[:, 128 * f : 128 * (f + 1)] = shards[f, 0:8, :].astype(f32)
        for i in range(4):
            b_up[f : f + 1, 128 * i : 128 * (i + 1)] = shards[f, 8 + i : 9 + i, :].astype(f32)


class Reduce:
    SLOTS = 3
    STEPS = ((16, "done"), (13, "share"), (10, "total"), (8, "planes"), (5, "relay"), (1, "cross"), (0, "pair"))

    def __init__(self, at, count, gp, r1, rx, ry, rz, fin, out, send, recv, osem, sizes):
        self.at, self.count, self.gp, self.r1, self.rx, self.ry, self.rz = at, count, gp, r1, rx, ry, rz
        self.fin, self.out, self.send, self.recv, self.osem, self.sizes = fin, out, send, recv, osem, sizes

    @classmethod
    def scratch(cls, count):
        s = cls.SLOTS
        return [pltpu.VMEM((s, 4, 256, CW), bf), pltpu.VMEM((2, 4, 128, CW), bf), pltpu.VMEM((s, 3, 4, 16, CW), bf),
                pltpu.VMEM((s, 3, 4, 16, CW), bf), pltpu.VMEM((s, 3, 32, CW), bf), pltpu.VMEM((count, 32, CW), bf),
                pltpu.SemaphoreType.DMA((count, 3)), pltpu.SemaphoreType.DMA((count, 6)), pltpu.SemaphoreType.DMA((count,))]

    def slot(self, t):
        return lax.rem(t, self.SLOTS)

    def rows(self, q, first, count):
        return pl.ds(pl.multiple_of(self.at.c * 128 + q * 32 + first, 16), count)

    def push(self, t, src, dst, stage, dev, group=0):
        remote(src, dst, self.send.at[t, group], self.recv.at[t, stage], dev).start()

    def landed(self, t, stage, rows):
        part = self.part(rows)
        remote(part, part, self.send.at[t, 0], self.recv.at[t, stage], self.at.x_dev).wait_recv()

    def part(self, rows):
        planes = 1 if rows <= 256 else 4
        return self.sizes.at[0, pl.ds(0, planes), pl.ds(0, rows // planes)]

    def left(self, t, group, rows):
        part = self.part(rows)
        remote(part, part, self.send.at[t, group], self.recv.at[t, 0], self.at.x_dev).wait_send()

    def add(self, t, q, first, *parts):
        s, sl = self.slot(t), self.rows(q, first, 16)
        total = self.gp[s, :, sl, :].astype(f32)
        for p in parts:
            total = total + p.astype(f32)
        self.gp[s, :, sl, :] = total.astype(bf)

    def pair(self, t):
        s = self.slot(t)
        other = pl.ds(pl.multiple_of((1 - self.at.c) * 128, 128), 128)
        self.push(t, self.gp.at[s, :, other], self.r1.at[lax.rem(t, 2)], 0, self.at.sib_dev)

    def cross(self, t):
        at, s = self.at, self.slot(t)
        self.landed(t, 0, 512)
        own = pl.ds(pl.multiple_of(at.c * 128, 128), 128)

        def plane(zz, carry):
            self.gp[s, zz, own, :] = (self.gp[s, zz, own, :].astype(f32) + self.r1[lax.rem(t, 2), zz].astype(f32)).astype(bf)
            return carry

        lax.fori_loop(0, 4, plane, 0)
        gp = self.gp
        self.push(t, gp.at[s, :, self.rows(at.dd, 0, 16)], self.rx.at[s, 0], 1, at.x_dev)
        self.push(t, gp.at[s, :, self.rows(at.dd, 16, 16)], self.ry.at[s, 0], 1, at.y_dev)
        self.push(t, gp.at[s, :, self.rows(at.dx, 0, 16)], self.rx.at[s, 1], 2, at.x_dev)
        self.push(t, gp.at[s, :, self.rows(at.dy, 16, 16)], self.ry.at[s, 1], 2, at.y_dev)

    def relay(self, t):
        at, s = self.at, self.slot(t)
        self.landed(t, 1, 128)
        self.add(t, at.dy, 0, self.rx[s, 0])
        self.add(t, at.dx, 16, self.ry[s, 0])
        self.push(t, self.gp.at[s, :, self.rows(at.dy, 0, 16)], self.ry.at[s, 2], 2, at.y_dev)
        self.push(t, self.gp.at[s, :, self.rows(at.dx, 16, 16)], self.rx.at[s, 2], 2, at.x_dev)

    def planes(self, t):
        at, s = self.at, self.slot(t)
        self.landed(t, 2, 256)
        self.add(t, at.d, 0, self.rx[s, 1], self.ry[s, 2])
        self.add(t, at.d, 16, self.ry[s, 1], self.rx[s, 2])
        for n, (zz, dev) in enumerate(zip(at.zs, at.z_devs)):
            self.push(t, self.gp.at[s, zz, self.rows(at.d, 0, 32)], self.rz.at[s, n], 3, dev, 2)

    def quarter(self, t, q, first=0, count=32):
        return self.out.at[t, pl.ds(pl.multiple_of(q * 32 + first, 16), count)]

    def total(self, t):
        at, s = self.at, self.slot(t)
        self.landed(t, 3, 96)
        total = self.gp[s, at.z, self.rows(at.d, 0, 32), :].astype(f32)
        for n in range(3):
            total = total + self.rz[s, n].astype(f32)
        self.fin[t] = total.astype(bf)
        pltpu.make_async_copy(self.fin.at[t], self.quarter(t, at.d), self.osem.at[t]).start()
        self.push(t, self.fin.at[t], self.quarter(t, at.d), 4, at.x_dev, 1)
        self.push(t, self.fin.at[t], self.quarter(t, at.d), 4, at.y_dev, 1)

    def share(self, t):
        at = self.at
        self.landed(t, 4, 64)
        self.push(t, self.quarter(t, at.dx, 0, 16), self.quarter(t, at.dx, 0, 16), 5, at.y_dev, 1)
        self.push(t, self.quarter(t, at.dy, 16, 16), self.quarter(t, at.dy, 16, 16), 5, at.x_dev, 1)

    def done(self, t):
        self.landed(t, 5, 32)
        self.left(t, 1, 96)
        pltpu.make_async_copy(self.fin.at[t], self.quarter(t, self.at.d), self.osem.at[t]).wait()

    def release(self, t):
        self.left(t, 0, 896)
        self.left(t, 2, 96)

    def tick(self, j, i):
        for offset, name in self.STEPS:
            if offset % 4 == i:
                t = j - offset // 4
                if isinstance(t, int):
                    if 0 <= t < self.count:
                        getattr(self, name)(t)
                else:
                    pl.when((t >= 0) & (t < self.count))(functools.partial(getattr(self, name), t))

    def drain(self, j, i, last):
        for k in range(4 * j + i, 4 * (last + 3) + 1):
            self.tick(k // 4, k % 4)


class Keep:
    SLOTS = 3

    def __init__(self, count, gp, out, sem):
        self.count, self.gp, self.out, self.sem = count, gp, out, sem

    @classmethod
    def scratch(cls, count):
        return [pltpu.VMEM((cls.SLOTS, 4, 256, CW), bf), pltpu.SemaphoreType.DMA((count,))]

    def slot(self, t):
        return lax.rem(t, self.SLOTS)

    def copy(self, t):
        return pltpu.make_async_copy(self.gp.at[self.slot(t)], self.out.at[t], self.sem.at[t])

    def tick(self, j, i):
        if i == 0:
            pl.when((j >= 0) & (j < self.count))(lambda: self.copy(j).start())

    def release(self, t):
        self.copy(t).wait()


class Small:
    def __init__(self, at, sums, ra, rb, one, rc, two, rd, out, send, recv):
        self.at, self.sums, self.ra, self.rb, self.one, self.rc, self.two, self.rd = at, sums, ra, rb, one, rc, two, rd
        self.out, self.send, self.recv = out, send, recv

    @staticmethod
    def scratch():
        slab = (16, 128)
        return [pltpu.VMEM(shape + slab, f32) for shape in ((4, 2), (4,), (3,), (), (), (), ())] + [
            pltpu.SemaphoreType.DMA((4,)), pltpu.SemaphoreType.DMA((4,))]

    def copy(self, n, src, dst, dev):
        return remote(src, dst, self.send.at[n], self.recv.at[n], dev)

    def pair(self):
        return self.copy(0, self.sums.at[:, 1 - self.at.c], self.ra, self.at.sib_dev)

    def step(self, n):
        at, c = self.at, self.at.c
        if n > 4:
            return
        if n == 0:
            self.pair().start()
        if n == 1:
            self.pair().wait()
            self.sums[:, c] = self.sums[:, c] + self.ra[...]
            for i, (zz, dev) in enumerate(zip(at.zs, at.z_devs)):
                self.copy(1, self.sums.at[zz, c], self.rb.at[i], dev).start()
        if n == 2:
            self.copy(1, self.rb, self.rb, at.x_dev).wait()
            self.one[...] = self.sums[at.z, c] + self.rb[0] + self.rb[1] + self.rb[2]
            self.copy(2, self.one, self.rc, at.x_dev).start()
        if n == 3:
            self.copy(2, self.one, self.rc, at.x_dev).wait()
            self.two[...] = self.one[...] + self.rc[...]
            self.copy(3, self.two, self.rd, at.y_dev).start()
        if n == 4:
            self.copy(3, self.two, self.rd, at.y_dev).wait()
            self.out[...] = self.two[...] + self.rd[...]


def transpose_rows(src, dst, rows):
    full = rows // 128

    def one(i, carry):
        o = pl.multiple_of(i * 128, 128)
        dst[0:D, pl.ds(o, 128)] = src[pl.ds(o, 128), :].T
        return carry

    lax.fori_loop(0, full, one, 0)
    if rows % 128:
        dst[0:D, full * 128 : rows] = src[full * 128 : rows, :].T
    dst[0:D, rows:] = jnp.zeros((D, dst.shape[1] - rows), bf)
    if dst.shape[0] > D:
        dst[D:, :] = jnp.ones((dst.shape[0] - D, dst.shape[1]), bf)


def iota(shape, dim):
    return lax.broadcasted_iota(jnp.int32, shape, dim)


def units_of(first, rows):
    d = iota((rows, 128), 0) + first - UNIT * iota((rows, 128), 1)
    return jnp.where((d >= 0) & (d < UNIT), 1.0, 0.0).astype(bf)


def places_of(first, rows, width):
    r = iota((rows, width), 0) + first
    lane = iota((rows, width), 1)
    down = r - GRID * lane
    unit = lax.shift_right_logical(lane * 9363, 16)
    t = r - UNIT * unit
    across = t - GRID * lax.shift_right_logical(t * 37, 8)
    yes = jnp.ones((rows, width), f32)
    no = jnp.zeros((rows, width), f32)
    ohy = jnp.where((down >= 0) & (down < GRID), yes, no).astype(bf)
    ohx = jnp.where((t >= 0) & (t < UNIT) & (across == lane - GRID * unit), yes, no).astype(bf)
    return ohy, ohx


FIRST_STEPS = ((("s", 9),), (("s", 11), ("p", 8), ("d", 9)), (("p", 9), ("d", 11)), (("p", 11),))
SECOND_STEPS = ((("s", 10), ("p", 7), ("d", 8)), (("s", 12), ("d", 10)), (("p", 10), ("d", 12)), (("p", 12),))


def layer_kernel(rows, comm, *refs):
    refs = list(refs)

    def take(n):
        got = refs[:n]
        del refs[:n]
        return got

    tok_h, g_h, tab, q_table, k_table = take(5)
    if comm:
        small, ws_h = take(2)
    else:
        vec_in, b_up_in, w_h = take(3)
    out_h, gt_h, gw_h = take(3)
    if comm:
        (sums_out,) = take(1)
    else:
        vg, db_qkv, db_up = take(3)
    x_h, normedt_h, mixed_h, att_h, stats_h = take(5)
    if comm:
        (w_h,) = take(1)
    a1, a2, b1, b2, w, q_feat, k_feat, vec, b_up, lsem, wsem, osem, isem, xsem, tsem = take(15)
    parts = w_h.shape[0]
    chunks = parts - 1
    feed = chunks - QUADS
    if comm:
        vg, db_qkv, db_up, smalls, ssem, gsend, grecv = take(7)
        small_refs = take(9)
        at = Place()
        gather = Gather(at, ws_h, w_h, gsend, grecv)
        tick = gather.run
        red = Reduce(at, chunks, *refs[:6], gw_h, *refs[6:], w_h)
    else:
        tick = lambda *steps: None
        red = Keep(chunks, refs[0], gw_h, refs[1])
    KP = normedt_h.shape[1]
    pairs = rows // PAIR
    RB = PAIR // 7
    blocks = rows // RB

    def block(r):
        return pl.ds(pl.multiple_of(r * RB, 16), RB)

    def pair_rows(r):
        return pl.ds(pl.multiple_of(r * PAIR, 16), PAIR)

    every, qkv, out = pl.ds(0, CW), pl.ds(0, 3 * QW), pl.ds(3 * QW, QW)

    def load(k, s, src=every, dst=every):
        if comm:
            gather.load(k, src, w.at[s, :, dst], wsem.at[s])
        else:
            pltpu.make_async_copy(w_h.at[k, :, src], w.at[s, :, dst], wsem.at[s]).start()

    def load_quad(k, s):
        load(k, s, qkv, qkv)
        load(QUADS, s, pl.ds(pl.multiple_of(k * QW, QW), QW), out)

    def loaded(s, cols=every):
        pltpu.make_async_copy(w.at[s, :, cols], w.at[s, :, cols], wsem.at[s]).wait()

    tok_in = pltpu.make_async_copy(tok_h, b2, lsem.at[0])
    tok_in.start()
    g_in = pltpu.make_async_copy(g_h, b2, lsem.at[1])
    if comm:
        at.barrier()
        own = smalls.at[at.f]
        smalls[at.f] = small[...]
        for dev in at.z_devs:
            remote(own, own, ssem.at[0], ssem.at[1], dev).start()
        gather.begin(0)
    else:
        load(0, 0, qkv, qkv)
        vec[...] = vec_in[...]
        b_up[...] = b_up_in[...]

    def forward(normed, normedt, mixed, att, stats):
        def features(r, carry):
            unit = units_of(r * RB, RB)
            q_feat[block(r), :] = dot(unit, q_table[...]).astype(bf)
            k_feat[block(r), :] = dot(unit, k_table[...]).astype(bf)
            return carry

        lax.fori_loop(0, blocks, features, 0)
        tok_in.wait()
        if comm:
            gather.begin(1)

        def place(r, carry):
            n = PAIR
            sl = pl.ds(pl.multiple_of(r * n, 16), n)
            for half, hot in enumerate(places_of(r * n, n, tab.shape[1])):
                cols = slice(D // 2 * half, D // 2 * (half + 1))
                a1[sl, cols] = b2[sl, cols].astype(f32) + (dot(hot, tab[0]) + dot(hot, tab[1]) + dot(hot, tab[2]))
            return carry

        def norm_one(r, carry):
            xhat, _ = norm_parts(a1[block(r), :])
            normed[block(r), :] = (xhat * vec[0:1, :] + vec[1:2, :]).astype(bf)
            return carry

        if comm:
            lax.fori_loop(0, pairs // 2, place, 0)
            three = smalls.at[pl.ds(0, 3)]
            remote(three, three, ssem.at[0], ssem.at[1], at.x_dev).wait()
            for zz in [at.z] + at.zs:
                slab = smalls.at[2 * zz + at.c]
                remote(slab, slab, ssem.at[2], ssem.at[3], at.sib_dev).start()
            gather.begin(2)
            tick(("s", 0))
            lax.fori_loop(pairs // 2, pairs, place, 0)
            four = smalls.at[pl.ds(0, 4)]
            remote(four, four, ssem.at[2], ssem.at[3], at.sib_dev).wait()
            spread_vectors(smalls, vec, b_up)
        else:
            lax.fori_loop(0, pairs, place, 0)
        x_out = pltpu.make_async_copy(a1, x_h, osem.at[0])
        tick(("s", 1))
        lax.fori_loop(0, blocks // 2, norm_one, 0)
        tick(("d", 0))
        lax.fori_loop(blocks // 2, blocks, norm_one, 0)
        tick(("s", 2), ("p", 0))
        transpose_rows(normed, normedt, rows)
        n_out = pltpu.make_async_copy(normedt, normedt_h, osem.at[1])
        tick(("d", 1))
        if comm:
            gather.ready(0)
            load(0, 0, qkv, qkv)
        x_out.start()
        n_out.start()

        def saves(k):
            return (pltpu.make_async_copy(mixed, mixed_h.at[k], osem.at[2]),
                    pltpu.make_async_copy(att.at[:, pl.ds(QW * k, QW)], att_h.at[k], osem.at[3]),
                    pltpu.make_async_copy(stats, stats_h.at[k], osem.at[4]))

        for k in range(QUADS):
            s = k % 2
            loaded(s, qkv)

            def following():
                if k + 1 < QUADS:
                    load(k + 1, 1 - s, qkv, qkv)
                else:
                    load(QUADS, 1 - s)

            if not comm:
                following()
            if k > 0:
                for c in saves(k - 1):
                    c.wait()
            cols = slice(QW * k, QW * (k + 1))
            b_qkv = jnp.concatenate([vec[2:3, cols], jnp.zeros((1, QW), f32), vec[3:4, cols]], axis=1)

            tick(("p", k + 1), ("s", k + 3))

            def project(r, carry):
                sl = pair_rows(r)
                mixed[sl, :] = (dot(normed[sl, :], w[s, :, 0 : 3 * QW]) + b_qkv).astype(bf)
                return carry

            lax.fori_loop(0, pairs, project, 0)
            tick(("d", k + 2))
            saves(k)[0].start()
            if k == 1:
                g_in.start()

            def advance():
                gather.ready(k + 1)
                following()

            def hook(i):
                if comm:
                    pl.when(i == pairs - 1)(advance)

            attention_forward(pairs, mixed, q_feat, k_feat, att.at[:, pl.ds(QW * k, QW)], stats, hook)
            saves(k)[1].start()
            saves(k)[2].start()
        tick(("p", QUADS + 1), ("s", QUADS + 3))
        loaded(0)
        x_out.wait()

        def project_out(r, carry):
            sl = pair_rows(r)
            a1[sl, :] += dot(att[sl, :], w[0], NT) + vec[4:5, :]
            return carry

        lax.fori_loop(0, pairs, project_out, 0)
        tick(("d", QUADS + 2))
        if comm:
            gather.ready(QUADS + 1)
        load(QUADS + 1, 1)

        def second(r, carry):
            xhat, _ = norm_parts(a1[block(r), :])
            b1[block(r), :] = (xhat * vec[5:6, :] + vec[6:7, :]).astype(bf)
            return carry

        lax.fori_loop(0, blocks, second, 0)
        tick(("s", 8), ("p", 6), ("d", 7))
        n_out.wait()
        for c in saves(QUADS - 1):
            c.wait()

    pl.run_scoped(forward, pltpu.VMEM((rows, D), bf), pltpu.VMEM(normedt_h.shape, bf), pltpu.VMEM((rows, 3 * QW), bf),
                  pltpu.VMEM((rows, D), bf), pltpu.VMEM((rows, QW), bf))

    def put(t, m, left, right):
        slot, n = red.slot(t), left.shape[1]
        for i in range(2):
            red.gp[slot, 2 * m + i, :, 0:n] = left[256 * i : 256 * (i + 1)].astype(bf)
            red.gp[slot, 2 * m + i, :, n:CW] = right[256 * i : 256 * (i + 1)].astype(bf)

    def out_copy():
        return pltpu.make_async_copy(b1, out_h, osem.at[0])

    def feed_forward(n2t, gt, act, dhid, acc):
        act[rows:KP, :] = jnp.zeros((KP - rows, FC), bf)
        dhid[rows:KP, :] = jnp.zeros((KP - rows, FC), bf)
        acc[...] = jnp.zeros_like(acc)
        a2[...] = jnp.zeros_like(a2)
        transpose_rows(b1, n2t, rows)
        g_in.wait()
        transpose_rows(b2, gt, rows)

        def chunk(j, carry):
            s = lax.rem(j + 1, 2)
            loaded(s)
            after = QUADS + 2 + j
            if comm:
                for n, steps in enumerate(FIRST_STEPS):
                    pl.when(j == n)(functools.partial(tick, *steps))
            red.tick(j - 1, 0)
            for r in range(pairs):
                sl = pair_rows(r)
                h = dot(b1[sl, :], w[s, :, 0:FC]) + b_up[pl.ds(j, 1), :]
                da = dot(b2[sl, :], w[s, :, FC:CW])
                phi = 0.5 * (1.0 + lax.erf(h * 0.7071067811865476))
                slope = phi + h * (jnp.exp(-0.5 * h * h) * 0.3989422804014327)
                a = (h * phi).astype(bf)
                dh = (da * slope).astype(bf)
                act[sl, :] = a
                dhid[sl, :] = dh
                acc[sl, :] += dot(a, w[s, :, FC:CW], NT)
                a2[sl, :] += dot(dh, w[s, :, 0:FC], NT)
                red.tick(j - 1, r + 1)
                if r == 0:
                    @pl.when(after < parts)
                    def _():
                        if comm:
                            gather.ready(after)
                        load(after, 1 - s)

                    pl.when(after == parts)(lambda: load_quad(0, 1 - s))
                    if comm:
                        for n, steps in enumerate(SECOND_STEPS):
                            pl.when(j == n)(functools.partial(tick, *steps))

            @pl.when(j >= red.SLOTS)
            def _():
                red.release(j - red.SLOTS)

            put(j, 0, dot(n2t[0:512, :], dhid[...]), dot(gt[0:512, :], act[...]))
            red.tick(j - 1, 3)
            left = dot(n2t[512:, :], dhid[...])
            db_up[pl.ds(j, 1), :] = left[512:513]
            put(j, 1, left, dot(gt[512:, :], act[...]))
            return carry

        lax.fori_loop(0, feed, chunk, 0)
        red.tick(feed - 1, 0)
        vg[...] = jnp.zeros_like(vg)

        def last(r, carry):
            sl = block(r)
            middle = a1[sl, :]
            b1[sl, :] = (middle + acc[sl, :] + vec[7:8, :]).astype(bf)
            a1[sl, :] = jnp.zeros_like(middle)
            xhat, inv = norm_parts(middle)
            dn = a2[sl, :]
            cot = b2[sl, :].astype(f32)
            e = dn * vec[5:6, :]
            gm = cot + (e - jnp.mean(e, axis=-1, keepdims=True) - xhat * jnp.mean(e * xhat, axis=-1, keepdims=True)) * inv
            a2[sl, :] = gm
            gb = gm.astype(bf)
            b2[sl, :] = gb
            vg[2:3, :] += jnp.sum(gb.astype(f32), axis=0, keepdims=True)
            vg[3:4, :] += jnp.sum(dn * xhat, axis=0, keepdims=True)
            vg[4:5, :] += jnp.sum(dn, axis=0, keepdims=True)
            vg[5:6, :] += jnp.sum(cot, axis=0, keepdims=True)
            pl.when(r == blocks // 2)(functools.partial(red.tick, feed - 1, 1))
            return carry

        lax.fori_loop(0, blocks, last, 0)
        out_copy().start()

    pl.run_scoped(feed_forward, pltpu.VMEM(normedt_h.shape, bf), pltpu.VMEM((D, KP), bf), pltpu.VMEM((KP, FC), bf),
                  pltpu.VMEM((KP, FC), bf), pltpu.VMEM((rows, D), f32))

    def backward(normedt, gbt, mixed, att, stats, datt, swap, dq, dk, dv, xb, ob):
        n_in = pltpu.make_async_copy(normedt_h, normedt, lsem.at[0])

        def inputs(k, s):
            return (pltpu.make_async_copy(mixed_h.at[k], mixed.at[s, pl.ds(0, rows)], isem.at[s, 0]),
                    pltpu.make_async_copy(att_h.at[k], att.at[s, pl.ds(0, rows)], isem.at[s, 1]),
                    pltpu.make_async_copy(stats_h.at[k], stats.at[s], isem.at[s, 2]))

        for c in inputs(0, 1):
            c.start()
        n_in.start()
        for s in range(2):
            mixed[s, rows:KP, :] = jnp.zeros((KP - rows, 3 * QW), bf)
            att[s, rows:KP, :] = jnp.zeros((KP - rows, QW), bf)
        swap[...] = jnp.where(low_lanes(128) != (iota((128, 128), 0) < 64), 1.0, 0.0).astype(bf)
        transpose_rows(b2, gbt, rows)

        def keep(k, s):
            return pltpu.make_async_copy(mixed.at[s, pl.ds(0, rows)], mixed_h.at[k], isem.at[s, 3])

        def quad(k, carry):
            s = lax.rem(k + 1, 2)
            t = feed + k
            loaded(s)
            for c in inputs(k, s):
                c.wait()

            @pl.when(k > 0)
            def _():
                keep(k - 1, 1 - s).wait()

            @pl.when(k + 1 < QUADS)
            def _():
                load_quad(k + 1, 1 - s)
                for c in inputs(k + 1, 1 - s):
                    c.start()

            def back(r, inner):
                sl = pair_rows(r)
                datt[sl, :] = dot(b2[sl, :], w[s, :, 3 * QW : CW]).astype(bf)
                return inner

            pl.when(k > 0)(lambda: red.tick(t - 1, 0))
            lax.fori_loop(0, pairs, back, 0)

            def hook(i):
                pl.when((i == pairs - 1) & (k > 0))(functools.partial(red.tick, t - 1, 1))
                pl.when(i == 2 * pairs - 1)(functools.partial(red.tick, t - 1, 2))

            attention_backward(pairs, mixed.at[s], att.at[s], stats.at[s], datt, k_feat, swap, dq, dk, dv, hook)
            red.release(t - red.SLOTS)
            pl.when(k == 0)(n_in.wait)
            put(t, 0, dot(normedt[0:512, :], mixed[s]), dot(gbt[0:512, :], att[s]))
            red.tick(t - 1, 3)
            left = dot(normedt[512:, :], mixed[s])
            db_qkv[pl.ds(k, 1), :] = left[512:513]
            put(t, 1, left, dot(gbt[512:, :], att[s]))

            pl.when(k + 1 < QUADS)(lambda: keep(k, s).start())
            return carry

        lax.fori_loop(0, QUADS, quad, 0)
        red.tick(chunks - 1, 0)

        def again(k, s):
            load(k, s, qkv, qkv)
            inputs(k, s)[0].start()

        again(0, 1)

        def back_in(n, carry):
            s = lax.rem(n, 2)

            @pl.when(n > 0)
            def _():
                loaded(s, qkv)
                inputs(n - 1, s)[0].wait()

            for r in range(pairs):
                sl = pl.ds(r * PAIR, PAIR)
                a1[sl, :] += dot(mixed[s, sl, :], w[s, :, 0 : 3 * QW], NT)

            pl.when(n + 2 < QUADS)(lambda: again(n + 1, s))

            if comm:
                for m, (j, i) in enumerate(((0, 1), (0, 2), (0, 3), (1, 0))):
                    pl.when(n == m)(functools.partial(red.tick, chunks - 1 + j, i))
            return carry

        lax.fori_loop(0, QUADS, back_in, 0)
        ring = xb.shape[0]

        def xcopy(r):
            s = lax.rem(r, ring)
            return pltpu.make_async_copy(x_h.at[block(r)], xb.at[s], xsem.at[s])

        def tcopy(r):
            s = lax.rem(r, 2)
            return pltpu.make_async_copy(ob.at[s], gt_h.at[block(r)], tsem.at[s])

        for r in range(ring):
            xcopy(r).start()

        def last(r, carry):
            xcopy(r).wait()
            pl.when(r >= 2)(lambda: tcopy(r - 2).wait())
            xhat, inv = norm_parts(xb[lax.rem(r, ring)])
            dn = a1[block(r), :]
            e = dn * vec[0:1, :]
            total = a2[block(r), :] + (e - jnp.mean(e, axis=-1, keepdims=True) - xhat * jnp.mean(e * xhat, axis=-1, keepdims=True)) * inv
            ob[lax.rem(r, 2)] = total.astype(bf)
            tcopy(r).start()
            vg[0:1, :] += jnp.sum(dn * xhat, axis=0, keepdims=True)
            vg[1:2, :] += jnp.sum(dn, axis=0, keepdims=True)
            pl.when(r + ring < blocks)(lambda: xcopy(r + ring).start())
            if comm:
                for at_r, steps in ((0, ((1, 1),)), (2, ((1, 2),)), (4, ((1, 3),)), (7, ((2, 0),)), (13, ((2, 1), (2, 2)))):
                    for j, i in steps:
                        pl.when(r == at_r)(functools.partial(red.tick, chunks - 1 + j, i))
            return carry

        lax.fori_loop(0, blocks, last, 0)
        out_copy().wait()
        if comm:
            share = Small(at, *small_refs[:7], sums_out, *small_refs[7:])
            sums = share.sums
            sums[...] = jnp.zeros_like(sums)
            for f in range(8):
                lanes = slice(128 * f, 128 * (f + 1))
                q, half = slice(f // 2, f // 2 + 1), 128 * (f % 2)
                rows_of = [vg[0:1, lanes], vg[1:2, lanes], db_qkv[q, half : half + 128],
                           db_qkv[q, 2 * QW + half : 2 * QW + half + 128]] + [vg[n : n + 1, lanes] for n in (2, 3, 4, 5)]
                rows_of += [db_up[f : f + 1, 128 * i : 128 * (i + 1)] for i in range(4)]
                for i, row in enumerate(rows_of):
                    sums[f // 2, f % 2, i : i + 1, :] = row
            for n, k in enumerate(range(11, 17)):
                red.tick(chunks - 1 + k // 4, k % 4)
                share.step(n)
            for k in range(parts):
                gather.finish(k)
        for r in (blocks - 2, blocks - 1):
            tcopy(r).wait()
        for t in range(chunks - red.SLOTS, chunks):
            red.release(t)

    pl.run_scoped(backward, pltpu.VMEM(normedt_h.shape, bf), pltpu.VMEM((D, KP), bf), pltpu.VMEM((2, KP, 3 * QW), bf),
                  pltpu.VMEM((2, KP, QW), bf), pltpu.VMEM((2, rows, QW), bf), pltpu.VMEM((rows, QW), bf), pltpu.VMEM((128, 128), bf), pltpu.VMEM((PAIR, 128), f32),
                  pltpu.VMEM((PAIR, 128), f32), pltpu.VMEM((PAIR, 128), f32), pltpu.VMEM((3, RB, D), f32),
                  pltpu.VMEM((2, RB, D), bf))


def layer(rows, comm, chunks, *args):
    A, V = any_spec(), vmem_spec()
    KP = -(-rows // 256) * 256
    sums = ((8, D), (QUADS, 3 * QW), (chunks - QUADS, FC))
    kept = [sds((rows, D), f32), sds((D + 16, KP), bf), sds((QUADS, rows, 3 * QW), bf), sds((QUADS, rows, QW), bf),
            sds((QUADS, rows, QW), bf)]
    first = [sds((rows, D), bf), sds((rows, D), bf), sds((chunks, 128, CW) if comm else (chunks, 4, 256, CW), bf)]
    scratch = [
        pltpu.VMEM((rows, D), f32), pltpu.VMEM((rows, D), f32), pltpu.VMEM((rows, D), bf), pltpu.VMEM((rows, D), bf),
        pltpu.VMEM((2, D, CW), bf), pltpu.VMEM((rows, 128), bf), pltpu.VMEM((rows, 128), bf), pltpu.VMEM((8, D), f32),
        pltpu.VMEM((chunks - QUADS, FC), f32),
        pltpu.SemaphoreType.DMA((2,)), pltpu.SemaphoreType.DMA((2,)), pltpu.SemaphoreType.DMA((5,)),
        pltpu.SemaphoreType.DMA((2, 4)), pltpu.SemaphoreType.DMA((3,)), pltpu.SemaphoreType.DMA((2,)),
    ]
    if comm:
        in_specs = [A, A, V, V, V, V, A]
        out_shape = first + [sds((16, 128), f32)] + kept + [sds((chunks + 1, 4, 256, CW), bf)]
        out_specs = [A, A, A, V] + [A] * 6
        scratch += [pltpu.VMEM(shape, f32) for shape in sums] + [
            pltpu.VMEM((8, 16, 128), bf), pltpu.SemaphoreType.DMA((4,)), pltpu.SemaphoreType.DMA((chunks + 1,)),
            pltpu.SemaphoreType.DMA((chunks + 1, 6))] + Small.scratch() + Reduce.scratch(chunks)
        params = pltpu.CompilerParams(vmem_limit_bytes=VMEM_LIMIT, collective_id=0, has_side_effects=True)
    else:
        in_specs = [A, A, V, V, V, V, V, A]
        out_shape = first + [sds(shape, f32) for shape in sums] + kept
        out_specs = [A, A, A, V, V, V] + [A] * 5
        scratch += Keep.scratch(chunks)
        params = pltpu.CompilerParams(vmem_limit_bytes=VMEM_LIMIT)
    return pl.pallas_call(
        functools.partial(layer_kernel, rows, comm), out_shape=out_shape, in_specs=in_specs, out_specs=out_specs,
        scratch_shapes=scratch, compiler_params=params, name="encoder_layer",
    )(*args)


def prepare_kernel(units, band, gsd, freq, qkv, out, up, down, *refs):
    *vectors, shard, tab, q_table, k_table = refs
    if vectors:
        *vectors, bias_up, shard, tab, q_table, k_table, small = refs
        rows = [v[...].reshape(1, 128) for v in vectors] + [bias_up[128 * i : 128 * (i + 1)].reshape(1, 128) for i in range(4)]
        rows.append(jnp.zeros((16 - len(rows), 128), bf))
        small[...] = jnp.concatenate([r.astype(f32) for r in rows], axis=0).astype(bf)
    for k in range(QUADS):
        for i in range(3):
            shard[k, :, QW * i : QW * (i + 1)] = qkv[:, D * i + QW * k : D * i + QW * (k + 1)]
        shard[QUADS, :, QW * k : QW * (k + 1)] = out[QW * k : QW * (k + 1), :].T
    for j in range(up.shape[1] // FC):
        shard[QUADS + 1 + j, :, 0:FC] = up[:, FC * j : FC * (j + 1)]
        shard[QUADS + 1 + j, :, FC:CW] = down[FC * j : FC * (j + 1), :].T
    entry = iota((tab.shape[1], 128), 0)
    unit = lax.shift_right_logical(entry * 9363, 16)
    level = jnp.zeros(entry.shape, jnp.int32)
    row = iota((128, 128), 0)
    item = jnp.full((128, 128), -100, jnp.int32)
    label = jnp.int32(0)
    for u in range(units):
        if u % UNITS_MB == 0:
            label = jnp.int32(-1 + UNITS_MB * (u // UNITS_MB % 2))
        label = label + jnp.where(band[u] <= 1, 1, 0)
        item = jnp.where(row == u, label, item)
        level = jnp.where(unit == u, gsd[u], level)
    place = (entry - GRID * unit).astype(f32) * jnp.exp2((level.astype(f32) - 3.0) * 0.5)
    angle = jnp.concatenate([place, place], axis=1) * freq[...]
    wave = jnp.concatenate([jnp.sin(angle), jnp.cos(angle)], axis=1)
    wave = jnp.where(iota(wave.shape, 0) < GRID * units, wave, 0.0)
    high = wave.astype(bf)
    rest = wave - high.astype(f32)
    middle = rest.astype(bf)
    tab[0] = high
    tab[1] = middle
    tab[2] = (rest - middle.astype(f32)).astype(bf)
    slot = (iota((128, 128), 1) & 63) - 3
    used = (slot >= 0) & (slot < 2 * UNITS_MB)
    real = row < units
    q_table[...] = jnp.where(real & (item == slot), 1.0, 0.0).astype(bf)
    k_table[...] = jnp.where(real, jnp.where(used & (item != slot), NEG, jnp.where(slot < 0, 1.0, 0.0)), 0.0).astype(bf)


def prepare(rows, band_code, gsd_code, qkv, out, up, down, *vectors):
    units = rows // UNIT
    n = qkv.shape[0]
    places = -(-GRID * units // 256) * 256
    quarter = D // 4
    freq = np.exp2(np.arange(quarter, dtype=np.float32) * np.float32(-math.log2(10000.0) / quarter)).astype(np.float32)
    V, S = vmem_spec(), pl.BlockSpec(memory_space=pltpu.SMEM)
    return pl.pallas_call(
        functools.partial(prepare_kernel, units),
        out_shape=(sds((QUADS + 1 + up.shape[1] // FC, n, CW), bf), sds((3, places, 2 * quarter), bf), sds((128, 128), bf),
                   sds((128, 128), bf)) + ((sds((16, 128), bf),) if vectors else ()),
        in_specs=[S, S, V, V, V, V, V] + [V] * len(vectors), out_specs=(V, V, V, V) + ((V,) if vectors else ()),
        compiler_params=pltpu.CompilerParams(vmem_limit_bytes=VMEM_LIMIT), name="prepare",
    )(band_code, gsd_code, jnp.asarray(freq)[None, :], qkv, out, up, down, *vectors)


def results_kernel(rows, out_i, gt_i, gw_i, sums, out_h, gt_h, dg1, db1, g_qkv, dbq, dbv, g_out, dbo, dg2, db2, g_up, db_up, g_down,
                   db_down, out_v, gt_v, gt_f, gw, qkv_v, o_v, up_v, down_v, sem_in, sem_out):
    loads = [pltpu.make_async_copy(src, dst, sem_in.at[i])
             for i, (src, dst) in enumerate(((gw_i, gw), (out_i, out_v), (gt_i, gt_v)))]
    stores = [pltpu.make_async_copy(src, dst, sem_out.at[i])
              for i, (src, dst) in enumerate(((out_v, out_h), (gt_f, gt_h), (qkv_v, g_qkv), (o_v, g_out), (up_v, g_up), (down_v, g_down)))]
    for c in loads:
        c.start()
    for i, ref in enumerate((dg1, db1, dbq, dbv, dbo, dg2, db2, db_down)):
        ref[...] = sums[i]
    for i in range(4):
        db_up[128 * i : 128 * (i + 1)] = sums[8 + i]
    loads[0].wait()
    feed = gw.shape[0] - QUADS
    for k in range(QUADS):
        for i in range(3):
            qkv_v[:, D * i + QW * k : D * i + QW * (k + 1)] = gw[feed + k, :, QW * i : QW * (i + 1)].astype(f32)
        o_v[QW * k : QW * (k + 1), :] = gw[feed + k, :, 3 * QW : CW].T.astype(f32)
    stores[2].start()
    stores[3].start()
    loads[1].wait()
    stores[0].start()
    for j in range(feed):
        up_v[:, FC * j : FC * (j + 1)] = gw[j, :, 0:FC].astype(f32)
        down_v[FC * j : FC * (j + 1), :] = gw[j, :, FC:CW].T.astype(f32)
    stores[4].start()
    stores[5].start()
    loads[2].wait()
    RB = PAIR // 7

    def widen(r, carry):
        sl = pl.ds(pl.multiple_of(r * RB, 16), RB)
        gt_f[sl, :] = gt_v[sl, :].astype(f32)
        return carry

    lax.fori_loop(0, rows // RB, widen, 0)
    stores[1].start()
    for c in stores:
        c.wait()


def results(out, gt, gw, sums):
    rows, chunks = out.shape[0], gw.shape[0]
    hidden = (chunks - QUADS) * FC
    A, V = any_spec(), vmem_spec()
    vec = sds((128,), f32)
    wide = [sds((128, 3 * D), f32), sds((D, 128), f32), sds((128, hidden), f32), sds((hidden, 128), f32)]
    return pl.pallas_call(
        functools.partial(results_kernel, rows),
        out_shape=(sds((rows, D), bf), sds((rows, D), f32), vec, vec, wide[0], vec, vec, wide[1], vec, vec, vec, wide[2],
                   sds((512,), f32), wide[3], vec),
        in_specs=[A, A, A, V], out_specs=(A, A, V, V, A, V, V, A, V, V, V, A, V, A, V),
        scratch_shapes=[pltpu.VMEM((rows, D), bf), pltpu.VMEM((rows, D), bf), pltpu.VMEM((rows, D), f32), pltpu.VMEM(gw.shape, bf)]
        + [pltpu.VMEM(v.shape, f32) for v in wide] + [pltpu.SemaphoreType.DMA((3,)), pltpu.SemaphoreType.DMA((6,))],
        compiler_params=pltpu.CompilerParams(vmem_limit_bytes=VMEM_LIMIT), name="results",
    )(out, gt, gw, sums)


def local(dp, fsdp, tokens, band_code, gsd_code, norm1_gain, norm1_bias, qkv_weight, bias_q, bias_v, out_weight, bias_out,
          norm2_gain, norm2_bias, up_weight, bias_up, down_weight, bias_down, grad_out):
    rows = tokens.shape[0]
    comm = dp == 4 and fsdp == 8
    vectors = (norm1_gain, norm1_bias, bias_q, bias_v, bias_out, norm2_gain, norm2_bias, bias_down)
    shard, tab, q_table, k_table, *small = prepare(rows, band_code, gsd_code, qkv_weight, out_weight, up_weight, down_weight,
                                                   *(vectors + (bias_up,) if comm else ()))
    chunks, n = shard.shape[0] - 1, shard.shape[1]
    args = (tokens, grad_out, tab, q_table, k_table)
    if comm:
        out, grad_tokens, gw, sg, *_ = layer(rows, True, chunks, *args, *small, shard)
        return results(out, grad_tokens, gw, sg)
    else:
        gathered = lax.all_gather(jnp.stack(vectors), "fsdp", axis=1, tiled=True).astype(f32)
        up_bias = lax.all_gather(bias_up, "fsdp", axis=0, tiled=True).astype(f32).reshape(-1, FC)
        whole = lax.all_gather(shard, "fsdp", axis=1, tiled=True)
        out, grad_tokens, gw, vg, db_qkv, db_up, *_ = layer(rows, False, chunks, *args, gathered, up_bias, whole)
        sg = jnp.concatenate([vg[0:2], db_qkv[:, 0:QW].reshape(1, D), db_qkv[:, 2 * QW :].reshape(1, D), vg[2:6]], axis=0)
        sg = jnp.concatenate([sg.reshape(8, fsdp, n).transpose(1, 0, 2).reshape(fsdp, 8 * n), db_up.reshape(fsdp, 4 * n)], axis=1)
        sg = lax.psum(lax.psum_scatter(sg, "fsdp", scatter_dimension=0, tiled=True), "dp").reshape(12, n)
        gw = lax.psum(lax.psum_scatter(gw.reshape(chunks, D, CW), "fsdp", scatter_dimension=1, tiled=True), "dp")
    gw = gw.astype(f32)
    g_ff, g_att = gw[: chunks - QUADS], gw[chunks - QUADS :]
    g_qkv = g_att[:, :, : 3 * QW].reshape(QUADS, n, 3, QW).transpose(1, 2, 0, 3).reshape(n, 3 * D)
    g_out = g_att[:, :, 3 * QW :].transpose(0, 2, 1).reshape(D, n)
    g_up = g_ff[:, :, :FC].transpose(1, 0, 2).reshape(n, -1)
    g_down = g_ff[:, :, FC:].transpose(0, 2, 1).reshape(-1, n)
    grad_tokens = grad_tokens.astype(f32)
    return (out, grad_tokens, sg[0], sg[1], g_qkv, sg[2], sg[3], g_out, sg[4], sg[5], sg[6], g_up, sg[8:12].reshape(4 * n), g_down, sg[7])


def solution(mesh):
    rows, vec, first, second = P(("dp", "fsdp"), None), P("fsdp"), P("fsdp", None), P(None, "fsdp")
    codes = P(("dp", "fsdp"))
    return jax.shard_map(
        functools.partial(local, mesh.shape["dp"], mesh.shape["fsdp"]),
        mesh=mesh,
        in_specs=(rows, codes, codes, vec, vec, first, vec, vec, second, vec, vec, vec, first, vec, second, vec, rows),
        out_specs=(rows, rows, vec, vec, first, vec, vec, second, vec, vec, vec, first, vec, second, vec),
        check_vma=False,
    )
```
